32 devices in a mesh: ctx: 4 (over x, core), tp: 8 (over z, y).
Axes of the slice: x: 2, y: 2, z: 4, core: 2. Of those that a mesh axis runs over, the one named last changes fastest.
Arguments:
- out_grad: bfloat16 [4096, 4096], P('ctx', 'tp'), may hold values from -6 to 6
- pre_act: bfloat16 [4096, 4096], P('ctx', 'tp'), may hold values from -6 to 6
- normed: bfloat16 [4096, 12800], P('ctx', 'tp'), may hold values from -5 to 5
- inverse_std: float32 [4096], P('ctx'), may hold values from 0.5 to 2
- w_up: bfloat16 [4096, 12800], P(None, 'tp')
- w_down: bfloat16 [4096, 4096], P(None, 'tp'), may hold values from -0.09375 to 0.09375
- ln_gain: float32 [12800], P('tp'), may hold values from 0.25 to 1.75
- owner_map: int32 [4, 4], P('ctx'), may hold values from 0 to 7, as said below
Outputs:
- grad_w2: float32 [4096, 4096], P('ctx', 'tp')
- grad_w1: float32 [4096, 12800], P('ctx', 'tp')
- grad_b1: float32 [4096], P('tp')
- grad_b2: float32 [4096], P('tp')
- ln_grads: float32 [2, 12800], P(None, 'tp')
- vit_grad: bfloat16 [8192, 12800], P(('ctx', 'tp'))
The draws below stay inside these ranges and needn't reach their ends.
Inputs may be any that keep to these rules, and one draw needn't show every extreme that they name: `owner_map`: within each context shard, every encoder rank owns at most 1 of the 4 images, and some rank owns exactly 1.
All inputs are finite; a program needn't handle non-finite values.
Results may differ from the reference program's by a relative error of at most 0.007.
Values may be sent and summed in bfloat16 or wider, within the bound.
No kernel may reach another device: no remote copies, remote signals or barrier semaphores. Data moves between devices by JAX's collectives and lax.ppermute only.
A program may use at most 192 MiB of HBM per device.

```python
import math
import jax
import jax.numpy as jnp

D = 4096
PH = 4096
PW = 12800
ROWS = 1024
IMG = 256
IMGS_GRP = 4
MOST = 1
NV = 4096
OWNER_ROWS = 8192
N_CTX = 4
N_TP = 8


def owner_group(group_key):
    key_busy, key_rest, key_shuffle = jax.random.split(group_key, 3)
    busiest = jax.random.randint(key_busy, (), 0, N_TP).astype(jnp.int32)
    others = jax.random.permutation(key_rest, (N_TP - 1) * MOST).astype(jnp.int32)
    remainder = (busiest + 1 + others // MOST) % N_TP
    listing = jnp.concatenate([jnp.full((MOST,), 1, jnp.int32) * busiest, remainder.astype(jnp.int32)])[:IMGS_GRP]
    shuffle = jax.random.permutation(key_shuffle, IMGS_GRP)
    return listing[shuffle].astype(jnp.int32)


def draw_owner_map(key, part):
    group_keys = jax.random.split(jax.random.fold_in(key, 17), N_CTX)
    return jax.vmap(owner_group)(group_keys)


def draw_w_up(key, part):
    key_noise, key_common = jax.random.split(jax.random.fold_in(key, 29))
    noise = jax.random.normal(key_noise, (PH, PW), jnp.float32)
    common = jax.random.normal(key_common, (PH, 1), jnp.float32)
    return ((noise + common) * float(PH) ** (-0.5)).astype(jnp.bfloat16)


def spiked(drawn, own_key, source, target, blocks, factor):
    def block_of(axis_at):
        return (jnp.arange(drawn.shape[axis_at]) // (drawn.shape[axis_at] // blocks)).reshape((-1,) + (1,) * (drawn.ndim - 1 - axis_at))

    first = jax.random.permutation(own_key, blocks)[block_of(target)]
    other_side = (block_of(target) + blocks // 2) % blocks
    return jnp.where((block_of(source) == first) | (block_of(source) == other_side), factor * drawn, drawn)


def level_of(rng, dims, shards, smallest, high):
    def one(dim, parts):
        heights = jax.random.uniform(jax.random.fold_in(jax.random.fold_in(rng, 6), dim), (parts,), jnp.float32, smallest / len(shards), high / len(shards))
        return jnp.repeat(jnp.exp(heights), dims[dim] // parts).reshape((-1,) + (1,) * (len(dims) - dim - 1))

    loudness = one(*shards[0])
    for cut in shards[1:]:
        loudness = loudness * one(*cut)
    return loudness


def centred(rng, extent, spread, reach, shards=(), dtype=jnp.bfloat16):
    level = level_of(rng, extent, shards, -0.22, 0.18) if shards else 1.0
    result = jax.random.normal(rng, extent, jnp.float32) * spread * level
    return jnp.minimum(jnp.maximum(result, -reach), reach).astype(dtype)


def heavy_noise(stream_key, extent, spread, most, cuts, heavy, dtype=jnp.bfloat16):
    result = spread * jax.random.normal(stream_key, extent, jnp.float32)
    if cuts:
        result = result * level_of(stream_key, extent, cuts, -0.22, 0.18)
    return jnp.clip(spiked(result, jax.random.fold_in(stream_key, 3), *heavy), -most, most).astype(dtype)


def setup_inputs(seed: int = 0) -> dict:
    streams_of = jax.random.split(jax.random.key(seed), 9)
    return {
        "out_grad": heavy_noise(streams_of[0], (NV, D), 1.0, 6.0, ((0, 4), (1, 8)), (0, 1, 8, 2.0)),
        "pre_act": centred(streams_of[1], (NV, PH), 1.5, 6.0, ((0, 4), (1, 8))),
        "normed": centred(streams_of[2], (NV, PW), 1.0, 5.0, ((0, 4), (1, 8))),
        "inverse_std": jnp.clip(jnp.exp(math.log(2.0) - 1.3862944 * jax.random.uniform(streams_of[3], (NV,), jnp.float32) ** level_of(streams_of[3], (NV,), ((0, 4),), -0.2, 0.2)), 0.5, 2.0),
        "w_up": draw_w_up(jax.random.fold_in(streams_of[8], 71), 0),
        "w_down": centred(streams_of[5], (D, PH), D ** -0.5, 0.09375, ((1, 8),)),
        "ln_gain": jnp.clip(1.0 + 0.15 * jax.random.normal(streams_of[6], (PW,), jnp.float32), 0.25, 1.75),
        "owner_map": draw_owner_map(jax.random.fold_in(streams_of[8], 71), 0),
    }


def gelu_parts(linear):
    normal_cdf = 0.5 * (1.0 + jax.scipy.special.erf(linear * (2.0 ** -0.5)))
    density = jnp.exp(-0.5 * linear * linear) * ((2.0 * math.pi) ** -0.5)
    return linear * normal_cdf, normal_cdf + linear * density


def slot_numbers(owners, capacity):
    position = jnp.arange(owners.shape[0]).astype(jnp.int32)
    earlier = (owners[None, :] == owners[:, None]) & (position[None, :] < position[:, None])
    return owners * capacity + jnp.sum(earlier.astype(jnp.int32), axis=1).astype(jnp.int32)


def reference(out_grad, pre_act, normed, inverse_std, w_up, w_down, ln_gain, owner_map):
    grad_scale = float(NV) ** -0.5
    gelu_value, gelu_slope = gelu_parts(pre_act.astype(jnp.float32))
    hidden = gelu_value.astype(jnp.bfloat16)
    back_hidden = jnp.dot(out_grad, w_down, preferred_element_type=jnp.float32)
    back_linear = (back_hidden * gelu_slope).astype(jnp.bfloat16)
    grad_w2 = jnp.dot(out_grad.T, hidden, preferred_element_type=jnp.float32) * grad_scale
    grad_b1 = jnp.sum(back_linear.astype(jnp.float32), axis=0) * grad_scale
    grad_b2 = jnp.sum(out_grad.astype(jnp.float32), axis=0) * grad_scale
    grad_w1 = jnp.dot(back_linear.T, normed, preferred_element_type=jnp.float32) * grad_scale
    norm_grad = jnp.dot(back_linear, w_up, preferred_element_type=jnp.float32)
    features = normed.astype(jnp.float32)
    gained = ln_gain[None, :] * norm_grad
    mean_first = jnp.mean(gained, axis=-1, keepdims=True)
    mean_second = jnp.mean(gained * features, axis=-1, keepdims=True)
    visual_grad = (inverse_std[:, None] * (gained - mean_first - features * mean_second)).astype(jnp.bfloat16)
    ln_grads = jnp.stack([jnp.sum(norm_grad * features, axis=0), jnp.sum(norm_grad, axis=0)]) * grad_scale
    slot_table = jax.vmap(lambda owners: slot_numbers(owners, MOST))(owner_map)
    row_ids = jnp.arange(NV).astype(jnp.int32)
    group_ids = row_ids // ROWS
    image_ids = (row_ids % ROWS) // IMG
    within = row_ids % IMG
    target = (group_ids * (N_TP * MOST) + slot_table[group_ids, image_ids]) * IMG + within
    vit_grad = jnp.zeros((OWNER_ROWS, PW), jnp.bfloat16).at[target].set(visual_grad)
    return grad_w2, grad_w1, grad_b1, grad_b2, ln_grads, vit_grad
```

```python
import math

import jax
import jax.numpy as jnp
from jax import lax
from jax.sharding import PartitionSpec as P

CHUNKS = 2


def gelu_parts(linear):
    normal_cdf = 0.5 * (1.0 + jax.scipy.special.erf(linear * 2.0 ** (-0.5)))
    density = jnp.exp(-0.5 * linear * linear) * (2.0 * math.pi) ** (-0.5)
    return (linear * normal_cdf, normal_cdf + linear * density)


def slot_numbers(owners, capacity):
    position = jnp.arange(owners.shape[0])
    earlier = (owners[None, :] == owners[:, None]) & (position[None, :] < position[:, None])
    return owners * capacity + jnp.sum(earlier.astype(jnp.int32), axis=1)


def row_product(left, right):
    return lax.dot_general(
        left, right, (((0,), (0,)), ((), ())), preferred_element_type=jnp.float32
    )


def ring_order(count):
    depth = 4 if count % 4 == 0 else count
    width = count // depth
    walk = [(z, 0) for z in range(depth)]
    if width > 1:
        for turn, z in enumerate(reversed(range(depth))):
            ys = list(range(1, width))
            walk += [(z, y) for y in (ys if turn % 2 == 0 else ys[::-1])]
    return [z * width + y for z, y in walk]


def ring_gather(block, count):
    order = ring_order(count)
    place = [order.index(j) for j in range(count)]
    ahead = [(order[p], order[(p + 1) % count]) for p in range(count)]
    behind = [(order[p], order[(p - 1) % count]) for p in range(count)]
    rows, width = block.shape
    me = lax.axis_index("tp")
    at = jnp.array(place, jnp.int32)[me]
    owner = jnp.array(order, jnp.int32)
    full = jnp.zeros((rows, count * width), block.dtype)
    full = lax.dynamic_update_slice(full, block, (0, me * width))
    up, down = block, block
    for step in range(1, count // 2):
        up = lax.ppermute(up, "tp", ahead)
        down = lax.ppermute(down, "tp", behind)
        full = lax.dynamic_update_slice(full, up, (0, owner[(at - step) % count] * width))
        full = lax.dynamic_update_slice(full, down, (0, owner[(at + step) % count] * width))
    half = rows // 2
    far = owner[(at + count // 2) % count] * width
    up = lax.ppermute(up[:half], "tp", ahead)
    down = lax.ppermute(down[half:], "tp", behind)
    full = lax.dynamic_update_slice(full, up, (0, far))
    full = lax.dynamic_update_slice(full, down, (half, far))
    return full


def ctx_scatter(partial, ctx_count):
    pairs = ctx_count // 2
    index = lax.axis_index("ctx")
    chip, core = index // 2, index % 2
    rows = partial.shape[0] // ctx_count
    parts = partial.reshape(pairs, 2, rows, partial.shape[1])
    other = lax.dynamic_index_in_dim(parts, 1 - core, axis=1, keepdims=False).astype(jnp.bfloat16)
    mine = lax.dynamic_index_in_dim(parts, core, axis=1, keepdims=False)
    swap = [(c, c ^ 1) for c in range(ctx_count)]
    total = mine + lax.ppermute(other, "ctx", swap).astype(jnp.float32)
    result = lax.dynamic_index_in_dim(total, chip, axis=0, keepdims=False)
    for shift in range(1, pairs):
        going = lax.dynamic_index_in_dim(
            total, (chip + shift) % pairs, axis=0, keepdims=False
        ).astype(jnp.bfloat16)
        route = [(c, (c + 2 * shift) % ctx_count) for c in range(ctx_count)]
        result = result + lax.ppermute(going, "ctx", route).astype(jnp.float32)
    return result


def ctx_sum(value, ctx_count):
    bit = 1
    while bit < ctx_count:
        value = value + lax.ppermute(value, "ctx", [(c, c ^ bit) for c in range(ctx_count)])
        bit *= 2
    return value


def tp_sum(value, tp_count):
    total = value
    for shift in range(1, tp_count):
        total = total + lax.ppermute(
            value, "tp", [(t, (t + shift) % tp_count) for t in range(tp_count)]
        )
    return total


def per_device(out_grad, pre_act, normed, inverse_std, w_up, w_down, ln_gain, owner_map):
    ctx_count = lax.axis_size("ctx")
    tp_count = lax.axis_size("tp")
    row_count = out_grad.shape[0]
    width = normed.shape[1]
    grad_scale = float(row_count * ctx_count) ** (-0.5)
    full_width = float(width * tp_count)

    owners = owner_map[0]
    image_count = owners.shape[0]
    image_rows = row_count // image_count
    part_rows = image_rows // CHUNKS
    capacity = max(1, 2 * image_count // tp_count)
    slot_of = slot_numbers(owners, capacity)
    slot_ids = jnp.arange(tp_count * capacity)
    matches = slot_of[None, :] == slot_ids[:, None]
    present = jnp.any(matches, axis=1)
    source_image = jnp.sum(jnp.where(matches, jnp.arange(image_count)[None, :], 0), axis=1)

    def rows_of(array, chunk):
        images = array.reshape((image_count, image_rows) + array.shape[1:])
        piece = images[:, chunk * part_rows : (chunk + 1) * part_rows]
        return piece.reshape((image_count * part_rows,) + array.shape[1:])

    grads, hiddens, back_parts = [], [], []
    for chunk in range(CHUNKS):
        grads.append(ring_gather(rows_of(out_grad, chunk), tp_count))
    for chunk in range(CHUNKS):
        gelu_value, gelu_slope = gelu_parts(rows_of(pre_act, chunk).astype(jnp.float32))
        hiddens.append(gelu_value.astype(jnp.bfloat16))
        back_hidden = jnp.dot(grads[chunk], w_down, preferred_element_type=jnp.float32)
        back_parts.append((back_hidden * gelu_slope).astype(jnp.bfloat16))
    back_linears = [ring_gather(part, tp_count) for part in back_parts]

    grad_w2 = (
        ctx_scatter(sum(row_product(grads[k], hiddens[k]) for k in range(CHUNKS)), ctx_count)
        * grad_scale
    )

    received, gain_sum, bias_sum = [], 0.0, 0.0
    for chunk in range(CHUNKS):
        norm_grad = jnp.dot(back_linears[chunk], w_up, preferred_element_type=jnp.float32)
        features = rows_of(normed, chunk).astype(jnp.float32)
        gained = ln_gain[None, :] * norm_grad
        sums = jnp.stack([jnp.sum(gained, axis=-1), jnp.sum(gained * features, axis=-1)])
        means = tp_sum(sums, tp_count) / full_width
        visual = (
            rows_of(inverse_std, chunk)[:, None]
            * (gained - means[0][:, None] - features * means[1][:, None])
        ).astype(jnp.bfloat16)
        gain_sum += jnp.sum(norm_grad * features, axis=0)
        bias_sum += jnp.sum(norm_grad, axis=0)
        images = visual.reshape(image_count, part_rows, width)
        picked = jnp.take(images, source_image, axis=0)
        outgoing = jnp.where(
            present[:, None, None], picked, jnp.zeros((), jnp.bfloat16)
        ).reshape(tp_count, capacity, part_rows, width)
        received.append(lax.all_to_all(outgoing, "tp", split_axis=0, concat_axis=3, tiled=True))
    vit_grad = jnp.concatenate(received, axis=2).reshape(
        capacity * image_rows, width * tp_count
    )

    grad_w1 = (
        ctx_scatter(
            sum(row_product(back_linears[k], rows_of(normed, k)) for k in range(CHUNKS)), ctx_count
        )
        * grad_scale
    )
    small = jnp.concatenate(
        [
            jnp.sum(out_grad.astype(jnp.float32), axis=0),
            sum(jnp.sum(part.astype(jnp.float32), axis=0) for part in back_parts),
            gain_sum,
            bias_sum,
        ]
    )
    small = ctx_sum(small, ctx_count) * grad_scale
    features_in = out_grad.shape[1]
    hidden_in = pre_act.shape[1]
    bias_down = small[:features_in]
    bias_up = small[features_in : features_in + hidden_in]
    ln_grads = small[features_in + hidden_in :].reshape(2, width)
    return (grad_w2, grad_w1, bias_up, bias_down, ln_grads, vit_grad)


def solution(mesh):
    return jax.shard_map(
        per_device,
        mesh=mesh,
        in_specs=(
            P("ctx", "tp"),
            P("ctx", "tp"),
            P("ctx", "tp"),
            P("ctx"),
            P(None, "tp"),
            P(None, "tp"),
            P("tp"),
            P("ctx", None),
        ),
        out_specs=(
            P("ctx", "tp"),
            P("ctx", "tp"),
            P("tp"),
            P("tp"),
            P(None, "tp"),
            P(("ctx", "tp"), None),
        ),
        check_vma=False,
    )
```

```python
import functools
import math

import jax
import jax.numpy as jnp
from jax import lax
from jax.experimental import pallas as pl
from jax.experimental.pallas import tpu as pltpu
from jax.sharding import PartitionSpec as P

CHUNKS = 2
VMEM_LIMIT = 48 * 1024 * 1024


def gelu_parts(linear):
    normal_cdf = 0.5 * (1.0 + jax.scipy.special.erf(linear * 2.0 ** (-0.5)))
    density = jnp.exp(-0.5 * linear * linear) * (2.0 * math.pi) ** (-0.5)
    return (linear * normal_cdf, normal_cdf + linear * density)


def slot_numbers(owners, capacity):
    position = jnp.arange(owners.shape[0])
    earlier = (owners[None, :] == owners[:, None]) & (position[None, :] < position[:, None])
    return owners * capacity + jnp.sum(earlier.astype(jnp.int32), axis=1)


def divisor(extent, most, unit):
    return max(d for d in range(unit, most + 1, unit) if extent % d == 0)


def ring_order(count):
    depth = 4 if count % 4 == 0 else count
    width = count // depth
    walk = [(z, 0) for z in range(depth)]
    if width > 1:
        for turn, z in enumerate(reversed(range(depth))):
            ys = list(range(1, width))
            walk += [(z, y) for y in (ys if turn % 2 == 0 else ys[::-1])]
    return [z * width + y for z, y in walk]


def ring_owners(count):
    order = ring_order(count)
    table = []
    for j in range(count):
        at = order.index(j)
        steps = [0]
        for step in range(1, count // 2):
            steps += [-step, step]
        steps += [count // 2]
        table.append([order[(at + s) % count] for s in steps])
    return jnp.array(table, jnp.int32)[lax.axis_index("tp")]


def ring_blocks(block, count):
    order = ring_order(count)
    ahead = [(order[p], order[(p + 1) % count]) for p in range(count)]
    behind = [(order[p], order[(p - 1) % count]) for p in range(count)]
    up, down = block, block
    blocks = [block]
    for _ in range(1, count // 2):
        up = lax.ppermute(up, "tp", ahead)
        down = lax.ppermute(down, "tp", behind)
        blocks += [up, down]
    half = block.shape[0] // 2
    blocks.append(lax.ppermute(up[:half], "tp", ahead))
    blocks.append(lax.ppermute(down[half:], "tp", behind))
    return blocks


def assemble(owners_ref, block_refs, held, sems):
    rows, width = block_refs[0].shape
    half = rows // 2
    last = len(block_refs) - 2
    copies = []
    for k, ref in enumerate(block_refs):
        columns = pl.ds(pl.multiple_of(owners_ref[min(k, last)] * width, width), width)
        if k < last:
            target = held.at[:, columns]
        else:
            target = held.at[pl.ds((k - last) * half, half), columns]
        copies.append(pltpu.make_async_copy(ref, target, sems.at[k]))
    return copies


def back_kernel(tile, owners_ref, *refs):
    *block_refs, w_ref, slope_ref, back_ref, full_ref, held, sems, out_sem = refs
    copies = assemble(owners_ref, block_refs, held, sems)
    for copy in copies:
        copy.start()
    for copy in copies:
        copy.wait()
    out = pltpu.make_async_copy(held, full_ref, out_sem)
    out.start()

    @pl.loop(0, back_ref.shape[0] // tile)
    def _(step):
        rows = pl.ds(pl.multiple_of(step * tile, tile), tile)
        total = jnp.dot(held[rows, :], w_ref[...], preferred_element_type=jnp.float32)
        back_ref[rows, :] = (total * slope_ref[rows, :]).astype(back_ref.dtype)

    out.wait()


def back_part(owners, blocks, w_down, slope):
    rows, width = blocks[0].shape
    full = w_down.shape[0]
    tile = divisor(rows, 256, 16)
    return pl.pallas_call(
        functools.partial(back_kernel, tile),
        out_shape=(
            jax.ShapeDtypeStruct((rows, w_down.shape[1]), jnp.bfloat16),
            jax.ShapeDtypeStruct((rows, full), jnp.bfloat16),
        ),
        in_specs=[pl.BlockSpec(memory_space=pltpu.SMEM)]
        + [pl.BlockSpec(memory_space=pl.ANY)] * len(blocks)
        + [pl.BlockSpec(memory_space=pltpu.VMEM)] * 2,
        out_specs=(pl.BlockSpec(memory_space=pltpu.VMEM), pl.BlockSpec(memory_space=pl.ANY)),
        scratch_shapes=[
            pltpu.VMEM((rows, full), jnp.bfloat16),
            pltpu.SemaphoreType.DMA((len(blocks),)),
            pltpu.SemaphoreType.DMA,
        ],
        compiler_params=pltpu.CompilerParams(vmem_limit_bytes=VMEM_LIMIT),
        cost_estimate=pl.CostEstimate(
            flops=2 * rows * full * w_down.shape[1],
            bytes_accessed=2 * (2 * rows * full + full * w_down.shape[1]),
            transcendentals=0,
        ),
    )(owners, *blocks, w_down, slope)


def norm_kernel(owners_ref, *refs):
    *block_refs, w_ref, normed_ref, gain_ref, grad_ref, sums_ref, ln_ref, full_ref, held, sems, out_sem = refs
    step = pl.program_id(0)
    out = pltpu.make_async_copy(held, full_ref, out_sem)

    @pl.when(step == 0)
    def _():
        copies = assemble(owners_ref, block_refs, held, sems)
        for copy in copies:
            copy.start()
        for copy in copies:
            copy.wait()
        out.start()

    grad = lax.dot_general(
        w_ref[...], held[...], (((1,), (1,)), ((), ())), preferred_element_type=jnp.float32
    )
    grad_ref[...] = grad
    features = normed_ref[...].astype(jnp.float32)
    gained = gain_ref[...] * grad
    first = jnp.sum(gained, axis=0, keepdims=True)
    second = jnp.sum(gained * features, axis=0, keepdims=True)

    @pl.when(step == 0)
    def _():
        sums_ref[0:1, :] = first
        sums_ref[1:2, :] = second

    @pl.when(step > 0)
    def _():
        sums_ref[0:1, :] += first
        sums_ref[1:2, :] += second

    gains = jnp.sum(grad * features, axis=1, keepdims=True)
    biases = jnp.sum(grad, axis=1, keepdims=True)
    lane = lax.broadcasted_iota(jnp.int32, ln_ref.shape, 1)
    ln_ref[...] = jnp.where(lane == 0, gains, biases)

    @pl.when(step == pl.num_programs(0) - 1)
    def _():
        out.wait()


def norm_part(owners, blocks, w_up_t, normed_t, gain):
    rows = blocks[0].shape[0]
    width, full = w_up_t.shape
    tile = divisor(width, 400, 16)
    return pl.pallas_call(
        norm_kernel,
        grid=(width // tile,),
        out_shape=(
            jax.ShapeDtypeStruct((width, rows), jnp.float32),
            jax.ShapeDtypeStruct((2, rows), jnp.float32),
            jax.ShapeDtypeStruct((width, 128), jnp.float32),
            jax.ShapeDtypeStruct((rows, full), jnp.bfloat16),
        ),
        in_specs=[pl.BlockSpec(memory_space=pltpu.SMEM)]
        + [pl.BlockSpec(memory_space=pl.ANY)] * len(blocks)
        + [
            pl.BlockSpec((tile, full), lambda t: (t, 0)),
            pl.BlockSpec((tile, rows), lambda t: (t, 0)),
            pl.BlockSpec((tile, 1), lambda t: (t, 0)),
        ],
        out_specs=(
            pl.BlockSpec((tile, rows), lambda t: (t, 0)),
            pl.BlockSpec((2, rows), lambda t: (0, 0)),
            pl.BlockSpec((tile, 128), lambda t: (t, 0)),
            pl.BlockSpec(memory_space=pl.ANY),
        ),
        scratch_shapes=[
            pltpu.VMEM((rows, full), jnp.bfloat16),
            pltpu.SemaphoreType.DMA((len(blocks),)),
            pltpu.SemaphoreType.DMA,
        ],
        compiler_params=pltpu.CompilerParams(vmem_limit_bytes=VMEM_LIMIT),
        cost_estimate=pl.CostEstimate(
            flops=2 * rows * full * width,
            bytes_accessed=2 * (full * width + 2 * rows * full) + 6 * rows * width,
            transcendentals=0,
        ),
    )(owners, *blocks, w_up_t, normed_t, gain)


def visual_kernel(source_ref, present_ref, grad_ref, normed_ref, gain_ref, stats_ref, out_ref):
    slot = pl.program_id(0)

    @pl.when(present_ref[slot] == 0)
    def _():
        out_ref[...] = jnp.zeros_like(out_ref)

    @pl.when(present_ref[slot] != 0)
    def _():
        gained = gain_ref[...] * grad_ref[...]
        features = normed_ref[...].astype(jnp.float32)
        first, second, inverse = stats_ref[0:1, :], stats_ref[1:2, :], stats_ref[2:3, :]
        out_ref[0] = (inverse * (gained - first - features * second)).astype(out_ref.dtype)


def visual_slots(source, present, grad_t, normed_t, gain, stats, part_rows):
    width = grad_t.shape[0]
    slots = source.shape[0]
    picked = lambda s, source, present: (0, source[s])
    return pl.pallas_call(
        visual_kernel,
        grid_spec=pltpu.PrefetchScalarGridSpec(
            num_scalar_prefetch=2,
            grid=(slots,),
            in_specs=[
                pl.BlockSpec((width, part_rows), picked),
                pl.BlockSpec((width, part_rows), picked),
                pl.BlockSpec((width, 1), lambda s, source, present: (0, 0)),
                pl.BlockSpec((stats.shape[0], part_rows), picked),
            ],
            out_specs=pl.BlockSpec((1, width, part_rows), lambda s, source, present: (s, 0, 0)),
        ),
        out_shape=jax.ShapeDtypeStruct((slots, width, part_rows), jnp.bfloat16),
        compiler_params=pltpu.CompilerParams(vmem_limit_bytes=VMEM_LIMIT),
        cost_estimate=pl.CostEstimate(
            flops=6 * slots * width * part_rows,
            bytes_accessed=8 * slots * width * part_rows,
            transcendentals=0,
        ),
    )(source, present, grad_t, normed_t, gain, stats)


def turn_kernel(in_ref, *refs):
    refs[-1][...] = in_ref[...].T


def turn_rows(received, chunk, rows, so_far):
    full, part_rows = received.shape
    tile = divisor(full, 2560, 128)
    operands, specs, aliases = [received], [pl.BlockSpec((tile, part_rows), lambda t: (t, 0))], {}
    if so_far is not None:
        operands.append(so_far)
        specs.append(pl.BlockSpec(memory_space=pl.ANY))
        aliases = {1: 0}
    return pl.pallas_call(
        turn_kernel,
        grid=(full // tile,),
        in_specs=specs,
        out_specs=pl.BlockSpec((part_rows, tile), lambda t: (chunk, t)),
        out_shape=jax.ShapeDtypeStruct((rows, full), received.dtype),
        input_output_aliases=aliases,
        compiler_params=pltpu.CompilerParams(vmem_limit_bytes=VMEM_LIMIT),
        cost_estimate=pl.CostEstimate(
            flops=0, bytes_accessed=4 * part_rows * full, transcendentals=0
        ),
    )(*operands)


def core_swap(value, ctx_count):
    return lax.ppermute(value, "ctx", [(c, c ^ 1) for c in range(ctx_count)])


def chip_scatter(partial_for, ctx_count):
    index = lax.axis_index("ctx")
    pairs = ctx_count // 2
    arrived = []
    for shift in range(1, pairs):
        going = partial_for((index + 2 * shift) % ctx_count).astype(jnp.bfloat16)
        route = [(c, (c + 2 * shift) % ctx_count) for c in range(ctx_count)]
        arrived.append(lax.ppermute(going, "ctx", route))
    total = partial_for(index)
    for part in arrived:
        total = total + part.astype(jnp.float32)
    return total


def doubling_sum(value, axis, count):
    bit = 1
    while bit < count:
        value = value + lax.ppermute(value, axis, [(t, t ^ bit) for t in range(count)])
        bit *= 2
    return value


def column_pair(fulls, ctx_count, swap_width):
    index = lax.axis_index("ctx")
    core = index % 2
    pairs = ctx_count // 2

    def columns(full, member):
        return lax.dynamic_slice(full, (0, member * swap_width), (full.shape[0], swap_width))

    other = [
        core_swap(
            jnp.concatenate([columns(full, 2 * x + 1 - core) for x in range(pairs)], axis=0),
            ctx_count,
        )
        for full in fulls
    ]

    def of_member(member):
        chip = member // 2
        own = [columns(full, member) for full in fulls]
        swapped = []
        for full, other_part in zip(fulls, other):
            rows = full.shape[0]
            swapped.append(
                lax.dynamic_slice(other_part, (chip * rows, 0), (rows, swap_width))
            )
        return jnp.concatenate(own + swapped, axis=0)

    return of_member


def per_device(out_grad, pre_act, normed, inverse_std, w_up, w_down, ln_gain, owner_map):
    ctx_count = lax.axis_size("ctx")
    tp_count = lax.axis_size("tp")
    row_count = out_grad.shape[0]
    width = normed.shape[1]
    grad_scale = float(row_count * ctx_count) ** (-0.5)
    full_width = float(width * tp_count)

    owners = owner_map[0]
    image_count = owners.shape[0]
    image_rows = row_count // image_count
    part_rows = image_rows // CHUNKS
    chunk_rows = row_count // CHUNKS
    capacity = max(1, 2 * image_count // tp_count)
    slot_of = slot_numbers(owners, capacity)
    slot_ids = jnp.arange(tp_count * capacity)
    matches = slot_of[None, :] == slot_ids[:, None]
    present = jnp.any(matches, axis=1).astype(jnp.int32)
    source = jnp.sum(jnp.where(matches, jnp.arange(image_count)[None, :], 0), axis=1).astype(
        jnp.int32
    )

    def by_chunk(array):
        images = array.reshape((image_count, CHUNKS, part_rows) + array.shape[1:])
        return [
            images[:, k].reshape((chunk_rows,) + array.shape[1:]) for k in range(CHUNKS)
        ]

    ring = ring_owners(tp_count)
    grad_blocks = [ring_blocks(part, tp_count) for part in by_chunk(out_grad)]

    gelus = [gelu_parts(part.astype(jnp.float32)) for part in by_chunk(pre_act)]
    hidden = jnp.concatenate([value.astype(jnp.bfloat16) for value, _ in gelus], axis=0)
    hidden_pair = jnp.concatenate([hidden, core_swap(hidden, ctx_count)], axis=0)
    normed_parts = [
        part.T for part in by_chunk(normed)
    ]
    normed_all = jnp.concatenate(normed_parts, axis=1)
    normed_pair = jnp.concatenate([normed_all, core_swap(normed_all, ctx_count)], axis=1)
    gain = ln_gain[:, None]
    w_up_t = w_up.T

    back_parts, grads, back_blocks = [], [], []
    for chunk in range(CHUNKS):
        part, full = back_part(ring, grad_blocks[chunk], w_down, gelus[chunk][1])
        back_parts.append(part)
        grads.append(full)
        back_blocks.append(ring_blocks(part, tp_count))

    member_rows = grads[0].shape[1] // ctx_count
    grad_columns = column_pair(grads, ctx_count, member_rows)
    grad_w2 = chip_scatter(
        lambda d: lax.dot_general(
            grad_columns(d),
            hidden_pair,
            (((0,), (0,)), ((), ())),
            preferred_element_type=jnp.float32,
        )
        * grad_scale,
        ctx_count,
    )

    back_linears, ln_parts = [], []
    vit_grad = None
    inverse_parts = by_chunk(inverse_std)
    for chunk in range(CHUNKS):
        grad_t, sums, ln_part, full = norm_part(
            ring, back_blocks[chunk], w_up_t, normed_parts[chunk], gain
        )
        back_linears.append(full)
        ln_parts.append(ln_part[:, :2])
        means = doubling_sum(sums, "tp", tp_count) / full_width
        stats = jnp.concatenate([means, inverse_parts[chunk][None, :]], axis=0)
        outgoing = visual_slots(
            source, present, grad_t, normed_parts[chunk], gain, stats, part_rows
        )
        received = lax.all_to_all(outgoing, "tp", split_axis=0, concat_axis=0, tiled=True)
        assert capacity == 1
        vit_grad = turn_rows(
            received.reshape(tp_count * width, part_rows), chunk, image_rows, vit_grad
        )

    member_hidden = back_linears[0].shape[1] // ctx_count
    back_columns = column_pair(back_linears, ctx_count, member_hidden)
    grad_w1 = chip_scatter(
        lambda d: jnp.dot(normed_pair, back_columns(d), preferred_element_type=jnp.float32)
        * grad_scale,
        ctx_count,
    ).T

    small = jnp.concatenate(
        [
            jnp.sum(out_grad.astype(jnp.float32), axis=0),
            sum(jnp.sum(part.astype(jnp.float32), axis=0) for part in back_parts),
            sum(ln_parts).T.reshape(-1),
        ]
    )
    small = doubling_sum(small, "ctx", ctx_count) * grad_scale
    features_in = out_grad.shape[1]
    hidden_in = pre_act.shape[1]
    bias_down = small[:features_in]
    bias_up = small[features_in : features_in + hidden_in]
    ln_grads = small[features_in + hidden_in :].reshape(2, width)
    return (grad_w2, grad_w1, bias_up, bias_down, ln_grads, vit_grad)


def solution(mesh):
    return jax.shard_map(
        per_device,
        mesh=mesh,
        in_specs=(
            P("ctx", "tp"),
            P("ctx", "tp"),
            P("ctx", "tp"),
            P("ctx"),
            P(None, "tp"),
            P(None, "tp"),
            P("tp"),
            P("ctx", None),
        ),
        out_specs=(
            P("ctx", "tp"),
            P("ctx", "tp"),
            P("tp"),
            P("tp"),
            P(None, "tp"),
            P(("ctx", "tp"), None),
        ),
        check_vma=False,
    )
```

```python
import functools
import math

import jax
import jax.numpy as jnp
from jax import lax
from jax.experimental import pallas as pl
from jax.experimental.pallas import tpu as pltpu
from jax.sharding import PartitionSpec as P

CHUNKS = 2
VMEM_LIMIT = 48 * 1024 * 1024


def gelu_parts(linear):
    normal_cdf = 0.5 * (1.0 + jax.scipy.special.erf(linear * 2.0 ** (-0.5)))
    density = jnp.exp(-0.5 * linear * linear) * (2.0 * math.pi) ** (-0.5)
    return (linear * normal_cdf, normal_cdf + linear * density)


def slot_numbers(owners, capacity):
    position = jnp.arange(owners.shape[0])
    earlier = (owners[None, :] == owners[:, None]) & (position[None, :] < position[:, None])
    return owners * capacity + jnp.sum(earlier.astype(jnp.int32), axis=1)


def divisor(extent, most, unit):
    return max(d for d in range(unit, most + 1, unit) if extent % d == 0)


def ring_order(count):
    depth = 4 if count % 4 == 0 else count
    width = count // depth
    walk = [(z, 0) for z in range(depth)]
    if width > 1:
        for turn, z in enumerate(reversed(range(depth))):
            ys = list(range(1, width))
            walk += [(z, y) for y in (ys if turn % 2 == 0 else ys[::-1])]
    return [z * width + y for z, y in walk]


def ring_owners(count):
    order = ring_order(count)
    table = []
    for j in range(count):
        at = order.index(j)
        steps = [0]
        for step in range(1, count // 2):
            steps += [-step, step]
        steps += [count // 2]
        table.append([order[(at + s) % count] for s in steps])
    core = (lax.axis_index("ctx") % 2).astype(jnp.int32)
    return jnp.concatenate([jnp.array(table, jnp.int32)[lax.axis_index("tp")], core[None]])


def ring_blocks(block, count):
    order = ring_order(count)
    ahead = [(order[p], order[(p + 1) % count]) for p in range(count)]
    behind = [(order[p], order[(p - 1) % count]) for p in range(count)]
    up, down = block, block
    blocks = [block]
    for _ in range(1, count // 2):
        up = lax.ppermute(up, "tp", ahead)
        down = lax.ppermute(down, "tp", behind)
        blocks += [up, down]
    half = block.shape[0] // 2
    blocks.append(lax.ppermute(up[:half], "tp", ahead))
    blocks.append(lax.ppermute(down[half:], "tp", behind))
    return blocks


def assemble(owners_ref, block_refs, held, sems):
    rows, width = block_refs[0].shape
    half = rows // 2
    last = len(block_refs) - 2
    copies = []
    for k, ref in enumerate(block_refs):
        columns = pl.ds(pl.multiple_of(owners_ref[min(k, last)] * width, width), width)
        if k < last:
            target = held.at[:, columns]
        else:
            target = held.at[pl.ds((k - last) * half, half), columns]
        copies.append(pltpu.make_async_copy(ref, target, sems.at[k]))
    return copies


def spread(ring_ref, held, full_ref, swap_ref, chunk, image_rows, sems):
    rows, part_rows = held.shape[0], image_rows // CHUNKS
    all_rows, member_width = full_ref.shape[0], swap_ref.shape[1]
    other = 1 - ring_ref[ring_ref.shape[0] - 1]
    copies = []
    for i in range(rows // part_rows):
        source = pl.ds(i * part_rows, part_rows)
        place = i * image_rows + chunk * part_rows
        copies.append((held.at[source, :], full_ref.at[pl.ds(place, part_rows), :]))
        for chip in range(swap_ref.shape[0] // all_rows):
            columns = pl.ds(
                pl.multiple_of((2 * chip + other) * member_width, member_width), member_width
            )
            target = swap_ref.at[pl.ds(chip * all_rows + place, part_rows), :]
            copies.append((held.at[source, columns], target))
    return [
        pltpu.make_async_copy(source, target, sems.at[n])
        for n, (source, target) in enumerate(copies)
    ]


def spread_shapes(rows, chunk_rows, full, ctx_count, images):
    shapes = (
        jax.ShapeDtypeStruct((rows, full), jnp.bfloat16),
        jax.ShapeDtypeStruct((rows * (ctx_count // 2), full // ctx_count), jnp.bfloat16),
    )
    scratch = [
        pltpu.VMEM((chunk_rows, full), jnp.bfloat16),
        pltpu.SemaphoreType.DMA((2 * tp_most(),)),
        pltpu.SemaphoreType.DMA((images * (1 + ctx_count // 2),)),
    ]
    return shapes, scratch


def tp_most():
    return lax.axis_size("tp")


def back_kernel(chunk, image_rows, blocks, carried, ring_ref, *refs):
    block_refs, refs = refs[:blocks], refs[blocks:]
    w_ref, slope_ref, *refs = refs
    back_ref, sum_ref, full_ref, swap_ref, held, sems, out_sems = refs[carried:]
    copies = assemble(ring_ref, block_refs, held, sems)
    for copy in copies:
        copy.start()
    for copy in copies:
        copy.wait()
    outs = spread(ring_ref, held, full_ref, swap_ref, chunk, image_rows, out_sems)
    for copy in outs:
        copy.start()
    rows, part_rows = held.shape[0], image_rows // CHUNKS
    tile = divisor(rows, 256, part_rows)
    sums = jnp.zeros(sum_ref.shape, jnp.float32)
    for start in range(0, rows, tile):
        total = jnp.dot(
            held[start : start + tile, :], w_ref[...], preferred_element_type=jnp.float32
        )
        for n in range(tile // part_rows):
            image = start // part_rows + n
            place = image * image_rows + chunk * part_rows
            part = (
                total[n * part_rows : (n + 1) * part_rows]
                * slope_ref[place : place + part_rows, :]
            ).astype(back_ref.dtype)
            back_ref[image * part_rows : (image + 1) * part_rows, :] = part
            sums += jnp.sum(part.astype(jnp.float32), axis=0, keepdims=True)
    sum_ref[...] = sums
    for copy in outs:
        copy.wait()


def back_part(ring, blocks, w_down, slope, chunk, image_rows, ctx_count, so_far):
    rows = blocks[0].shape[0]
    full, width = w_down.shape
    images = slope.shape[0] // image_rows
    shapes, scratch = spread_shapes(slope.shape[0], rows, full, ctx_count, images)
    first = 1 + len(blocks) + 2
    return pl.pallas_call(
        functools.partial(back_kernel, chunk, image_rows, len(blocks), len(so_far)),
        out_shape=(
            jax.ShapeDtypeStruct((rows, width), jnp.bfloat16),
            jax.ShapeDtypeStruct((1, width), jnp.float32),
        )
        + shapes,
        in_specs=[pl.BlockSpec(memory_space=pltpu.SMEM)]
        + [pl.BlockSpec(memory_space=pl.ANY)] * len(blocks)
        + [pl.BlockSpec(memory_space=pltpu.VMEM)] * 2
        + [pl.BlockSpec(memory_space=pl.ANY)] * len(so_far),
        out_specs=(pl.BlockSpec(memory_space=pltpu.VMEM),) * 2
        + (pl.BlockSpec(memory_space=pl.ANY),) * 2,
        scratch_shapes=scratch,
        input_output_aliases={first + n: 2 + n for n in range(len(so_far))},
        compiler_params=pltpu.CompilerParams(vmem_limit_bytes=VMEM_LIMIT),
        cost_estimate=pl.CostEstimate(
            flops=2 * rows * full * width,
            bytes_accessed=2 * (2 * rows * full + full * width),
            transcendentals=0,
        ),
    )(ring, *blocks, w_down, slope, *so_far)


def norm_kernel(chunk, image_rows, blocks, images, carried, ring_ref, *refs):
    block_refs, refs = refs[:blocks], refs[blocks:]
    w_ref, gain_ref, *refs = refs
    normed_refs, refs = refs[:images], refs[images:]
    grad_ref, sums_ref, ln_ref, full_ref, swap_ref, held, sems, out_sems = refs[carried:]
    step = pl.program_id(0)
    outs = spread(ring_ref, held, full_ref, swap_ref, chunk, image_rows, out_sems)

    @pl.when(step == 0)
    def _():
        copies = assemble(ring_ref, block_refs, held, sems)
        for copy in copies:
            copy.start()
        for copy in copies:
            copy.wait()
        for copy in outs:
            copy.start()
        sums_ref[...] = jnp.zeros_like(sums_ref)

    grad = lax.dot_general(
        w_ref[...], held[...], (((1,), (1,)), ((), ())), preferred_element_type=jnp.float32
    )
    grad_ref[...] = grad
    features = jnp.concatenate([ref[...] for ref in normed_refs], axis=1).astype(jnp.float32)
    gained = gain_ref[...] * grad
    sums_ref[0:1, :] += jnp.sum(gained, axis=0, keepdims=True)
    sums_ref[1:2, :] += jnp.sum(gained * features, axis=0, keepdims=True)
    gains = jnp.sum(grad * features, axis=1, keepdims=True)
    biases = jnp.sum(grad, axis=1, keepdims=True)
    lane = lax.broadcasted_iota(jnp.int32, ln_ref.shape, 1)
    ln_ref[...] = jnp.where(lane == 0, gains, biases)

    @pl.when(step == pl.num_programs(0) - 1)
    def _():
        for copy in outs:
            copy.wait()


def norm_part(ring, blocks, w_up_t, gain, normed_t, chunk, image_rows, ctx_count, so_far):
    rows = blocks[0].shape[0]
    width, full = w_up_t.shape
    part_rows = image_rows // CHUNKS
    images = rows // part_rows
    tile = divisor(width, 400, 16)
    shapes, scratch = spread_shapes(normed_t.shape[1], rows, full, ctx_count, images)
    first = 1 + len(blocks) + 2 + images
    return pl.pallas_call(
        functools.partial(norm_kernel, chunk, image_rows, len(blocks), images, len(so_far)),
        grid=(width // tile,),
        out_shape=(
            jax.ShapeDtypeStruct((width, rows), jnp.float32),
            jax.ShapeDtypeStruct((2, rows), jnp.float32),
            jax.ShapeDtypeStruct((width, 128), jnp.float32),
        )
        + shapes,
        in_specs=[pl.BlockSpec(memory_space=pltpu.SMEM)]
        + [pl.BlockSpec(memory_space=pl.ANY)] * len(blocks)
        + [
            pl.BlockSpec((tile, full), lambda t: (t, 0)),
            pl.BlockSpec((tile, 1), lambda t: (t, 0)),
        ]
        + [
            pl.BlockSpec((tile, part_rows), lambda t, i=i: (t, i * CHUNKS + chunk))
            for i in range(images)
        ]
        + [pl.BlockSpec(memory_space=pl.ANY)] * len(so_far),
        out_specs=(
            pl.BlockSpec((tile, rows), lambda t: (t, 0)),
            pl.BlockSpec((2, rows), lambda t: (0, 0)),
            pl.BlockSpec((tile, 128), lambda t: (t, 0)),
        )
        + (pl.BlockSpec(memory_space=pl.ANY),) * 2,
        scratch_shapes=scratch,
        input_output_aliases={first + n: 3 + n for n in range(len(so_far))},
        compiler_params=pltpu.CompilerParams(vmem_limit_bytes=VMEM_LIMIT),
        cost_estimate=pl.CostEstimate(
            flops=2 * rows * full * width,
            bytes_accessed=2 * (full * width + 2 * rows * full) + 6 * rows * width,
            transcendentals=0,
        ),
    )(ring, *blocks, w_up_t, gain, *[normed_t] * images, *so_far)


def pair_kernel(contract, scale, member_ref, a_ref, a_other_ref, b_ref, b_other_ref, *refs):
    *arrived, out_ref = refs
    dims = (contract, ((), ()))
    total = lax.dot_general(a_ref[...], b_ref[...], dims, preferred_element_type=jnp.float32)
    total += lax.dot_general(
        a_other_ref[...], b_other_ref[...], dims, preferred_element_type=jnp.float32
    )
    total *= scale
    for ref in arrived:
        total += ref[...].astype(jnp.float32)
    out_ref[...] = total.astype(out_ref.dtype)


def pair_product(operands, specs, contract, shape, tile, depth, member, scale, arrived, dtype):
    out_spec = pl.BlockSpec((tile, shape[1]), lambda t, m: (t, 0))
    return pl.pallas_call(
        functools.partial(pair_kernel, contract, scale),
        grid_spec=pltpu.PrefetchScalarGridSpec(
            num_scalar_prefetch=1,
            grid=(shape[0] // tile,),
            in_specs=specs + [out_spec] * len(arrived),
            out_specs=out_spec,
        ),
        out_shape=jax.ShapeDtypeStruct(shape, dtype),
        compiler_params=pltpu.CompilerParams(vmem_limit_bytes=VMEM_LIMIT),
        cost_estimate=pl.CostEstimate(
            flops=4 * shape[0] * shape[1] * depth,
            bytes_accessed=4 * depth * (shape[0] + shape[1]) + 4 * shape[0] * shape[1],
            transcendentals=0,
        ),
    )(member.reshape(1).astype(jnp.int32), *operands, *arrived)


def chip_scatter(product, ctx_count):
    index = lax.axis_index("ctx")
    arrived = []
    for shift in range(1, ctx_count // 2):
        going = product((index + 2 * shift) % ctx_count, [], jnp.bfloat16)
        route = [(c, (c + 2 * shift) % ctx_count) for c in range(ctx_count)]
        arrived.append(lax.ppermute(going, "ctx", route))
    return product(index, arrived, jnp.float32)


def tie_kernel(*refs):
    del refs


def tie(value, *others):
    anywhere = pl.BlockSpec(memory_space=pl.ANY)
    return pl.pallas_call(
        tie_kernel,
        in_specs=[anywhere] * (1 + len(others)),
        out_specs=anywhere,
        out_shape=jax.ShapeDtypeStruct(value.shape, value.dtype),
        input_output_aliases={0: 0},
    )(value, *others)


def visual_kernel(
    source_ref, present_ref, grad_ref, normed_ref, gain_ref, means_ref, inverse_ref, out_ref
):
    slot = pl.program_id(0)

    @pl.when(present_ref[slot] == 0)
    def _():
        out_ref[...] = jnp.zeros_like(out_ref)

    @pl.when(present_ref[slot] != 0)
    def _():
        gained = gain_ref[...] * grad_ref[...]
        features = normed_ref[...].astype(jnp.float32)
        first, second = means_ref[0:1, :], means_ref[1:2, :]
        out_ref[0] = (inverse_ref[...] * (gained - first - features * second)).astype(
            out_ref.dtype
        )


def visual_slots(source, present, grad_t, normed_t, gain, means, inverse, chunk, part_rows):
    width = grad_t.shape[0]
    slots = source.shape[0]
    picked = lambda s, source, present: (0, source[s])
    natural = lambda s, source, present: (0, source[s] * CHUNKS + chunk)
    return pl.pallas_call(
        visual_kernel,
        grid_spec=pltpu.PrefetchScalarGridSpec(
            num_scalar_prefetch=2,
            grid=(slots,),
            in_specs=[
                pl.BlockSpec((width, part_rows), picked),
                pl.BlockSpec((width, part_rows), natural),
                pl.BlockSpec((width, 1), lambda s, source, present: (0, 0)),
                pl.BlockSpec((2, part_rows), picked),
                pl.BlockSpec((1, part_rows), natural),
            ],
            out_specs=pl.BlockSpec((1, width, part_rows), lambda s, source, present: (s, 0, 0)),
        ),
        out_shape=jax.ShapeDtypeStruct((slots, width, part_rows), jnp.bfloat16),
        compiler_params=pltpu.CompilerParams(vmem_limit_bytes=VMEM_LIMIT),
        cost_estimate=pl.CostEstimate(
            flops=6 * slots * width * part_rows,
            bytes_accessed=8 * slots * width * part_rows,
            transcendentals=0,
        ),
    )(source, present, grad_t, normed_t, gain, means, inverse)


def turn_kernel(in_ref, *refs):
    refs[-1][...] = in_ref[...].T


def turn_rows(received, chunk, rows, so_far):
    full, part_rows = received.shape
    tile = divisor(full, 2560, 128)
    operands, specs, aliases = [received], [pl.BlockSpec((tile, part_rows), lambda t: (t, 0))], {}
    if so_far is not None:
        operands.append(so_far)
        specs.append(pl.BlockSpec(memory_space=pl.ANY))
        aliases = {1: 0}
    return pl.pallas_call(
        turn_kernel,
        grid=(full // tile,),
        in_specs=specs,
        out_specs=pl.BlockSpec((part_rows, tile), lambda t: (chunk, t)),
        out_shape=jax.ShapeDtypeStruct((rows, full), received.dtype),
        input_output_aliases=aliases,
        compiler_params=pltpu.CompilerParams(vmem_limit_bytes=VMEM_LIMIT),
        cost_estimate=pl.CostEstimate(
            flops=0, bytes_accessed=4 * part_rows * full, transcendentals=0
        ),
    )(*operands)


def core_swap(value, ctx_count):
    return lax.ppermute(value, "ctx", [(c, c ^ 1) for c in range(ctx_count)])


def doubling_sum(value, axis, count):
    bit = 1
    while bit < count:
        value = value + lax.ppermute(value, axis, [(t, t ^ bit) for t in range(count)])
        bit *= 2
    return value


def per_device(out_grad, pre_act, normed, inverse_std, w_up, w_down, ln_gain, owner_map):
    ctx_count = lax.axis_size("ctx")
    tp_count = lax.axis_size("tp")
    row_count = out_grad.shape[0]
    width = normed.shape[1]
    grad_scale = float(row_count * ctx_count) ** (-0.5)
    full_width = float(width * tp_count)

    owners = owner_map[0]
    image_count = owners.shape[0]
    image_rows = row_count // image_count
    part_rows = image_rows // CHUNKS
    chunk_rows = row_count // CHUNKS
    capacity = max(1, 2 * image_count // tp_count)
    slot_of = slot_numbers(owners, capacity)
    slot_ids = jnp.arange(tp_count * capacity)
    matches = slot_of[None, :] == slot_ids[:, None]
    present = jnp.any(matches, axis=1).astype(jnp.int32)
    source = jnp.sum(jnp.where(matches, jnp.arange(image_count)[None, :], 0), axis=1).astype(
        jnp.int32
    )

    def chunk_of(array, chunk):
        images = array.reshape((image_count, image_rows) + array.shape[1:])
        piece = images[:, chunk * part_rows : (chunk + 1) * part_rows]
        return piece.reshape((chunk_rows,) + array.shape[1:])

    ring = ring_owners(tp_count)
    grad_blocks = [ring_blocks(chunk_of(out_grad, k), tp_count) for k in range(CHUNKS)]

    gelu_value, slope = gelu_parts(pre_act.astype(jnp.float32))
    hidden = gelu_value.astype(jnp.bfloat16)
    hidden_other = core_swap(hidden, ctx_count)
    normed_t = normed.T
    normed_other = core_swap(normed_t, ctx_count)
    gain = ln_gain[:, None]
    w_up_t = w_up.T

    back_sum, back_blocks, so_far = 0.0, [], ()
    for chunk in range(CHUNKS):
        part, part_sum, *so_far = back_part(
            ring, grad_blocks[chunk], w_down, slope, chunk, image_rows, ctx_count, so_far
        )
        back_sum += part_sum[0]
        back_blocks.append(ring_blocks(part, tp_count))
    grads, grads_swap = so_far
    grads_other = core_swap(grads_swap, ctx_count)

    def grad_w2_share(member, arrived, dtype):
        share, local = grads.shape[1] // ctx_count, hidden.shape[1]
        tile = divisor(share, 256, 128)
        steps = share // tile
        return pair_product(
            (grads, grads_other, hidden, hidden_other),
            [
                pl.BlockSpec((row_count, tile), lambda t, m: (0, m[0] * steps + t)),
                pl.BlockSpec((row_count, tile), lambda t, m: (m[0] // 2, t)),
                pl.BlockSpec((row_count, local), lambda t, m: (0, 0)),
                pl.BlockSpec((row_count, local), lambda t, m: (0, 0)),
            ],
            ((0,), (0,)), (share, local), tile, row_count, member, grad_scale, arrived, dtype,
        )

    grad_w2 = chip_scatter(grad_w2_share, ctx_count)

    ln_sum, vit_grad, so_far = 0.0, None, ()
    for chunk in range(CHUNKS):
        grad_t, sums, ln_part, *so_far = norm_part(
            ring, back_blocks[chunk], w_up_t, gain, normed_t, chunk, image_rows, ctx_count, so_far
        )
        ln_sum += ln_part[:, :2]
        means = doubling_sum(sums, "tp", tp_count) / full_width
        outgoing = visual_slots(
            source, present, grad_t, normed_t, gain, means, inverse_std[None, :], chunk, part_rows
        )
        if chunk + 1 < CHUNKS:
            outgoing = tie(outgoing, *back_blocks[-1][-2:])
        received = lax.all_to_all(outgoing, "tp", split_axis=0, concat_axis=0, tiled=True)
        assert capacity == 1
        vit_grad = turn_rows(
            received.reshape(tp_count * width, part_rows), chunk, image_rows, vit_grad
        )
    backs, backs_swap = so_far
    backs_other = core_swap(backs_swap, ctx_count)

    def grad_w1_share(member, arrived, dtype):
        share = backs.shape[1] // ctx_count
        tile = divisor(width, 400, 16)
        return pair_product(
            (normed_t, normed_other, backs, backs_other),
            [
                pl.BlockSpec((tile, row_count), lambda t, m: (t, 0)),
                pl.BlockSpec((tile, row_count), lambda t, m: (t, 0)),
                pl.BlockSpec((row_count, share), lambda t, m: (0, m[0])),
                pl.BlockSpec((row_count, share), lambda t, m: (m[0] // 2, 0)),
            ],
            ((1,), (0,)), (width, share), tile, row_count, member, grad_scale, arrived, dtype,
        )

    grad_w1 = chip_scatter(grad_w1_share, ctx_count).T

    small = jnp.concatenate(
        [jnp.sum(out_grad.astype(jnp.float32), axis=0), back_sum, ln_sum.T.reshape(-1)]
    )
    small = doubling_sum(small, "ctx", ctx_count) * grad_scale
    features_in = out_grad.shape[1]
    hidden_in = pre_act.shape[1]
    bias_down = small[:features_in]
    bias_up = small[features_in : features_in + hidden_in]
    ln_grads = small[features_in + hidden_in :].reshape(2, width)
    return (grad_w2, grad_w1, bias_up, bias_down, ln_grads, vit_grad)


def solution(mesh):
    return jax.shard_map(
        per_device,
        mesh=mesh,
        in_specs=(
            P("ctx", "tp"),
            P("ctx", "tp"),
            P("ctx", "tp"),
            P("ctx"),
            P(None, "tp"),
            P(None, "tp"),
            P("tp"),
            P("ctx", None),
        ),
        out_specs=(
            P("ctx", "tp"),
            P("ctx", "tp"),
            P("tp"),
            P("tp"),
            P(None, "tp"),
            P(("ctx", "tp"), None),
        ),
        check_vma=False,
    )
```

```python
import functools
import math

import jax
import jax.numpy as jnp
from jax import lax
from jax.experimental import pallas as pl
from jax.experimental.pallas import tpu as pltpu
from jax.sharding import PartitionSpec as P

CHUNKS = 2
VMEM_LIMIT = 60 * 1024 * 1024


def gelu_parts(linear):
    normal_cdf = 0.5 * (1.0 + jax.scipy.special.erf(linear * 2.0 ** (-0.5)))
    density = jnp.exp(-0.5 * linear * linear) * (2.0 * math.pi) ** (-0.5)
    return (linear * normal_cdf, normal_cdf + linear * density)


def slot_numbers(owners, capacity):
    position = jnp.arange(owners.shape[0])
    earlier = (owners[None, :] == owners[:, None]) & (position[None, :] < position[:, None])
    return owners * capacity + jnp.sum(earlier.astype(jnp.int32), axis=1)


def divisor(extent, most, unit):
    return max(d for d in range(unit, most + 1, unit) if extent % d == 0)


def ring_order(count):
    depth = 4 if count % 4 == 0 else count
    width = count // depth
    walk = [(z, 0) for z in range(depth)]
    if width > 1:
        for turn, z in enumerate(reversed(range(depth))):
            ys = list(range(1, width))
            walk += [(z, y) for y in (ys if turn % 2 == 0 else ys[::-1])]
    return [z * width + y for z, y in walk]


def ring_owners(count):
    order = ring_order(count)
    table = []
    for j in range(count):
        at = order.index(j)
        steps = [0]
        for step in range(1, count // 2):
            steps += [-step, step]
        steps += [count // 2]
        table.append([order[(at + s) % count] for s in steps])
    core = (lax.axis_index("ctx") % 2).astype(jnp.int32)
    return jnp.concatenate([jnp.array(table, jnp.int32)[lax.axis_index("tp")], core[None]])


def ring_blocks(block, count):
    order = ring_order(count)
    ahead = [(order[p], order[(p + 1) % count]) for p in range(count)]
    behind = [(order[p], order[(p - 1) % count]) for p in range(count)]
    up, down = block, block
    blocks = [block]
    for _ in range(1, count // 2):
        up = lax.ppermute(up, "tp", ahead)
        down = lax.ppermute(down, "tp", behind)
        blocks += [up, down]
    half = block.shape[0] // 2
    blocks.append(lax.ppermute(up[:half], "tp", ahead))
    blocks.append(lax.ppermute(down[half:], "tp", behind))
    return blocks


def assemble(owners_ref, block_refs, held, sems):
    rows, width = block_refs[0].shape
    half = rows // 2
    last = len(block_refs) - 2
    copies = []
    for k, ref in enumerate(block_refs):
        columns = pl.ds(pl.multiple_of(owners_ref[min(k, last)] * width, width), width)
        if k < last:
            target = held.at[:, columns]
        else:
            target = held.at[pl.ds((k - last) * half, half), columns]
        copies.append(pltpu.make_async_copy(ref, target, sems.at[k]))
    return copies


def spread(ring_ref, held, full_ref, swap_ref, chunk, image_rows, sems):
    rows, part_rows = held.shape[0], image_rows // CHUNKS
    all_rows, member_width = full_ref.shape[0], swap_ref.shape[1]
    other = 1 - ring_ref[ring_ref.shape[0] - 1]
    copies = []
    for i in range(rows // part_rows):
        source = pl.ds(i * part_rows, part_rows)
        place = i * image_rows + chunk * part_rows
        copies.append((held.at[source, :], full_ref.at[pl.ds(place, part_rows), :]))
        for chip in range(swap_ref.shape[0] // all_rows):
            columns = pl.ds(
                pl.multiple_of((2 * chip + other) * member_width, member_width), member_width
            )
            target = swap_ref.at[pl.ds(chip * all_rows + place, part_rows), :]
            copies.append((held.at[source, columns], target))
    return [
        pltpu.make_async_copy(source, target, sems.at[n])
        for n, (source, target) in enumerate(copies)
    ]


def spread_shapes(rows, chunk_rows, full, ctx_count, images):
    shapes = (
        jax.ShapeDtypeStruct((rows, full), jnp.bfloat16),
        jax.ShapeDtypeStruct((rows * (ctx_count // 2), full // ctx_count), jnp.bfloat16),
    )
    scratch = [
        pltpu.VMEM((chunk_rows, full), jnp.bfloat16),
        pltpu.SemaphoreType.DMA((2 * tp_most(),)),
        pltpu.SemaphoreType.DMA((images * (1 + ctx_count // 2),)),
    ]
    return shapes, scratch


def tp_most():
    return lax.axis_size("tp")


def back_kernel(chunk, image_rows, blocks, carried, ring_ref, *refs):
    block_refs, refs = refs[:blocks], refs[blocks:]
    w_ref, slope_ref, *refs = refs
    back_ref, sum_ref, full_ref, swap_ref, held, sems, out_sems = refs[carried:]
    copies = assemble(ring_ref, block_refs, held, sems)
    for copy in copies:
        copy.start()
    for copy in copies:
        copy.wait()
    outs = spread(ring_ref, held, full_ref, swap_ref, chunk, image_rows, out_sems)
    for copy in outs:
        copy.start()
    rows, part_rows = held.shape[0], image_rows // CHUNKS
    tile = divisor(rows, 256, part_rows)
    sums = jnp.zeros(sum_ref.shape, jnp.float32)
    for start in range(0, rows, tile):
        total = jnp.dot(
            held[start : start + tile, :], w_ref[...], preferred_element_type=jnp.float32
        )
        for n in range(tile // part_rows):
            image = start // part_rows + n
            place = image * image_rows + chunk * part_rows
            part = (
                total[n * part_rows : (n + 1) * part_rows]
                * slope_ref[place : place + part_rows, :]
            ).astype(back_ref.dtype)
            back_ref[image * part_rows : (image + 1) * part_rows, :] = part
            sums += jnp.sum(part.astype(jnp.float32), axis=0, keepdims=True)
    sum_ref[...] = sums
    for copy in outs:
        copy.wait()


def back_part(ring, blocks, w_down, slope, chunk, image_rows, ctx_count, so_far):
    rows = blocks[0].shape[0]
    full, width = w_down.shape
    images = slope.shape[0] // image_rows
    shapes, scratch = spread_shapes(slope.shape[0], rows, full, ctx_count, images)
    first = 1 + len(blocks) + 2
    return pl.pallas_call(
        functools.partial(back_kernel, chunk, image_rows, len(blocks), len(so_far)),
        out_shape=(
            jax.ShapeDtypeStruct((rows, width), jnp.bfloat16),
            jax.ShapeDtypeStruct((1, width), jnp.float32),
        )
        + shapes,
        in_specs=[pl.BlockSpec(memory_space=pltpu.SMEM)]
        + [pl.BlockSpec(memory_space=pltpu.HBM)] * len(blocks)
        + [pl.BlockSpec(memory_space=pltpu.VMEM)] * 2
        + [pl.BlockSpec(memory_space=pltpu.HBM)] * len(so_far),
        out_specs=(pl.BlockSpec(memory_space=pltpu.VMEM),) * 2
        + (pl.BlockSpec(memory_space=pltpu.HBM),) * 2,
        scratch_shapes=scratch,
        input_output_aliases={first + n: 2 + n for n in range(len(so_far))},
        compiler_params=pltpu.CompilerParams(vmem_limit_bytes=VMEM_LIMIT),
        cost_estimate=pl.CostEstimate(
            flops=2 * rows * full * width,
            bytes_accessed=2 * (2 * rows * full + full * width),
            transcendentals=0,
        ),
    )(ring, *blocks, w_down, slope, *so_far)


def norm_kernel(chunk, image_rows, blocks, images, carried, ring_ref, *refs):
    block_refs, refs = refs[:blocks], refs[blocks:]
    w_ref, gain_ref, *refs = refs
    normed_refs, refs = refs[:images], refs[images:]
    grad_ref, sums_ref, ln_ref, full_ref, swap_ref, held, sems, out_sems = refs[carried:]
    step = pl.program_id(0)
    outs = spread(ring_ref, held, full_ref, swap_ref, chunk, image_rows, out_sems)

    @pl.when(step == 0)
    def _():
        copies = assemble(ring_ref, block_refs, held, sems)
        for copy in copies:
            copy.start()
        for copy in copies:
            copy.wait()
        for copy in outs:
            copy.start()
        sums_ref[...] = jnp.zeros_like(sums_ref)

    grad = lax.dot_general(
        w_ref[...], held[...], (((1,), (1,)), ((), ())), preferred_element_type=jnp.float32
    )
    grad_ref[...] = grad
    features = jnp.concatenate([ref[...] for ref in normed_refs], axis=1).astype(jnp.float32)
    gained = gain_ref[...] * grad
    sums_ref[0:1, :] += jnp.sum(gained, axis=0, keepdims=True)
    sums_ref[1:2, :] += jnp.sum(gained * features, axis=0, keepdims=True)
    gains = jnp.sum(grad * features, axis=1, keepdims=True)
    biases = jnp.sum(grad, axis=1, keepdims=True)
    lane = lax.broadcasted_iota(jnp.int32, ln_ref.shape, 1)
    ln_ref[...] = jnp.where(lane == 0, gains, biases)

    @pl.when(step == pl.num_programs(0) - 1)
    def _():
        for copy in outs:
            copy.wait()


def norm_part(ring, blocks, w_up_t, gain, normed_t, chunk, image_rows, ctx_count, so_far, after):
    rows = blocks[0].shape[0]
    width, full = w_up_t.shape
    part_rows = image_rows // CHUNKS
    images = rows // part_rows
    tile = divisor(width, 400, 16)
    shapes, scratch = spread_shapes(normed_t.shape[1], rows, full, ctx_count, images)
    first = 1 + len(blocks) + 2 + images
    return pl.pallas_call(
        functools.partial(
            norm_kernel, chunk, image_rows, len(blocks), images, len(so_far) + len(after)
        ),
        grid=(width // tile,),
        out_shape=(
            jax.ShapeDtypeStruct((width, rows), jnp.float32),
            jax.ShapeDtypeStruct((2, rows), jnp.float32),
            jax.ShapeDtypeStruct((width, 128), jnp.float32),
        )
        + shapes,
        in_specs=[pl.BlockSpec(memory_space=pltpu.SMEM)]
        + [pl.BlockSpec(memory_space=pltpu.HBM)] * len(blocks)
        + [
            pl.BlockSpec((tile, full), lambda t: (t, 0)),
            pl.BlockSpec((tile, 1), lambda t: (t, 0)),
        ]
        + [
            pl.BlockSpec((tile, part_rows), lambda t, i=i: (t, i * CHUNKS + chunk))
            for i in range(images)
        ]
        + [pl.BlockSpec(memory_space=pltpu.HBM)] * (len(so_far) + len(after)),
        out_specs=(
            pl.BlockSpec((tile, rows), lambda t: (t, 0)),
            pl.BlockSpec((2, rows), lambda t: (0, 0)),
            pl.BlockSpec((tile, 128), lambda t: (t, 0)),
        )
        + (pl.BlockSpec(memory_space=pltpu.HBM),) * 2,
        scratch_shapes=scratch,
        input_output_aliases={first + n: 3 + n for n in range(len(so_far))},
        compiler_params=pltpu.CompilerParams(vmem_limit_bytes=VMEM_LIMIT),
        cost_estimate=pl.CostEstimate(
            flops=2 * rows * full * width,
            bytes_accessed=2 * (full * width + 2 * rows * full) + 6 * rows * width,
            transcendentals=0,
        ),
    )(ring, *blocks, w_up_t, gain, *[normed_t] * images, *so_far, *after)


def pair_kernel(
    contract, scale, arrivals, member_ref, a_ref, a_other_ref, b_ref, b_other_ref, *refs
):
    arrived, out_ref = refs[:arrivals], refs[-1]
    dims = (contract, ((), ()))
    total = lax.dot_general(a_ref[...], b_ref[...], dims, preferred_element_type=jnp.float32)
    total += lax.dot_general(
        a_other_ref[...], b_other_ref[...], dims, preferred_element_type=jnp.float32
    )
    total *= scale
    for ref in arrived:
        total += ref[...].astype(jnp.float32)
    out_ref[...] = total.astype(out_ref.dtype)


def pair_product(
    operands, specs, contract, shape, tile, depth, member, scale, arrived, dtype, after
):
    out_spec = pl.BlockSpec((tile, shape[1]), lambda t, m: (t, 0))
    return pl.pallas_call(
        functools.partial(pair_kernel, contract, scale, len(arrived)),
        grid_spec=pltpu.PrefetchScalarGridSpec(
            num_scalar_prefetch=1,
            grid=(shape[0] // tile,),
            in_specs=specs
            + [out_spec] * len(arrived)
            + [pl.BlockSpec(memory_space=pltpu.HBM)] * len(after),
            out_specs=out_spec,
        ),
        out_shape=jax.ShapeDtypeStruct(shape, dtype),
        compiler_params=pltpu.CompilerParams(vmem_limit_bytes=VMEM_LIMIT),
        cost_estimate=pl.CostEstimate(
            flops=4 * shape[0] * shape[1] * depth,
            bytes_accessed=4 * depth * (shape[0] + shape[1]) + 4 * shape[0] * shape[1],
            transcendentals=0,
        ),
    )(member.reshape(1).astype(jnp.int32), *operands, *arrived, *after)


def chip_products(product, ctx_count, after):
    index = lax.axis_index("ctx")
    going, arrived = [], []
    for shift in range(1, ctx_count // 2):
        going.append(product((index + 2 * shift) % ctx_count, [], jnp.bfloat16, after))
        route = [(c, (c + 2 * shift) % ctx_count) for c in range(ctx_count)]
        arrived.append(lax.ppermute(going[-1], "ctx", route))
    return going, arrived


def tie_kernel(*refs):
    del refs


def tie(value, *others):
    anywhere = pl.BlockSpec(memory_space=pltpu.HBM)
    return pl.pallas_call(
        tie_kernel,
        in_specs=[anywhere] * (1 + len(others)),
        out_specs=anywhere,
        out_shape=jax.ShapeDtypeStruct(value.shape, value.dtype),
        input_output_aliases={0: 0},
        compiler_params=pltpu.CompilerParams(vmem_limit_bytes=VMEM_LIMIT),
    )(value, *others)


def visual_kernel(
    source_ref, present_ref, grad_ref, normed_ref, gain_ref, means_ref, inverse_ref, *refs
):
    out_ref = refs[-1]
    slot = pl.program_id(0)

    @pl.when(present_ref[slot] == 0)
    def _():
        out_ref[...] = jnp.zeros_like(out_ref)

    @pl.when(present_ref[slot] != 0)
    def _():
        gained = gain_ref[...] * grad_ref[...]
        features = normed_ref[...].astype(jnp.float32)
        first, second = means_ref[0:1, :], means_ref[1:2, :]
        out_ref[0] = (inverse_ref[...] * (gained - first - features * second)).astype(
            out_ref.dtype
        )


def visual_slots(source, present, grad_t, normed_t, gain, means, inverse, chunk, part_rows, after):
    width = grad_t.shape[0]
    slots = source.shape[0]
    picked = lambda s, source, present: (0, source[s])
    natural = lambda s, source, present: (0, source[s] * CHUNKS + chunk)
    return pl.pallas_call(
        visual_kernel,
        grid_spec=pltpu.PrefetchScalarGridSpec(
            num_scalar_prefetch=2,
            grid=(slots,),
            in_specs=[
                pl.BlockSpec((width, part_rows), picked),
                pl.BlockSpec((width, part_rows), natural),
                pl.BlockSpec((width, 1), lambda s, source, present: (0, 0)),
                pl.BlockSpec((2, part_rows), picked),
                pl.BlockSpec((1, part_rows), natural),
            ]
            + [pl.BlockSpec(memory_space=pltpu.HBM)] * len(after),
            out_specs=pl.BlockSpec((1, width, part_rows), lambda s, source, present: (s, 0, 0)),
        ),
        out_shape=jax.ShapeDtypeStruct((slots, width, part_rows), jnp.bfloat16),
        compiler_params=pltpu.CompilerParams(vmem_limit_bytes=VMEM_LIMIT),
        cost_estimate=pl.CostEstimate(
            flops=6 * slots * width * part_rows,
            bytes_accessed=8 * slots * width * part_rows,
            transcendentals=0,
        ),
    )(source, present, grad_t, normed_t, gain, means, inverse, *after)


def turn_kernel(in_ref, *refs):
    refs[-1][...] = in_ref[...].T


def turn_rows(received, chunk, rows, so_far, after):
    full, part_rows = received.shape
    tile = divisor(full, 2560, 128)
    operands, aliases = [received], {}
    if so_far is not None:
        operands.append(so_far)
        aliases = {1: 0}
    operands += after
    specs = [pl.BlockSpec((tile, part_rows), lambda t: (t, 0))]
    specs += [pl.BlockSpec(memory_space=pltpu.HBM)] * (len(operands) - 1)
    return pl.pallas_call(
        turn_kernel,
        grid=(full // tile,),
        in_specs=specs,
        out_specs=pl.BlockSpec((part_rows, tile), lambda t: (chunk, t)),
        out_shape=jax.ShapeDtypeStruct((rows, full), received.dtype),
        input_output_aliases=aliases,
        compiler_params=pltpu.CompilerParams(vmem_limit_bytes=VMEM_LIMIT),
        cost_estimate=pl.CostEstimate(
            flops=0, bytes_accessed=4 * part_rows * full, transcendentals=0
        ),
    )(*operands)


def core_swap(value, ctx_count):
    return lax.ppermute(value, "ctx", [(c, c ^ 1) for c in range(ctx_count)])


def doubling_sum(value, axis, count):
    bit = 1
    while bit < count:
        value = value + lax.ppermute(value, axis, [(t, t ^ bit) for t in range(count)])
        bit *= 2
    return value


def per_device(out_grad, pre_act, normed, inverse_std, w_up, w_down, ln_gain, owner_map):
    ctx_count = lax.axis_size("ctx")
    tp_count = lax.axis_size("tp")
    row_count = out_grad.shape[0]
    width = normed.shape[1]
    grad_scale = float(row_count * ctx_count) ** (-0.5)
    full_width = float(width * tp_count)

    owners = owner_map[0]
    image_count = owners.shape[0]
    image_rows = row_count // image_count
    part_rows = image_rows // CHUNKS
    chunk_rows = row_count // CHUNKS
    capacity = max(1, 2 * image_count // tp_count)
    slot_of = slot_numbers(owners, capacity)
    slot_ids = jnp.arange(tp_count * capacity)
    matches = slot_of[None, :] == slot_ids[:, None]
    present = jnp.any(matches, axis=1).astype(jnp.int32)
    source = jnp.sum(jnp.where(matches, jnp.arange(image_count)[None, :], 0), axis=1).astype(
        jnp.int32
    )

    def chunk_of(array, chunk):
        images = array.reshape((image_count, image_rows) + array.shape[1:])
        piece = images[:, chunk * part_rows : (chunk + 1) * part_rows]
        return piece.reshape((chunk_rows,) + array.shape[1:])

    ring = ring_owners(tp_count)
    grad_blocks = []
    for chunk in range(CHUNKS):
        block = chunk_of(out_grad, chunk)
        if chunk > 0:
            block = tie(block, *grad_blocks[-1][3:5])
        grad_blocks.append(ring_blocks(block, tp_count))

    gelu_value, slope = gelu_parts(pre_act.astype(jnp.float32))
    hidden = gelu_value.astype(jnp.bfloat16)
    hidden_other = core_swap(hidden, ctx_count)
    normed_t = normed.T
    normed_other = core_swap(normed_t, ctx_count)
    gain = ln_gain[:, None]
    w_up_t = w_up.T

    back_sum, back_blocks, so_far = 0.0, [], ()
    for chunk in range(CHUNKS):
        part, part_sum, *so_far = back_part(
            ring, grad_blocks[chunk], w_down, slope, chunk, image_rows, ctx_count, so_far
        )
        back_sum += part_sum[0]
        back_blocks.append(ring_blocks(part, tp_count))
    grads, grads_swap = so_far
    grads_other = core_swap(grads_swap, ctx_count)

    def grad_w2_share(member, arrived, dtype, after):
        share, local = grads.shape[1] // ctx_count, hidden.shape[1]
        tile = divisor(share, 256, 128)
        steps = share // tile
        return pair_product(
            (grads, grads_other, hidden, hidden_other),
            [
                pl.BlockSpec((row_count, tile), lambda t, m: (0, m[0] * steps + t)),
                pl.BlockSpec((row_count, tile), lambda t, m: (m[0] // 2, t)),
                pl.BlockSpec((row_count, local), lambda t, m: (0, 0)),
                pl.BlockSpec((row_count, local), lambda t, m: (0, 0)),
            ],
            ((0,), (0,)), (share, local), tile, row_count, member, grad_scale, arrived, dtype,
            after,
        )

    going_w2, arrived_w2 = chip_products(grad_w2_share, ctx_count, [])

    member = lax.axis_index("ctx")
    grad_ts, chunk_means, ln_sum, so_far = [], [], 0.0, ()
    for chunk in range(CHUNKS):
        grad_t, sums, ln_part, *so_far = norm_part(
            ring,
            back_blocks[chunk],
            w_up_t,
            gain,
            normed_t,
            chunk,
            image_rows,
            ctx_count,
            so_far,
            going_w2,
        )
        ln_sum += ln_part[:, :2]
        grad_ts.append(grad_t)
        chunk_means.append(doubling_sum(sums, "tp", tp_count) / full_width)
    backs, backs_swap = so_far
    backs_other = core_swap(backs_swap, ctx_count)
    small = jnp.concatenate(
        [jnp.sum(out_grad.astype(jnp.float32), axis=0), back_sum, ln_sum.T.reshape(-1)]
    )
    small = doubling_sum(small, "ctx", ctx_count) * grad_scale
    grad_w2 = grad_w2_share(member, arrived_w2, jnp.float32, [])

    def grad_w1_share(member, arrived, dtype, after):
        share = backs.shape[1] // ctx_count
        tile = divisor(width, 400, 16)
        return pair_product(
            (normed_t, normed_other, backs, backs_other),
            [
                pl.BlockSpec((tile, row_count), lambda t, m: (t, 0)),
                pl.BlockSpec((tile, row_count), lambda t, m: (t, 0)),
                pl.BlockSpec((row_count, share), lambda t, m: (0, m[0])),
                pl.BlockSpec((row_count, share), lambda t, m: (m[0] // 2, 0)),
            ],
            ((1,), (0,)), (width, share), tile, row_count, member, grad_scale, arrived, dtype,
            after,
        )

    going_w1, arrived_w1 = chip_products(grad_w1_share, ctx_count, [small])

    received = []
    for chunk in range(CHUNKS):
        last = chunk + 1 == CHUNKS
        outgoing = visual_slots(
            source,
            present,
            grad_ts[chunk],
            normed_t,
            gain,
            chunk_means[chunk],
            inverse_std[None, :],
            chunk,
            part_rows,
            going_w1 + [grad_w2] if last else [],
        )
        if not last:
            outgoing = tie(outgoing, *back_blocks[-1][-2:])
        received.append(lax.all_to_all(outgoing, "tp", split_axis=0, concat_axis=0, tiled=True))
    grad_w1_t = grad_w1_share(member, arrived_w1, jnp.float32, [])
    assert capacity == 1
    vit_grad = None
    for chunk in range(CHUNKS):
        columns = received[chunk].reshape(tp_count * width, part_rows)
        after = [grad_w1_t] if chunk + 1 == CHUNKS else []
        vit_grad = turn_rows(columns, chunk, image_rows, vit_grad, after)

    features_in = out_grad.shape[1]
    hidden_in = pre_act.shape[1]
    bias_down = small[:features_in]
    bias_up = small[features_in : features_in + hidden_in]
    ln_grads = small[features_in + hidden_in :].reshape(2, width)
    return (grad_w2, grad_w1_t.T, bias_up, bias_down, ln_grads, vit_grad)


def solution(mesh):
    return jax.shard_map(
        per_device,
        mesh=mesh,
        in_specs=(
            P("ctx", "tp"),
            P("ctx", "tp"),
            P("ctx", "tp"),
            P("ctx"),
            P(None, "tp"),
            P(None, "tp"),
            P("tp"),
            P("ctx", None),
        ),
        out_specs=(
            P("ctx", "tp"),
            P("ctx", "tp"),
            P("tp"),
            P("tp"),
            P(None, "tp"),
            P(("ctx", "tp"), None),
        ),
        check_vma=False,
    )
```

```python
import functools
import math

import jax
import jax.numpy as jnp
from jax import lax
from jax.experimental import pallas as pl
from jax.experimental.pallas import tpu as pltpu
from jax.sharding import PartitionSpec as P

CHUNKS = 2
VMEM_LIMIT = 48 * 1024 * 1024


def gelu_parts(linear):
    normal_cdf = 0.5 * (1.0 + jax.scipy.special.erf(linear * 2.0 ** (-0.5)))
    density = jnp.exp(-0.5 * linear * linear) * (2.0 * math.pi) ** (-0.5)
    return (linear * normal_cdf, normal_cdf + linear * density)


def slot_numbers(owners, capacity):
    position = jnp.arange(owners.shape[0])
    earlier = (owners[None, :] == owners[:, None]) & (position[None, :] < position[:, None])
    return owners * capacity + jnp.sum(earlier.astype(jnp.int32), axis=1)


def divisor(extent, most, unit):
    return max(d for d in range(unit, most + 1, unit) if extent % d == 0)


def ring_order(count):
    depth = 4 if count % 4 == 0 else count
    width = count // depth
    walk = [(z, 0) for z in range(depth)]
    if width > 1:
        for turn, z in enumerate(reversed(range(depth))):
            ys = list(range(1, width))
            walk += [(z, y) for y in (ys if turn % 2 == 0 else ys[::-1])]
    return [z * width + y for z, y in walk]


def ring_owners(count):
    order = ring_order(count)
    table = []
    for j in range(count):
        at = order.index(j)
        steps = [0]
        for step in range(1, count // 2):
            steps += [-step, step]
        steps += [count // 2]
        table.append([order[(at + s) % count] for s in steps])
    core = (lax.axis_index("ctx") % 2).astype(jnp.int32)
    return jnp.concatenate([jnp.array(table, jnp.int32)[lax.axis_index("tp")], core[None]])


def ring_blocks(block, count, after=()):
    order = ring_order(count)
    ahead = [(order[p], order[(p + 1) % count]) for p in range(count)]
    behind = [(order[p], order[(p - 1) % count]) for p in range(count)]
    blocks = [block]
    for step in range(1, count // 2 + 1):
        waits = after[step - 1] if step <= len(after) else []
        if waits:
            blocks[-2:] = tie(blocks[-2:], waits)
        up, down = blocks[-2:] if step > 1 else blocks * 2
        if step == count // 2:
            half = block.shape[0] // 2
            up, down = up[:half], down[half:]
        blocks += [lax.ppermute(up, "tp", ahead), lax.ppermute(down, "tp", behind)]
    return blocks


def assemble(owners_ref, block_refs, held, sems):
    rows, width = block_refs[0].shape
    half = rows // 2
    last = len(block_refs) - 2
    copies = []
    for k, ref in enumerate(block_refs):
        columns = pl.ds(pl.multiple_of(owners_ref[min(k, last)] * width, width), width)
        if k < last:
            target = held.at[:, columns]
        else:
            target = held.at[pl.ds((k - last) * half, half), columns]
        copies.append(pltpu.make_async_copy(ref, target, sems.at[k]))
    return copies


def spread(ring_ref, held, full_ref, swap_ref, chunk, image_rows, sems):
    rows, part_rows = held.shape[0], image_rows // CHUNKS
    all_rows, member_width = full_ref.shape[0], swap_ref.shape[1]
    other = 1 - ring_ref[ring_ref.shape[0] - 1]
    copies = []
    for i in range(rows // part_rows):
        source = pl.ds(i * part_rows, part_rows)
        place = i * image_rows + chunk * part_rows
        copies.append((held.at[source, :], full_ref.at[pl.ds(place, part_rows), :]))
        for chip in range(swap_ref.shape[0] // all_rows):
            columns = pl.ds(
                pl.multiple_of((2 * chip + other) * member_width, member_width), member_width
            )
            target = swap_ref.at[pl.ds(chip * all_rows + place, part_rows), :]
            copies.append((held.at[source, columns], target))
    return [
        pltpu.make_async_copy(source, target, sems.at[n])
        for n, (source, target) in enumerate(copies)
    ]


def spread_shapes(rows, chunk_rows, full, ctx_count, images):
    shapes = (
        jax.ShapeDtypeStruct((rows, full), jnp.bfloat16),
        jax.ShapeDtypeStruct((rows * (ctx_count // 2), full // ctx_count), jnp.bfloat16),
    )
    scratch = [
        pltpu.VMEM((chunk_rows, full), jnp.bfloat16),
        pltpu.SemaphoreType.DMA((2 * tp_most(),)),
        pltpu.SemaphoreType.DMA((images * (1 + ctx_count // 2),)),
    ]
    return shapes, scratch


def tp_most():
    return lax.axis_size("tp")


def back_kernel(chunk, image_rows, blocks, carried, ring_ref, *refs):
    block_refs, refs = refs[:blocks], refs[blocks:]
    w_ref, slope_ref, *refs = refs
    back_ref, sum_ref, full_ref, swap_ref, held, sems, out_sems = refs[carried:]
    copies = assemble(ring_ref, block_refs, held, sems)
    for copy in copies:
        copy.start()
    for copy in copies:
        copy.wait()
    outs = spread(ring_ref, held, full_ref, swap_ref, chunk, image_rows, out_sems)
    for copy in outs:
        copy.start()
    rows, part_rows = held.shape[0], image_rows // CHUNKS
    tile = divisor(rows, 256, part_rows)
    sums = jnp.zeros(sum_ref.shape, jnp.float32)
    for start in range(0, rows, tile):
        total = jnp.dot(
            held[start : start + tile, :], w_ref[...], preferred_element_type=jnp.float32
        )
        for n in range(tile // part_rows):
            image = start // part_rows + n
            place = image * image_rows + chunk * part_rows
            part = (
                total[n * part_rows : (n + 1) * part_rows]
                * slope_ref[place : place + part_rows, :]
            ).astype(back_ref.dtype)
            back_ref[image * part_rows : (image + 1) * part_rows, :] = part
            sums += jnp.sum(part.astype(jnp.float32), axis=0, keepdims=True)
    sum_ref[...] = sums
    for copy in outs:
        copy.wait()


def back_part(ring, blocks, w_down, slope, chunk, image_rows, ctx_count, so_far):
    rows = blocks[0].shape[0]
    full, width = w_down.shape
    images = slope.shape[0] // image_rows
    shapes, scratch = spread_shapes(slope.shape[0], rows, full, ctx_count, images)
    first = 1 + len(blocks) + 2
    return pl.pallas_call(
        functools.partial(back_kernel, chunk, image_rows, len(blocks), len(so_far)),
        out_shape=(
            jax.ShapeDtypeStruct((rows, width), jnp.bfloat16),
            jax.ShapeDtypeStruct((1, width), jnp.float32),
        )
        + shapes,
        in_specs=[pl.BlockSpec(memory_space=pltpu.SMEM)]
        + [pl.BlockSpec(memory_space=pl.ANY)] * len(blocks)
        + [pl.BlockSpec(memory_space=pltpu.VMEM)] * 2
        + [pl.BlockSpec(memory_space=pltpu.HBM)] * len(so_far),
        out_specs=(pl.BlockSpec(memory_space=pltpu.VMEM),) * 2
        + (pl.BlockSpec(memory_space=pltpu.HBM),) * 2,
        scratch_shapes=scratch,
        input_output_aliases={first + n: 2 + n for n in range(len(so_far))},
        compiler_params=pltpu.CompilerParams(vmem_limit_bytes=VMEM_LIMIT),
        cost_estimate=pl.CostEstimate(
            flops=2 * rows * full * width,
            bytes_accessed=2 * (2 * rows * full + full * width),
            transcendentals=0,
        ),
    )(ring, *blocks, w_down, slope, *so_far)


def norm_kernel(chunk, image_rows, blocks, images, carried, ring_ref, *refs):
    block_refs, refs = refs[:blocks], refs[blocks:]
    w_ref, gain_ref, *refs = refs
    normed_refs, refs = refs[:images], refs[images:]
    grad_ref, sums_ref, ln_ref, full_ref, swap_ref, held, sems, out_sems = refs[carried:]
    step = pl.program_id(0)
    outs = spread(ring_ref, held, full_ref, swap_ref, chunk, image_rows, out_sems)

    @pl.when(step == 0)
    def _():
        copies = assemble(ring_ref, block_refs, held, sems)
        for copy in copies:
            copy.start()
        for copy in copies:
            copy.wait()
        for copy in outs:
            copy.start()
        sums_ref[...] = jnp.zeros_like(sums_ref)

    grad = lax.dot_general(
        w_ref[...], held[...], (((1,), (1,)), ((), ())), preferred_element_type=jnp.float32
    )
    grad_ref[...] = grad
    features = jnp.concatenate([ref[...] for ref in normed_refs], axis=1).astype(jnp.float32)
    gained = gain_ref[...] * grad
    sums_ref[0:1, :] += jnp.sum(gained, axis=0, keepdims=True)
    sums_ref[1:2, :] += jnp.sum(gained * features, axis=0, keepdims=True)
    gains = jnp.sum(grad * features, axis=1, keepdims=True)
    biases = jnp.sum(grad, axis=1, keepdims=True)
    lane = lax.broadcasted_iota(jnp.int32, ln_ref.shape, 1)
    ln_ref[...] = jnp.where(lane == 0, gains, biases)

    @pl.when(step == pl.num_programs(0) - 1)
    def _():
        for copy in outs:
            copy.wait()


def norm_part(ring, blocks, w_up_t, gain, normed_t, chunk, image_rows, ctx_count, so_far, after):
    rows = blocks[0].shape[0]
    width, full = w_up_t.shape
    part_rows = image_rows // CHUNKS
    images = rows // part_rows
    tile = divisor(width, 400, 16)
    shapes, scratch = spread_shapes(normed_t.shape[1], rows, full, ctx_count, images)
    first = 1 + len(blocks) + 2 + images
    return pl.pallas_call(
        functools.partial(
            norm_kernel, chunk, image_rows, len(blocks), images, len(so_far) + len(after)
        ),
        grid=(width // tile,),
        out_shape=(
            jax.ShapeDtypeStruct((width, rows), jnp.float32),
            jax.ShapeDtypeStruct((2, rows), jnp.float32),
            jax.ShapeDtypeStruct((width, 128), jnp.float32),
        )
        + shapes,
        in_specs=[pl.BlockSpec(memory_space=pltpu.SMEM)]
        + [pl.BlockSpec(memory_space=pl.ANY)] * len(blocks)
        + [
            pl.BlockSpec((tile, full), lambda t: (t, 0)),
            pl.BlockSpec((tile, 1), lambda t: (t, 0)),
        ]
        + [
            pl.BlockSpec((tile, part_rows), lambda t, i=i: (t, i * CHUNKS + chunk))
            for i in range(images)
        ]
        + [pl.BlockSpec(memory_space=pltpu.HBM)] * (len(so_far) + len(after)),
        out_specs=(
            pl.BlockSpec((tile, rows), lambda t: (t, 0)),
            pl.BlockSpec((2, rows), lambda t: (0, 0)),
            pl.BlockSpec((tile, 128), lambda t: (t, 0)),
        )
        + (pl.BlockSpec(memory_space=pltpu.HBM),) * 2,
        scratch_shapes=scratch,
        input_output_aliases={first + n: 3 + n for n in range(len(so_far))},
        compiler_params=pltpu.CompilerParams(vmem_limit_bytes=VMEM_LIMIT),
        cost_estimate=pl.CostEstimate(
            flops=2 * rows * full * width,
            bytes_accessed=2 * (full * width + 2 * rows * full) + 6 * rows * width,
            transcendentals=0,
        ),
    )(ring, *blocks, w_up_t, gain, *[normed_t] * images, *so_far, *after)


def pair_kernel(
    contract, scale, arrivals, member_ref, a_ref, a_other_ref, b_ref, b_other_ref, *refs
):
    arrived, out_ref = refs[:arrivals], refs[-1]
    dims = (contract, ((), ()))
    total = lax.dot_general(a_ref[...], b_ref[...], dims, preferred_element_type=jnp.float32)
    total += lax.dot_general(
        a_other_ref[...], b_other_ref[...], dims, preferred_element_type=jnp.float32
    )
    total *= scale
    for ref in arrived:
        total += ref[...].astype(jnp.float32)
    out_ref[...] = total.astype(out_ref.dtype)


def pair_product(
    operands, specs, contract, shape, tile, depth, member, scale, arrived, dtype, after
):
    out_spec = pl.BlockSpec((tile, shape[1]), lambda t, m: (t, 0))
    return pl.pallas_call(
        functools.partial(pair_kernel, contract, scale, len(arrived)),
        grid_spec=pltpu.PrefetchScalarGridSpec(
            num_scalar_prefetch=1,
            grid=(shape[0] // tile,),
            in_specs=specs
            + [out_spec] * len(arrived)
            + [pl.BlockSpec(memory_space=pltpu.HBM)] * len(after),
            out_specs=out_spec,
        ),
        out_shape=jax.ShapeDtypeStruct(shape, dtype),
        compiler_params=pltpu.CompilerParams(vmem_limit_bytes=VMEM_LIMIT),
        cost_estimate=pl.CostEstimate(
            flops=4 * shape[0] * shape[1] * depth,
            bytes_accessed=4 * depth * (shape[0] + shape[1]) + 4 * shape[0] * shape[1],
            transcendentals=0,
        ),
    )(member.reshape(1).astype(jnp.int32), *operands, *arrived, *after)


def chip_products(product, ctx_count, after):
    index = lax.axis_index("ctx")
    going, arrived = [], []
    for shift in range(1, ctx_count // 2):
        going.append(product((index + 2 * shift) % ctx_count, [], jnp.bfloat16, after))
        route = [(c, (c + 2 * shift) % ctx_count) for c in range(ctx_count)]
        arrived.append(lax.ppermute(going[-1], "ctx", route))
    return going, arrived


def tie_kernel(*refs):
    del refs


def tie(values, others):
    return pl.pallas_call(
        tie_kernel,
        in_specs=[pl.BlockSpec(memory_space=pl.ANY)] * (len(values) + len(others)),
        out_specs=[pl.BlockSpec(memory_space=pl.ANY)] * len(values),
        out_shape=[jax.ShapeDtypeStruct(value.shape, value.dtype) for value in values],
        input_output_aliases={n: n for n in range(len(values))},
        compiler_params=pltpu.CompilerParams(vmem_limit_bytes=VMEM_LIMIT),
    )(*values, *others)


def visual_kernel(
    source_ref, present_ref, grad_ref, normed_ref, gain_ref, means_ref, inverse_ref, *refs
):
    out_ref = refs[-1]
    slot = pl.program_id(0)

    @pl.when(present_ref[slot] == 0)
    def _():
        out_ref[...] = jnp.zeros_like(out_ref)

    @pl.when(present_ref[slot] != 0)
    def _():
        gained = gain_ref[...] * grad_ref[...]
        features = normed_ref[...].astype(jnp.float32)
        first, second = means_ref[0:1, :], means_ref[1:2, :]
        out_ref[0] = (inverse_ref[...] * (gained - first - features * second)).astype(
            out_ref.dtype
        )


def visual_slots(source, present, grad_t, normed_t, gain, means, inverse, chunk, part_rows, after):
    width = grad_t.shape[0]
    slots = source.shape[0]
    picked = lambda s, source, present: (0, source[s])
    natural = lambda s, source, present: (0, source[s] * CHUNKS + chunk)
    return pl.pallas_call(
        visual_kernel,
        grid_spec=pltpu.PrefetchScalarGridSpec(
            num_scalar_prefetch=2,
            grid=(slots,),
            in_specs=[
                pl.BlockSpec((width, part_rows), picked),
                pl.BlockSpec((width, part_rows), natural),
                pl.BlockSpec((width, 1), lambda s, source, present: (0, 0)),
                pl.BlockSpec((2, part_rows), picked),
                pl.BlockSpec((1, part_rows), natural),
            ]
            + [pl.BlockSpec(memory_space=pltpu.HBM)] * len(after),
            out_specs=pl.BlockSpec((1, width, part_rows), lambda s, source, present: (s, 0, 0)),
        ),
        out_shape=jax.ShapeDtypeStruct((slots, width, part_rows), jnp.bfloat16),
        compiler_params=pltpu.CompilerParams(vmem_limit_bytes=VMEM_LIMIT),
        cost_estimate=pl.CostEstimate(
            flops=6 * slots * width * part_rows,
            bytes_accessed=8 * slots * width * part_rows,
            transcendentals=0,
        ),
    )(source, present, grad_t, normed_t, gain, means, inverse, *after)


def turn_kernel(in_ref, *refs):
    refs[-1][...] = in_ref[...].T


def turn_rows(received, chunk, rows, so_far, after):
    full, part_rows = received.shape
    tile = divisor(full, 2560, 128)
    operands, aliases = [received], {}
    if so_far is not None:
        operands.append(so_far)
        aliases = {1: 0}
    operands += after
    specs = [pl.BlockSpec((tile, part_rows), lambda t: (t, 0))]
    specs += [pl.BlockSpec(memory_space=pltpu.HBM)] * (len(operands) - 1)
    return pl.pallas_call(
        turn_kernel,
        grid=(full // tile,),
        in_specs=specs,
        out_specs=pl.BlockSpec((part_rows, tile), lambda t: (chunk, t)),
        out_shape=jax.ShapeDtypeStruct((rows, full), received.dtype),
        input_output_aliases=aliases,
        compiler_params=pltpu.CompilerParams(vmem_limit_bytes=VMEM_LIMIT),
        cost_estimate=pl.CostEstimate(
            flops=0, bytes_accessed=4 * part_rows * full, transcendentals=0
        ),
    )(*operands)


def core_swap(value, ctx_count):
    return lax.ppermute(value, "ctx", [(c, c ^ 1) for c in range(ctx_count)])


def doubling_sum(value, axis, count, after=()):
    bit = 1
    while bit < count:
        if after and 2 * bit >= count:
            (value,) = tie([value], after)
        value = value + lax.ppermute(value, axis, [(t, t ^ bit) for t in range(count)])
        bit *= 2
    return value


def per_device(out_grad, pre_act, normed, inverse_std, w_up, w_down, ln_gain, owner_map):
    ctx_count = lax.axis_size("ctx")
    tp_count = lax.axis_size("tp")
    row_count = out_grad.shape[0]
    width = normed.shape[1]
    grad_scale = float(row_count * ctx_count) ** (-0.5)
    full_width = float(width * tp_count)

    owners = owner_map[0]
    image_count = owners.shape[0]
    image_rows = row_count // image_count
    part_rows = image_rows // CHUNKS
    chunk_rows = row_count // CHUNKS
    capacity = max(1, 2 * image_count // tp_count)
    slot_of = slot_numbers(owners, capacity)
    slot_ids = jnp.arange(tp_count * capacity)
    matches = slot_of[None, :] == slot_ids[:, None]
    present = jnp.any(matches, axis=1).astype(jnp.int32)
    source = jnp.sum(jnp.where(matches, jnp.arange(image_count)[None, :], 0), axis=1).astype(
        jnp.int32
    )

    def chunk_of(array, chunk):
        images = array.reshape((image_count, image_rows) + array.shape[1:])
        piece = images[:, chunk * part_rows : (chunk + 1) * part_rows]
        return piece.reshape((chunk_rows,) + array.shape[1:])

    ring = ring_owners(tp_count)
    gelu_value, slope = gelu_parts(pre_act.astype(jnp.float32))
    hidden = gelu_value.astype(jnp.bfloat16)
    hidden_other = core_swap(hidden, ctx_count)
    normed_t = normed.T
    normed_other = core_swap(normed_t, ctx_count)
    gain = ln_gain[:, None]
    w_up_t = w_up.T

    def back_of(chunk, blocks, so_far):
        return back_part(ring, blocks, w_down, slope, chunk, image_rows, ctx_count, so_far)

    def steps(blocks):
        return [blocks[n : n + 2] for n in range(1, len(blocks), 2)]

    first_grads = ring_blocks(chunk_of(out_grad, 0), tp_count)
    first_back, first_sum, *so_far = back_of(0, first_grads, ())
    first_backs = ring_blocks(first_back, tp_count)
    second_grads = ring_blocks(
        chunk_of(out_grad, 1), tp_count, steps(first_grads)[1:] + steps(first_backs)[:1]
    )
    second_back, second_sum, grads, grads_swap = back_of(1, second_grads, so_far)
    grads_other = core_swap(grads_swap, ctx_count)
    back_sum = first_sum[0] + second_sum[0]

    def grad_w2_share(member, arrived, dtype, after):
        share, local = grads.shape[1] // ctx_count, hidden.shape[1]
        tile = divisor(share, 256, 128)
        steps = share // tile
        return pair_product(
            (grads, grads_other, hidden, hidden_other),
            [
                pl.BlockSpec((row_count, tile), lambda t, m: (0, m[0] * steps + t)),
                pl.BlockSpec((row_count, tile), lambda t, m: (m[0] // 2, t)),
                pl.BlockSpec((row_count, local), lambda t, m: (0, 0)),
                pl.BlockSpec((row_count, local), lambda t, m: (0, 0)),
            ],
            ((0,), (0,)), (share, local), tile, row_count, member, grad_scale, arrived, dtype,
            after,
        )

    going_w2, arrived_w2 = chip_products(grad_w2_share, ctx_count, [])
    waits = steps(first_backs)[1:]
    waits[1] = waits[1] + going_w2
    second_backs = ring_blocks(second_back, tp_count, waits)

    member = lax.axis_index("ctx")
    grad_w2 = grad_w2_share(member, arrived_w2, jnp.float32, [])

    def norm_of(chunk, blocks, so_far, after):
        return norm_part(
            ring, blocks, w_up_t, gain, normed_t, chunk, image_rows, ctx_count, so_far, after
        )

    def slots_of(chunk, grad_t, means):
        return visual_slots(
            source, present, grad_t, normed_t, gain, means, inverse_std[None, :], chunk, part_rows, []
        )

    first_grad, first_rows, first_ln, *so_far = norm_of(0, first_backs, (), [])
    first_means = doubling_sum(first_rows, "tp", tp_count) / full_width
    outgoing = [*tie([slots_of(0, first_grad, first_means)], second_backs[-2:])]
    second_grad, second_rows, second_ln, backs, backs_swap = norm_of(
        1, second_backs, so_far, outgoing
    )
    backs_other = core_swap(backs_swap, ctx_count)

    def grad_w1_share(member, arrived, dtype, after):
        share = backs.shape[1] // ctx_count
        tile = divisor(width, 400, 16)
        return pair_product(
            (normed_t, normed_other, backs, backs_other),
            [
                pl.BlockSpec((tile, row_count), lambda t, m: (t, 0)),
                pl.BlockSpec((tile, row_count), lambda t, m: (t, 0)),
                pl.BlockSpec((row_count, share), lambda t, m: (0, m[0])),
                pl.BlockSpec((row_count, share), lambda t, m: (m[0] // 2, 0)),
            ],
            ((1,), (0,)), (width, share), tile, row_count, member, grad_scale, arrived, dtype,
            after,
        )

    going_w1, arrived_w1 = chip_products(grad_w1_share, ctx_count, [])

    second_means = doubling_sum(second_rows, "tp", tp_count, going_w1 + [grad_w2]) / full_width
    outgoing.append(slots_of(1, second_grad, second_means))
    received = [
        lax.all_to_all(part, "tp", split_axis=0, concat_axis=0, tiled=True) for part in outgoing
    ]
    ln_sum = (first_ln + second_ln)[:, :2]
    small = jnp.concatenate(
        [jnp.sum(out_grad.astype(jnp.float32), axis=0), back_sum, ln_sum.T.reshape(-1)]
    )
    small = doubling_sum(small, "ctx", ctx_count, arrived_w1) * grad_scale
    grad_w1_t = grad_w1_share(member, arrived_w1, jnp.float32, [])
    assert capacity == 1
    vit_grad = None
    for chunk in range(CHUNKS):
        columns = received[chunk].reshape(tp_count * width, part_rows)
        after = [grad_w1_t] if chunk + 1 == CHUNKS else []
        vit_grad = turn_rows(columns, chunk, image_rows, vit_grad, after)

    features_in = out_grad.shape[1]
    hidden_in = pre_act.shape[1]
    bias_down = small[:features_in]
    bias_up = small[features_in : features_in + hidden_in]
    ln_grads = small[features_in + hidden_in :].reshape(2, width)
    return (grad_w2, grad_w1_t.T, bias_up, bias_down, ln_grads, vit_grad)


def solution(mesh):
    return jax.shard_map(
        per_device,
        mesh=mesh,
        in_specs=(
            P("ctx", "tp"),
            P("ctx", "tp"),
            P("ctx", "tp"),
            P("ctx"),
            P(None, "tp"),
            P(None, "tp"),
            P("tp"),
            P("ctx", None),
        ),
        out_specs=(
            P("ctx", "tp"),
            P("ctx", "tp"),
            P("tp"),
            P("tp"),
            P(None, "tp"),
            P(("ctx", "tp"), None),
        ),
        check_vma=False,
    )
```

```python
import functools
import math

import jax
import jax.numpy as jnp
from jax import lax
from jax.experimental import pallas as pl
from jax.experimental.pallas import tpu as pltpu
from jax.sharding import PartitionSpec as P

CHUNKS = 2
VMEM_LIMIT = 48 * 1024 * 1024


def gelu_parts(linear):
    normal_cdf = 0.5 * (1.0 + jax.scipy.special.erf(linear * 2.0 ** (-0.5)))
    density = jnp.exp(-0.5 * linear * linear) * (2.0 * math.pi) ** (-0.5)
    return (linear * normal_cdf, normal_cdf + linear * density)


def slot_numbers(owners, capacity):
    position = jnp.arange(owners.shape[0])
    earlier = (owners[None, :] == owners[:, None]) & (position[None, :] < position[:, None])
    return owners * capacity + jnp.sum(earlier.astype(jnp.int32), axis=1)


def divisor(extent, most, unit):
    return max(d for d in range(unit, most + 1, unit) if extent % d == 0)


def ring_order(count):
    depth = 4 if count % 4 == 0 else count
    width = count // depth
    walk = [(z, 0) for z in range(depth)]
    if width > 1:
        for turn, z in enumerate(reversed(range(depth))):
            ys = list(range(1, width))
            walk += [(z, y) for y in (ys if turn % 2 == 0 else ys[::-1])]
    return [z * width + y for z, y in walk]


def ring_owners(count):
    order = ring_order(count)
    table = []
    for j in range(count):
        at = order.index(j)
        steps = [0]
        for step in range(1, count // 2):
            steps += [-step, step]
        steps += [count // 2]
        table.append([order[(at + s) % count] for s in steps])
    core = (lax.axis_index("ctx") % 2).astype(jnp.int32)
    return jnp.concatenate([jnp.array(table, jnp.int32)[lax.axis_index("tp")], core[None]])


def ring_blocks(block, count):
    order = ring_order(count)
    ahead = [(order[p], order[(p + 1) % count]) for p in range(count)]
    behind = [(order[p], order[(p - 1) % count]) for p in range(count)]
    up, down = block, block
    blocks = [block]
    for _ in range(1, count // 2):
        up = lax.ppermute(up, "tp", ahead)
        down = lax.ppermute(down, "tp", behind)
        blocks += [up, down]
    half = block.shape[0] // 2
    blocks.append(lax.ppermute(up[:half], "tp", ahead))
    blocks.append(lax.ppermute(down[half:], "tp", behind))
    return blocks


def assemble(owners_ref, block_refs, held, sems):
    rows, width = block_refs[0].shape
    half = rows // 2
    last = len(block_refs) - 2
    copies = []
    for k, ref in enumerate(block_refs):
        columns = pl.ds(pl.multiple_of(owners_ref[min(k, last)] * width, width), width)
        if k < last:
            target = held.at[:, columns]
        else:
            target = held.at[pl.ds((k - last) * half, half), columns]
        copies.append(pltpu.make_async_copy(ref, target, sems.at[k]))
    return copies


def spread(ring_ref, held, full_ref, swap_ref, chunk, image_rows, sems):
    rows, part_rows = held.shape[0], image_rows // CHUNKS
    all_rows, member_width = full_ref.shape[0], swap_ref.shape[1]
    other = 1 - ring_ref[ring_ref.shape[0] - 1]
    copies = []
    for i in range(rows // part_rows):
        source = pl.ds(i * part_rows, part_rows)
        place = i * image_rows + chunk * part_rows
        copies.append((held.at[source, :], full_ref.at[pl.ds(place, part_rows), :]))
        for chip in range(swap_ref.shape[0] // all_rows):
            columns = pl.ds(
                pl.multiple_of((2 * chip + other) * member_width, member_width), member_width
            )
            target = swap_ref.at[pl.ds(chip * all_rows + place, part_rows), :]
            copies.append((held.at[source, columns], target))
    return [
        pltpu.make_async_copy(source, target, sems.at[n])
        for n, (source, target) in enumerate(copies)
    ]


def spread_shapes(rows, chunk_rows, full, ctx_count, images):
    shapes = (
        jax.ShapeDtypeStruct((rows, full), jnp.bfloat16),
        jax.ShapeDtypeStruct((rows * (ctx_count // 2), full // ctx_count), jnp.bfloat16),
    )
    scratch = [
        pltpu.VMEM((chunk_rows, full), jnp.bfloat16),
        pltpu.SemaphoreType.DMA((2 * tp_most(),)),
        pltpu.SemaphoreType.DMA((images * (1 + ctx_count // 2),)),
    ]
    return shapes, scratch


def tp_most():
    return lax.axis_size("tp")


def back_kernel(chunk, image_rows, blocks, carried, ring_ref, *refs):
    block_refs, refs = refs[:blocks], refs[blocks:]
    w_ref, slope_ref, *refs = refs
    back_ref, sum_ref, full_ref, swap_ref, held, sems, out_sems = refs[carried:]
    copies = assemble(ring_ref, block_refs, held, sems)
    for copy in copies:
        copy.start()
    for copy in copies:
        copy.wait()
    outs = spread(ring_ref, held, full_ref, swap_ref, chunk, image_rows, out_sems)
    for copy in outs:
        copy.start()
    rows, part_rows = held.shape[0], image_rows // CHUNKS
    tile = divisor(rows, 256, part_rows)
    sums = jnp.zeros(sum_ref.shape, jnp.float32)
    for start in range(0, rows, tile):
        total = jnp.dot(
            held[start : start + tile, :], w_ref[...], preferred_element_type=jnp.float32
        )
        for n in range(tile // part_rows):
            image = start // part_rows + n
            place = image * image_rows + chunk * part_rows
            part = (
                total[n * part_rows : (n + 1) * part_rows]
                * slope_ref[place : place + part_rows, :]
            ).astype(back_ref.dtype)
            back_ref[image * part_rows : (image + 1) * part_rows, :] = part
            sums += jnp.sum(part.astype(jnp.float32), axis=0, keepdims=True)
    sum_ref[...] = sums
    for copy in outs:
        copy.wait()


def back_part(ring, blocks, w_down, slope, chunk, image_rows, ctx_count, so_far):
    rows = blocks[0].shape[0]
    full, width = w_down.shape
    images = slope.shape[0] // image_rows
    shapes, scratch = spread_shapes(slope.shape[0], rows, full, ctx_count, images)
    first = 1 + len(blocks) + 2
    return pl.pallas_call(
        functools.partial(back_kernel, chunk, image_rows, len(blocks), len(so_far)),
        out_shape=(
            jax.ShapeDtypeStruct((rows, width), jnp.bfloat16),
            jax.ShapeDtypeStruct((1, width), jnp.float32),
        )
        + shapes,
        in_specs=[pl.BlockSpec(memory_space=pltpu.SMEM)]
        + [pl.BlockSpec(memory_space=pl.ANY)] * len(blocks)
        + [pl.BlockSpec(memory_space=pltpu.VMEM)] * 2
        + [pl.BlockSpec(memory_space=pltpu.HBM)] * len(so_far),
        out_specs=(pl.BlockSpec(memory_space=pltpu.VMEM),) * 2
        + (pl.BlockSpec(memory_space=pltpu.HBM),) * 2,
        scratch_shapes=scratch,
        input_output_aliases={first + n: 2 + n for n in range(len(so_far))},
        compiler_params=pltpu.CompilerParams(vmem_limit_bytes=VMEM_LIMIT),
        cost_estimate=pl.CostEstimate(
            flops=2 * rows * full * width,
            bytes_accessed=2 * (2 * rows * full + full * width),
            transcendentals=0,
        ),
    )(ring, *blocks, w_down, slope, *so_far)


def norm_kernel(chunk, image_rows, blocks, images, carried, ring_ref, *refs):
    block_refs, refs = refs[:blocks], refs[blocks:]
    w_ref, gain_ref, *refs = refs
    normed_refs, refs = refs[:images], refs[images:]
    grad_ref, sums_ref, ln_ref, full_ref, swap_ref, held, sems, out_sems = refs[carried:]
    step = pl.program_id(0)
    outs = spread(ring_ref, held, full_ref, swap_ref, chunk, image_rows, out_sems)

    @pl.when(step == 0)
    def _():
        copies = assemble(ring_ref, block_refs, held, sems)
        for copy in copies:
            copy.start()
        for copy in copies:
            copy.wait()
        for copy in outs:
            copy.start()
        sums_ref[...] = jnp.zeros_like(sums_ref)

    grad = lax.dot_general(
        w_ref[...], held[...], (((1,), (1,)), ((), ())), preferred_element_type=jnp.float32
    )
    grad_ref[...] = grad
    features = jnp.concatenate([ref[...] for ref in normed_refs], axis=1).astype(jnp.float32)
    gained = gain_ref[...] * grad
    sums_ref[0:1, :] += jnp.sum(gained, axis=0, keepdims=True)
    sums_ref[1:2, :] += jnp.sum(gained * features, axis=0, keepdims=True)
    gains = jnp.sum(grad * features, axis=1, keepdims=True)
    biases = jnp.sum(grad, axis=1, keepdims=True)
    lane = lax.broadcasted_iota(jnp.int32, ln_ref.shape, 1)
    ln_ref[...] = jnp.where(lane == 0, gains, biases)

    @pl.when(step == pl.num_programs(0) - 1)
    def _():
        for copy in outs:
            copy.wait()


def norm_part(ring, blocks, w_up_t, gain, normed_t, chunk, image_rows, ctx_count, so_far, after):
    rows = blocks[0].shape[0]
    width, full = w_up_t.shape
    part_rows = image_rows // CHUNKS
    images = rows // part_rows
    tile = divisor(width, 400, 16)
    shapes, scratch = spread_shapes(normed_t.shape[1], rows, full, ctx_count, images)
    first = 1 + len(blocks) + 2 + images
    return pl.pallas_call(
        functools.partial(
            norm_kernel, chunk, image_rows, len(blocks), images, len(so_far) + len(after)
        ),
        grid=(width // tile,),
        out_shape=(
            jax.ShapeDtypeStruct((width, rows), jnp.float32),
            jax.ShapeDtypeStruct((2, rows), jnp.float32),
            jax.ShapeDtypeStruct((width, 128), jnp.float32),
        )
        + shapes,
        in_specs=[pl.BlockSpec(memory_space=pltpu.SMEM)]
        + [pl.BlockSpec(memory_space=pl.ANY)] * len(blocks)
        + [
            pl.BlockSpec((tile, full), lambda t: (t, 0)),
            pl.BlockSpec((tile, 1), lambda t: (t, 0)),
        ]
        + [
            pl.BlockSpec((tile, part_rows), lambda t, i=i: (t, i * CHUNKS + chunk))
            for i in range(images)
        ]
        + [pl.BlockSpec(memory_space=pltpu.HBM)] * (len(so_far) + len(after)),
        out_specs=(
            pl.BlockSpec((tile, rows), lambda t: (t, 0)),
            pl.BlockSpec((2, rows), lambda t: (0, 0)),
            pl.BlockSpec((tile, 128), lambda t: (t, 0)),
        )
        + (pl.BlockSpec(memory_space=pltpu.HBM),) * 2,
        scratch_shapes=scratch,
        input_output_aliases={first + n: 3 + n for n in range(len(so_far))},
        compiler_params=pltpu.CompilerParams(vmem_limit_bytes=VMEM_LIMIT),
        cost_estimate=pl.CostEstimate(
            flops=2 * rows * full * width,
            bytes_accessed=2 * (full * width + 2 * rows * full) + 6 * rows * width,
            transcendentals=0,
        ),
    )(ring, *blocks, w_up_t, gain, *[normed_t] * images, *so_far, *after)


def pair_kernel(
    contract, scale, ranges, member_ref, a_ref, a_other_ref, b_ref, b_other_ref, *refs
):
    arrived, out_ref = refs[: len(ranges)], refs[-1]
    dims = (contract, ((), ()))
    total = lax.dot_general(a_ref[...], b_ref[...], dims, preferred_element_type=jnp.float32)
    total += lax.dot_general(
        a_other_ref[...], b_other_ref[...], dims, preferred_element_type=jnp.float32
    )
    total *= scale
    step = pl.program_id(0)
    for (first, last), ref in zip(ranges, arrived):
        part = ref[...].astype(jnp.float32)
        total += jnp.where((step >= first) & (step < last), part, 0.0)
    out_ref[...] = total.astype(out_ref.dtype)


def pair_product(
    operands, specs, contract, shape, tile, depth, member, scale, arrived, dtype, after
):
    row_spec = lambda first, last: pl.BlockSpec(
        (tile, shape[1]), lambda t, m: (jnp.clip(t - first, 0, last - first - 1), 0)
    )
    steps = shape[0] // tile
    return pl.pallas_call(
        functools.partial(pair_kernel, contract, scale, [span for span, _ in arrived]),
        grid_spec=pltpu.PrefetchScalarGridSpec(
            num_scalar_prefetch=1,
            grid=(steps,),
            in_specs=specs
            + [row_spec(*span) for span, _ in arrived]
            + [pl.BlockSpec(memory_space=pltpu.HBM)] * len(after),
            out_specs=row_spec(0, steps),
        ),
        out_shape=jax.ShapeDtypeStruct(shape, dtype),
        compiler_params=pltpu.CompilerParams(vmem_limit_bytes=VMEM_LIMIT),
        cost_estimate=pl.CostEstimate(
            flops=4 * shape[0] * shape[1] * depth,
            bytes_accessed=4 * depth * (shape[0] + shape[1]) + 4 * shape[0] * shape[1],
            transcendentals=0,
        ),
    )(
        member.reshape(1).astype(jnp.int32),
        *operands,
        *[part for _, part in arrived],
        *after,
    )


def chip_products(product, spans, ctx_count, after):
    index = lax.axis_index("ctx")
    going, arrived = [], []
    for span in spans:
        for shift in range(1, ctx_count // 2):
            member = (index + 2 * shift) % ctx_count
            going.append(product(member, span, [], jnp.bfloat16, after))
            route = [(c, (c + 2 * shift) % ctx_count) for c in range(ctx_count)]
            arrived.append((span, lax.ppermute(going[-1], "ctx", route)))
    return going, arrived


def tie_kernel(*refs):
    del refs


def tie(values, others):
    return pl.pallas_call(
        tie_kernel,
        in_specs=[pl.BlockSpec(memory_space=pl.ANY)] * (len(values) + len(others)),
        out_specs=[pl.BlockSpec(memory_space=pl.ANY)] * len(values),
        out_shape=[jax.ShapeDtypeStruct(value.shape, value.dtype) for value in values],
        input_output_aliases={n: n for n in range(len(values))},
        compiler_params=pltpu.CompilerParams(vmem_limit_bytes=VMEM_LIMIT),
    )(*values, *others)


def visual_kernel(
    source_ref, present_ref, grad_ref, normed_ref, gain_ref, means_ref, inverse_ref, *refs
):
    out_ref = refs[-1]
    slot = pl.program_id(0)

    @pl.when(present_ref[slot] == 0)
    def _():
        out_ref[...] = jnp.zeros_like(out_ref)

    @pl.when(present_ref[slot] != 0)
    def _():
        gained = gain_ref[...] * grad_ref[...]
        features = normed_ref[...].astype(jnp.float32)
        first, second = means_ref[0:1, :], means_ref[1:2, :]
        out_ref[0] = (inverse_ref[...] * (gained - first - features * second)).astype(
            out_ref.dtype
        )


def visual_slots(source, present, grad_t, normed_t, gain, means, inverse, chunk, part_rows, after):
    width = grad_t.shape[0]
    slots = source.shape[0]
    picked = lambda s, source, present: (0, source[s])
    natural = lambda s, source, present: (0, source[s] * CHUNKS + chunk)
    return pl.pallas_call(
        visual_kernel,
        grid_spec=pltpu.PrefetchScalarGridSpec(
            num_scalar_prefetch=2,
            grid=(slots,),
            in_specs=[
                pl.BlockSpec((width, part_rows), picked),
                pl.BlockSpec((width, part_rows), natural),
                pl.BlockSpec((width, 1), lambda s, source, present: (0, 0)),
                pl.BlockSpec((2, part_rows), picked),
                pl.BlockSpec((1, part_rows), natural),
            ]
            + [pl.BlockSpec(memory_space=pltpu.HBM)] * len(after),
            out_specs=pl.BlockSpec((1, width, part_rows), lambda s, source, present: (s, 0, 0)),
        ),
        out_shape=jax.ShapeDtypeStruct((slots, width, part_rows), jnp.bfloat16),
        compiler_params=pltpu.CompilerParams(vmem_limit_bytes=VMEM_LIMIT),
        cost_estimate=pl.CostEstimate(
            flops=6 * slots * width * part_rows,
            bytes_accessed=8 * slots * width * part_rows,
            transcendentals=0,
        ),
    )(source, present, grad_t, normed_t, gain, means, inverse, *after)


def turn_kernel(in_ref, *refs):
    refs[-1][...] = in_ref[...].T


def turn_rows(received, chunk, rows, so_far, after):
    full, part_rows = received.shape
    tile = divisor(full, 2560, 128)
    operands, aliases = [received], {}
    if so_far is not None:
        operands.append(so_far)
        aliases = {1: 0}
    operands += after
    specs = [pl.BlockSpec((tile, part_rows), lambda t: (t, 0))]
    specs += [pl.BlockSpec(memory_space=pltpu.HBM)] * (len(operands) - 1)
    return pl.pallas_call(
        turn_kernel,
        grid=(full // tile,),
        in_specs=specs,
        out_specs=pl.BlockSpec((part_rows, tile), lambda t: (chunk, t)),
        out_shape=jax.ShapeDtypeStruct((rows, full), received.dtype),
        input_output_aliases=aliases,
        compiler_params=pltpu.CompilerParams(vmem_limit_bytes=VMEM_LIMIT),
        cost_estimate=pl.CostEstimate(
            flops=0, bytes_accessed=4 * part_rows * full, transcendentals=0
        ),
    )(*operands)


def core_swap(value, ctx_count):
    return lax.ppermute(value, "ctx", [(c, c ^ 1) for c in range(ctx_count)])


def doubling_sum(value, axis, count, after=()):
    bit = 1
    while bit < count:
        if after and 2 * bit >= count:
            (value,) = tie([value], after)
        value = value + lax.ppermute(value, axis, [(t, t ^ bit) for t in range(count)])
        bit *= 2
    return value


def per_device(out_grad, pre_act, normed, inverse_std, w_up, w_down, ln_gain, owner_map):
    ctx_count = lax.axis_size("ctx")
    tp_count = lax.axis_size("tp")
    row_count = out_grad.shape[0]
    width = normed.shape[1]
    grad_scale = float(row_count * ctx_count) ** (-0.5)
    full_width = float(width * tp_count)

    owners = owner_map[0]
    image_count = owners.shape[0]
    image_rows = row_count // image_count
    part_rows = image_rows // CHUNKS
    chunk_rows = row_count // CHUNKS
    capacity = max(1, 2 * image_count // tp_count)
    slot_of = slot_numbers(owners, capacity)
    slot_ids = jnp.arange(tp_count * capacity)
    matches = slot_of[None, :] == slot_ids[:, None]
    present = jnp.any(matches, axis=1).astype(jnp.int32)
    source = jnp.sum(jnp.where(matches, jnp.arange(image_count)[None, :], 0), axis=1).astype(
        jnp.int32
    )

    def chunk_of(array, chunk):
        images = array.reshape((image_count, image_rows) + array.shape[1:])
        piece = images[:, chunk * part_rows : (chunk + 1) * part_rows]
        return piece.reshape((chunk_rows,) + array.shape[1:])

    ring = ring_owners(tp_count)
    gelu_value, slope = gelu_parts(pre_act.astype(jnp.float32))
    hidden = gelu_value.astype(jnp.bfloat16)
    hidden_other = core_swap(hidden, ctx_count)
    normed_t = normed.T
    normed_other = core_swap(normed_t, ctx_count)
    gain = ln_gain[:, None]
    w_up_t = w_up.T

    def back_of(chunk, blocks, so_far):
        return back_part(ring, blocks, w_down, slope, chunk, image_rows, ctx_count, so_far)

    first_grads, second_grads = [
        ring_blocks(chunk_of(out_grad, chunk), tp_count) for chunk in range(CHUNKS)
    ]
    first_back, first_sum, *so_far = back_of(0, first_grads, ())
    first_backs = ring_blocks(first_back, tp_count)
    second_back, second_sum, grads, grads_swap = back_of(1, second_grads, so_far)
    second_backs = ring_blocks(second_back, tp_count)
    grads_other = core_swap(grads_swap, ctx_count)
    back_sum = first_sum[0] + second_sum[0]

    def grad_w2_share(member, span, arrived, dtype, after):
        share, local = grads.shape[1] // ctx_count, hidden.shape[1]
        tile = divisor(share, 256, 128)
        steps = share // tile
        return pair_product(
            (grads, grads_other, hidden, hidden_other),
            [
                pl.BlockSpec((row_count, tile), lambda t, m: (0, m[0] * steps + t)),
                pl.BlockSpec((row_count, tile), lambda t, m: (m[0] // 2, t)),
                pl.BlockSpec((row_count, local), lambda t, m: (0, 0)),
                pl.BlockSpec((row_count, local), lambda t, m: (0, 0)),
            ],
            ((0,), (0,)), (share, local), tile, row_count, member, grad_scale, arrived, dtype,
            after,
        )

    w2_span = (0, grads.shape[1] // ctx_count // divisor(grads.shape[1] // ctx_count, 256, 128))
    going_w2, arrived_w2 = chip_products(grad_w2_share, [w2_span], ctx_count, [])
    member = lax.axis_index("ctx")

    def norm_of(chunk, blocks, so_far, after):
        return norm_part(
            ring, blocks, w_up_t, gain, normed_t, chunk, image_rows, ctx_count, so_far, after
        )

    def slots_of(chunk, grad_t, means):
        return visual_slots(
            source, present, grad_t, normed_t, gain, means, inverse_std[None, :], chunk, part_rows, []
        )

    first_grad, first_rows, first_ln, *so_far = norm_of(0, first_backs, (), [])
    first_means = doubling_sum(first_rows, "tp", tp_count) / full_width
    first_slots, first_means = tie(
        [slots_of(0, first_grad, first_means), first_means], second_backs[-2:]
    )
    outgoing = [first_slots]
    second_grad, second_rows, second_ln, backs, backs_swap = norm_of(
        1, second_backs, so_far, [first_means]
    )
    backs_other = core_swap(backs_swap, ctx_count)

    w1_tile = divisor(width, 400, 16)
    w1_tiles = width // w1_tile

    def grad_w1_share(member, span, arrived, dtype, after):
        share = backs.shape[1] // ctx_count
        first, last = span
        return pair_product(
            (normed_t, normed_other, backs, backs_other),
            [
                pl.BlockSpec((w1_tile, row_count), lambda t, m: (first + t, 0)),
                pl.BlockSpec((w1_tile, row_count), lambda t, m: (first + t, 0)),
                pl.BlockSpec((row_count, share), lambda t, m: (0, m[0])),
                pl.BlockSpec((row_count, share), lambda t, m: (m[0] // 2, 0)),
            ],
            ((1,), (0,)), ((last - first) * w1_tile, share), w1_tile, row_count, member,
            grad_scale, arrived, dtype, after,
        )

    spans = [(0, 1), (1, w1_tiles)] if w1_tiles > 1 else [(0, 1)]
    going_w1, arrived_w1 = chip_products(grad_w1_share, spans, ctx_count, going_w2)

    second_means = doubling_sum(second_rows, "tp", tp_count, going_w1) / full_width
    early = [part for span, part in arrived_w1 if span == spans[0]]
    outgoing += tie([slots_of(1, second_grad, second_means)], early)
    received = [
        lax.all_to_all(part, "tp", split_axis=0, concat_axis=0, tiled=True) for part in outgoing
    ]
    ln_sum = (first_ln + second_ln)[:, :2]
    small = jnp.concatenate(
        [jnp.sum(out_grad.astype(jnp.float32), axis=0), back_sum, ln_sum.T.reshape(-1)]
    )
    (small,) = tie([small], [part for _, part in arrived_w1])
    grad_w2 = grad_w2_share(member, w2_span, arrived_w2, jnp.float32, [small])
    small = doubling_sum(small, "ctx", ctx_count) * grad_scale
    grad_w1_t = grad_w1_share(member, (0, w1_tiles), arrived_w1, jnp.float32, [])
    assert capacity == 1
    vit_grad = None
    for chunk in range(CHUNKS):
        columns = received[chunk].reshape(tp_count * width, part_rows)
        after = [grad_w1_t, grad_w2] if chunk + 1 == CHUNKS else []
        vit_grad = turn_rows(columns, chunk, image_rows, vit_grad, after)

    features_in = out_grad.shape[1]
    hidden_in = pre_act.shape[1]
    bias_down = small[:features_in]
    bias_up = small[features_in : features_in + hidden_in]
    ln_grads = small[features_in + hidden_in :].reshape(2, width)
    return (grad_w2, grad_w1_t.T, bias_up, bias_down, ln_grads, vit_grad)


def solution(mesh):
    return jax.shard_map(
        per_device,
        mesh=mesh,
        in_specs=(
            P("ctx", "tp"),
            P("ctx", "tp"),
            P("ctx", "tp"),
            P("ctx"),
            P(None, "tp"),
            P(None, "tp"),
            P("tp"),
            P("ctx", None),
        ),
        out_specs=(
            P("ctx", "tp"),
            P("ctx", "tp"),
            P("tp"),
            P("tp"),
            P(None, "tp"),
            P(("ctx", "tp"), None),
        ),
        check_vma=False,
    )
```

```python
import functools
import math

import jax
import jax.numpy as jnp
from jax import lax
from jax.experimental import pallas as pl
from jax.experimental.pallas import tpu as pltpu
from jax.sharding import PartitionSpec as P

CHUNKS = 2
VMEM_LIMIT = 48 * 1024 * 1024


def gelu_parts(linear):
    normal_cdf = 0.5 * (1.0 + jax.scipy.special.erf(linear * 2.0 ** (-0.5)))
    density = jnp.exp(-0.5 * linear * linear) * (2.0 * math.pi) ** (-0.5)
    return (linear * normal_cdf, normal_cdf + linear * density)


def slot_numbers(owners, capacity):
    position = jnp.arange(owners.shape[0])
    earlier = (owners[None, :] == owners[:, None]) & (position[None, :] < position[:, None])
    return owners * capacity + jnp.sum(earlier.astype(jnp.int32), axis=1)


def divisor(extent, most, unit):
    return max(d for d in range(unit, most + 1, unit) if extent % d == 0)


def ring_order(count):
    depth = 4 if count % 4 == 0 else count
    width = count // depth
    walk = [(z, 0) for z in range(depth)]
    if width > 1:
        for turn, z in enumerate(reversed(range(depth))):
            ys = list(range(1, width))
            walk += [(z, y) for y in (ys if turn % 2 == 0 else ys[::-1])]
    return [z * width + y for z, y in walk]


def ring_owners(count):
    order = ring_order(count)
    table = []
    for j in range(count):
        at = order.index(j)
        steps = [0]
        for step in range(1, count // 2):
            steps += [-step, step]
        steps += [count // 2]
        table.append([order[(at + s) % count] for s in steps])
    core = (lax.axis_index("ctx") % 2).astype(jnp.int32)
    return jnp.concatenate([jnp.array(table, jnp.int32)[lax.axis_index("tp")], core[None]])


def ring_blocks(block, count):
    order = ring_order(count)
    ahead = [(order[p], order[(p + 1) % count]) for p in range(count)]
    behind = [(order[p], order[(p - 1) % count]) for p in range(count)]
    up, down = block, block
    blocks = [block]
    for _ in range(1, count // 2):
        up = lax.ppermute(up, "tp", ahead)
        down = lax.ppermute(down, "tp", behind)
        blocks += [up, down]
    half = block.shape[0] // 2
    blocks.append(lax.ppermute(up[:half], "tp", ahead))
    blocks.append(lax.ppermute(down[half:], "tp", behind))
    return blocks


def assemble(owners_ref, block_refs, held, sems):
    rows, width = block_refs[0].shape
    half = rows // 2
    last = len(block_refs) - 2
    copies = []
    for k, ref in enumerate(block_refs):
        columns = pl.ds(pl.multiple_of(owners_ref[min(k, last)] * width, width), width)
        if k < last:
            target = held.at[:, columns]
        else:
            target = held.at[pl.ds((k - last) * half, half), columns]
        copies.append(pltpu.make_async_copy(ref, target, sems.at[k]))
    return copies


def spread(ring_ref, held, full_ref, swap_ref, chunk, image_rows, sems):
    rows, part_rows = held.shape[0], image_rows // CHUNKS
    all_rows, member_width = full_ref.shape[0], swap_ref.shape[1]
    other = 1 - ring_ref[ring_ref.shape[0] - 1]
    copies = []
    for i in range(rows // part_rows):
        source = pl.ds(i * part_rows, part_rows)
        place = i * image_rows + chunk * part_rows
        copies.append((held.at[source, :], full_ref.at[pl.ds(place, part_rows), :]))
        for chip in range(swap_ref.shape[0] // all_rows):
            columns = pl.ds(
                pl.multiple_of((2 * chip + other) * member_width, member_width), member_width
            )
            target = swap_ref.at[pl.ds(chip * all_rows + place, part_rows), :]
            copies.append((held.at[source, columns], target))
    return [
        pltpu.make_async_copy(source, target, sems.at[n])
        for n, (source, target) in enumerate(copies)
    ]


def spread_shapes(rows, chunk_rows, full, ctx_count, images):
    shapes = (
        jax.ShapeDtypeStruct((rows, full), jnp.bfloat16),
        jax.ShapeDtypeStruct((rows * (ctx_count // 2), full // ctx_count), jnp.bfloat16),
    )
    scratch = [
        pltpu.VMEM((chunk_rows, full), jnp.bfloat16),
        pltpu.SemaphoreType.DMA((2 * tp_most(),)),
        pltpu.SemaphoreType.DMA((images * (1 + ctx_count // 2),)),
    ]
    return shapes, scratch


def tp_most():
    return lax.axis_size("tp")


def back_kernel(chunk, image_rows, blocks, carried, ring_ref, *refs):
    block_refs, refs = refs[:blocks], refs[blocks:]
    w_ref, slope_ref, *refs = refs
    back_ref, sum_ref, full_ref, swap_ref, held, sems, out_sems = refs[carried:]
    copies = assemble(ring_ref, block_refs, held, sems)
    for copy in copies:
        copy.start()
    for copy in copies:
        copy.wait()
    outs = spread(ring_ref, held, full_ref, swap_ref, chunk, image_rows, out_sems)
    for copy in outs:
        copy.start()
    rows, part_rows = held.shape[0], image_rows // CHUNKS
    tile = divisor(rows, 256, part_rows)
    sums = jnp.zeros(sum_ref.shape, jnp.float32)
    for start in range(0, rows, tile):
        total = jnp.dot(
            held[start : start + tile, :], w_ref[...], preferred_element_type=jnp.float32
        )
        for n in range(tile // part_rows):
            image = start // part_rows + n
            place = image * image_rows + chunk * part_rows
            part = (
                total[n * part_rows : (n + 1) * part_rows]
                * slope_ref[place : place + part_rows, :]
            ).astype(back_ref.dtype)
            back_ref[image * part_rows : (image + 1) * part_rows, :] = part
            sums += jnp.sum(part.astype(jnp.float32), axis=0, keepdims=True)
    sum_ref[...] = sums
    for copy in outs:
        copy.wait()


def back_part(ring, blocks, w_down, slope, chunk, image_rows, ctx_count, so_far, after):
    rows = blocks[0].shape[0]
    full, width = w_down.shape
    images = slope.shape[0] // image_rows
    shapes, scratch = spread_shapes(slope.shape[0], rows, full, ctx_count, images)
    first = 1 + len(blocks) + 2
    return pl.pallas_call(
        functools.partial(
            back_kernel, chunk, image_rows, len(blocks), len(so_far) + len(after)
        ),
        out_shape=(
            jax.ShapeDtypeStruct((rows, width), jnp.bfloat16),
            jax.ShapeDtypeStruct((1, width), jnp.float32),
        )
        + shapes,
        in_specs=[pl.BlockSpec(memory_space=pltpu.SMEM)]
        + [pl.BlockSpec(memory_space=pl.ANY)] * len(blocks)
        + [pl.BlockSpec(memory_space=pltpu.VMEM)] * 2
        + [pl.BlockSpec(memory_space=pltpu.HBM)] * (len(so_far) + len(after)),
        out_specs=(pl.BlockSpec(memory_space=pltpu.VMEM),) * 2
        + (pl.BlockSpec(memory_space=pltpu.HBM),) * 2,
        scratch_shapes=scratch,
        input_output_aliases={first + n: 2 + n for n in range(len(so_far))},
        compiler_params=pltpu.CompilerParams(vmem_limit_bytes=VMEM_LIMIT),
        cost_estimate=pl.CostEstimate(
            flops=2 * rows * full * width,
            bytes_accessed=2 * (2 * rows * full + full * width),
            transcendentals=0,
        ),
    )(ring, *blocks, w_down, slope, *so_far, *after)


def norm_kernel(chunk, image_rows, blocks, images, carried, ring_ref, *refs):
    block_refs, refs = refs[:blocks], refs[blocks:]
    w_ref, gain_ref, *refs = refs
    normed_refs, refs = refs[:images], refs[images:]
    gained_ref, sums_ref, ln_ref, full_ref, swap_ref, held, sems, out_sems = refs[carried:]
    step = pl.program_id(0)
    outs = spread(ring_ref, held, full_ref, swap_ref, chunk, image_rows, out_sems)

    @pl.when(step == 0)
    def _():
        copies = assemble(ring_ref, block_refs, held, sems)
        for copy in copies:
            copy.start()
        for copy in copies:
            copy.wait()
        for copy in outs:
            copy.start()
        sums_ref[...] = jnp.zeros_like(sums_ref)

    grad = lax.dot_general(
        w_ref[...], held[...], (((1,), (1,)), ((), ())), preferred_element_type=jnp.float32
    )
    features = jnp.concatenate([ref[...] for ref in normed_refs], axis=1).astype(jnp.float32)
    gained = gain_ref[...] * grad
    gained_ref[...] = gained
    sums_ref[0:1, :] += jnp.sum(gained, axis=0, keepdims=True)
    sums_ref[1:2, :] += jnp.sum(gained * features, axis=0, keepdims=True)
    gains = jnp.sum(grad * features, axis=1, keepdims=True)
    biases = jnp.sum(grad, axis=1, keepdims=True)
    lane = lax.broadcasted_iota(jnp.int32, ln_ref.shape, 1)
    ln_ref[...] = jnp.where(lane == 0, gains, biases)

    @pl.when(step == pl.num_programs(0) - 1)
    def _():
        for copy in outs:
            copy.wait()


def norm_part(ring, blocks, w_up_t, gain, normed_t, chunk, image_rows, ctx_count, so_far, after):
    rows = blocks[0].shape[0]
    width, full = w_up_t.shape
    part_rows = image_rows // CHUNKS
    images = rows // part_rows
    tile = divisor(width, 400, 16)
    shapes, scratch = spread_shapes(normed_t.shape[1], rows, full, ctx_count, images)
    first = 1 + len(blocks) + 2 + images
    return pl.pallas_call(
        functools.partial(
            norm_kernel, chunk, image_rows, len(blocks), images, len(so_far) + len(after)
        ),
        grid=(width // tile,),
        out_shape=(
            jax.ShapeDtypeStruct((width, rows), jnp.float32),
            jax.ShapeDtypeStruct((2, rows), jnp.float32),
            jax.ShapeDtypeStruct((width, 128), jnp.float32),
        )
        + shapes,
        in_specs=[pl.BlockSpec(memory_space=pltpu.SMEM)]
        + [pl.BlockSpec(memory_space=pltpu.HBM if chunk > 0 else pl.ANY)] * len(blocks)
        + [
            pl.BlockSpec((tile, full), lambda t: (t, 0)),
            pl.BlockSpec((tile, 1), lambda t: (t, 0)),
        ]
        + [
            pl.BlockSpec((tile, part_rows), lambda t, i=i: (t, i * CHUNKS + chunk))
            for i in range(images)
        ]
        + [pl.BlockSpec(memory_space=pltpu.HBM)] * (len(so_far) + len(after)),
        out_specs=(
            pl.BlockSpec((tile, rows), lambda t: (t, 0)),
            pl.BlockSpec((2, rows), lambda t: (0, 0)),
            pl.BlockSpec((tile, 128), lambda t: (t, 0)),
        )
        + (pl.BlockSpec(memory_space=pltpu.HBM),) * 2,
        scratch_shapes=scratch,
        input_output_aliases={first + n: 3 + n for n in range(len(so_far))},
        compiler_params=pltpu.CompilerParams(vmem_limit_bytes=VMEM_LIMIT),
        cost_estimate=pl.CostEstimate(
            flops=2 * rows * full * width,
            bytes_accessed=2 * (full * width + 2 * rows * full) + 6 * rows * width,
            transcendentals=0,
        ),
    )(ring, *blocks, w_up_t, gain, *[normed_t] * images, *so_far, *after)


def pair_kernel(contract, scale, member_ref, a_ref, a_other_ref, b_ref, b_other_ref, *refs):
    dims = (contract, ((), ()))
    total = lax.dot_general(a_ref[...], b_ref[...], dims, preferred_element_type=jnp.float32)
    total += lax.dot_general(
        a_other_ref[...], b_other_ref[...], dims, preferred_element_type=jnp.float32
    )
    refs[-1][...] = (total * scale).astype(refs[-1].dtype)


def pair_product(operands, specs, contract, shape, tile, depth, member, scale, dtype, after):
    return pl.pallas_call(
        functools.partial(pair_kernel, contract, scale),
        grid_spec=pltpu.PrefetchScalarGridSpec(
            num_scalar_prefetch=1,
            grid=(shape[0] // tile,),
            in_specs=specs + [pl.BlockSpec(memory_space=pltpu.HBM)] * len(after),
            out_specs=pl.BlockSpec((tile, shape[1]), lambda t, m: (t, 0)),
        ),
        out_shape=jax.ShapeDtypeStruct(shape, dtype),
        compiler_params=pltpu.CompilerParams(vmem_limit_bytes=VMEM_LIMIT),
        cost_estimate=pl.CostEstimate(
            flops=4 * shape[0] * shape[1] * depth,
            bytes_accessed=4 * depth * (shape[0] + shape[1]) + 4 * shape[0] * shape[1],
            transcendentals=0,
        ),
    )(member.reshape(1).astype(jnp.int32), *operands, *after)


def add_kernel(own_ref, *refs):
    total = own_ref[...]
    for ref in refs[:-1]:
        total += ref[...].astype(jnp.float32)
    refs[-1][...] = total


def add_arrived(own, first_row, arrived):
    rows, width = arrived[0].shape
    tile = divisor(math.gcd(rows, first_row), 512, 16)
    place = lambda t: (first_row // tile + t, 0)
    return pl.pallas_call(
        add_kernel,
        grid=(rows // tile,),
        in_specs=[pl.BlockSpec((tile, width), place)]
        + [pl.BlockSpec((tile, width), lambda t: (t, 0))] * len(arrived),
        out_specs=pl.BlockSpec((tile, width), place),
        out_shape=jax.ShapeDtypeStruct(own.shape, own.dtype),
        input_output_aliases={0: 0},
        compiler_params=pltpu.CompilerParams(vmem_limit_bytes=VMEM_LIMIT),
        cost_estimate=pl.CostEstimate(
            flops=rows * width * len(arrived),
            bytes_accessed=rows * width * (8 + 2 * len(arrived)),
            transcendentals=0,
        ),
    )(own, *arrived)


def chip_products(product, spans, ctx_count, after):
    index = lax.axis_index("ctx")
    going, arrived = [], []
    for span in spans:
        arrived.append([])
        for shift in range(1, ctx_count // 2):
            member = (index + 2 * shift) % ctx_count
            going.append(product(member, span, jnp.bfloat16, after))
            route = [(c, (c + 2 * shift) % ctx_count) for c in range(ctx_count)]
            arrived[-1].append(lax.ppermute(going[-1], "ctx", route))
    return going, arrived


def tie_kernel(*refs):
    del refs


def tie(values, others):
    return pl.pallas_call(
        tie_kernel,
        in_specs=[pl.BlockSpec(memory_space=pl.ANY)] * (len(values) + len(others)),
        out_specs=[pl.BlockSpec(memory_space=pl.ANY)] * len(values),
        out_shape=[jax.ShapeDtypeStruct(value.shape, value.dtype) for value in values],
        input_output_aliases={n: n for n in range(len(values))},
        compiler_params=pltpu.CompilerParams(vmem_limit_bytes=VMEM_LIMIT),
    )(*values, *others)


def visual_kernel(
    source_ref, present_ref, gained_ref, normed_ref, means_ref, inverse_ref, out_ref
):
    slot = pl.program_id(0)

    @pl.when(present_ref[slot] == 0)
    def _():
        out_ref[...] = jnp.zeros_like(out_ref)

    @pl.when(present_ref[slot] != 0)
    def _():
        gained = gained_ref[...]
        features = normed_ref[...].astype(jnp.float32)
        first, second = means_ref[0:1, :], means_ref[1:2, :]
        out_ref[0] = (inverse_ref[...] * (gained - first - features * second)).astype(
            out_ref.dtype
        )


def visual_slots(source, present, gained_t, normed_t, means, inverse, chunk, part_rows):
    width = gained_t.shape[0]
    slots = source.shape[0]
    picked = lambda s, source, present: (0, source[s])
    natural = lambda s, source, present: (0, source[s] * CHUNKS + chunk)
    return pl.pallas_call(
        visual_kernel,
        grid_spec=pltpu.PrefetchScalarGridSpec(
            num_scalar_prefetch=2,
            grid=(slots,),
            in_specs=[
                pl.BlockSpec((width, part_rows), picked),
                pl.BlockSpec((width, part_rows), natural),
                pl.BlockSpec((2, part_rows), picked),
                pl.BlockSpec((1, part_rows), natural),
            ],
            out_specs=pl.BlockSpec((1, width, part_rows), lambda s, source, present: (s, 0, 0)),
        ),
        out_shape=jax.ShapeDtypeStruct((slots, width, part_rows), jnp.bfloat16),
        compiler_params=pltpu.CompilerParams(vmem_limit_bytes=VMEM_LIMIT),
        cost_estimate=pl.CostEstimate(
            flops=6 * slots * width * part_rows,
            bytes_accessed=8 * slots * width * part_rows,
            transcendentals=0,
        ),
    )(source, present, gained_t, normed_t, means, inverse)


def turn_kernel(in_ref, *refs):
    refs[-1][...] = in_ref[...].T


def turn_rows(received, chunk, rows, so_far, after):
    full, part_rows = received.shape
    tile = divisor(full, 2560, 128)
    operands, aliases = [received], {}
    if so_far is not None:
        operands.append(so_far)
        aliases = {1: 0}
    operands += after
    specs = [pl.BlockSpec((tile, part_rows), lambda t: (t, 0))]
    specs += [pl.BlockSpec(memory_space=pltpu.HBM)] * (len(operands) - 1)
    return pl.pallas_call(
        turn_kernel,
        grid=(full // tile,),
        in_specs=specs,
        out_specs=pl.BlockSpec((part_rows, tile), lambda t: (chunk, t)),
        out_shape=jax.ShapeDtypeStruct((rows, full), received.dtype),
        input_output_aliases=aliases,
        compiler_params=pltpu.CompilerParams(vmem_limit_bytes=VMEM_LIMIT),
        cost_estimate=pl.CostEstimate(
            flops=0, bytes_accessed=4 * part_rows * full, transcendentals=0
        ),
    )(*operands)


def core_swap(value, ctx_count):
    return lax.ppermute(value, "ctx", [(c, c ^ 1) for c in range(ctx_count)])


def doubling_sum(value, axis, count, after=()):
    bit = 1
    while bit < count:
        if after and 2 * bit >= count:
            (value,) = tie([value], after)
        value = value + lax.ppermute(value, axis, [(t, t ^ bit) for t in range(count)])
        bit *= 2
    return value


def per_device(out_grad, pre_act, normed, inverse_std, w_up, w_down, ln_gain, owner_map):
    ctx_count = lax.axis_size("ctx")
    tp_count = lax.axis_size("tp")
    row_count = out_grad.shape[0]
    width = normed.shape[1]
    grad_scale = float(row_count * ctx_count) ** (-0.5)
    full_width = float(width * tp_count)

    owners = owner_map[0]
    image_count = owners.shape[0]
    image_rows = row_count // image_count
    part_rows = image_rows // CHUNKS
    chunk_rows = row_count // CHUNKS
    capacity = max(1, 2 * image_count // tp_count)
    slot_of = slot_numbers(owners, capacity)
    slot_ids = jnp.arange(tp_count * capacity)
    matches = slot_of[None, :] == slot_ids[:, None]
    present = jnp.any(matches, axis=1).astype(jnp.int32)
    source = jnp.sum(jnp.where(matches, jnp.arange(image_count)[None, :], 0), axis=1).astype(
        jnp.int32
    )

    def chunk_of(array, chunk):
        images = array.reshape((image_count, image_rows) + array.shape[1:])
        piece = images[:, chunk * part_rows : (chunk + 1) * part_rows]
        return piece.reshape((chunk_rows,) + array.shape[1:])

    ring = ring_owners(tp_count)
    gelu_value, slope = gelu_parts(pre_act.astype(jnp.float32))
    hidden = gelu_value.astype(jnp.bfloat16)
    hidden_other = core_swap(hidden, ctx_count)
    normed_t = normed.T
    normed_other = core_swap(normed_t, ctx_count)
    gain = ln_gain[:, None]
    w_up_t = w_up.T

    def back_of(chunk, blocks, so_far, after):
        return back_part(
            ring, blocks, w_down, slope, chunk, image_rows, ctx_count, so_far, after
        )

    first_grads, second_grads = [
        ring_blocks(chunk_of(out_grad, chunk), tp_count) for chunk in range(CHUNKS)
    ]
    first_back, first_sum, *so_far = back_of(0, first_grads, (), [])
    first_backs = ring_blocks(first_back, tp_count)
    second_back, second_sum, grads, grads_swap = back_of(
        1, second_grads, so_far, [normed_other, hidden_other]
    )
    second_backs = ring_blocks(second_back, tp_count)
    grads_other = core_swap(grads_swap, ctx_count)
    back_sum = first_sum[0] + second_sum[0]

    def grad_w2_share(member, span, dtype, after):
        share, local = grads.shape[1] // ctx_count, hidden.shape[1]
        tile = divisor(share, 256, 128)
        steps = share // tile
        return pair_product(
            (grads, grads_other, hidden, hidden_other),
            [
                pl.BlockSpec((row_count, tile), lambda t, m: (0, m[0] * steps + t)),
                pl.BlockSpec((row_count, tile), lambda t, m: (m[0] // 2, t)),
                pl.BlockSpec((row_count, local), lambda t, m: (0, 0)),
                pl.BlockSpec((row_count, local), lambda t, m: (0, 0)),
            ],
            ((0,), (0,)), (share, local), tile, row_count, member, grad_scale, dtype, after,
        )

    going_w2, (arrived_w2,) = chip_products(grad_w2_share, [None], ctx_count, [])
    member = lax.axis_index("ctx")

    def norm_of(chunk, blocks, so_far, after):
        return norm_part(
            ring, blocks, w_up_t, gain, normed_t, chunk, image_rows, ctx_count, so_far, after
        )

    def slots_of(chunk, gained_t, means):
        return visual_slots(
            source, present, gained_t, normed_t, means, inverse_std[None, :], chunk, part_rows
        )

    first_gained, first_rows, first_ln, *so_far = norm_of(0, first_backs, (), [])
    first_means = doubling_sum(first_rows, "tp", tp_count) / full_width
    first_slots, first_means = tie(
        [slots_of(0, first_gained, first_means), first_means], second_backs[-2:]
    )
    outgoing = [first_slots]
    second_gained, second_rows, second_ln, backs, backs_swap = norm_of(
        1, second_backs, so_far, [first_means, grads_other]
    )
    backs_other = core_swap(backs_swap, ctx_count)

    w1_tile = divisor(width, 400, 16)
    w1_tiles = width // w1_tile

    def grad_w1_share(member, span, dtype, after):
        share = backs.shape[1] // ctx_count
        first, last = span
        return pair_product(
            (normed_t, normed_other, backs, backs_other),
            [
                pl.BlockSpec((w1_tile, row_count), lambda t, m: (first + t, 0)),
                pl.BlockSpec((w1_tile, row_count), lambda t, m: (first + t, 0)),
                pl.BlockSpec((row_count, share), lambda t, m: (0, m[0])),
                pl.BlockSpec((row_count, share), lambda t, m: (m[0] // 2, 0)),
            ],
            ((1,), (0,)), ((last - first) * w1_tile, share), w1_tile, row_count, member,
            grad_scale, dtype, after,
        )

    spans = [(0, 1), (1, w1_tiles)] if w1_tiles > 1 else [(0, 1)]
    going_w1, arrived_w1 = chip_products(grad_w1_share, spans, ctx_count, going_w2)

    second_means = doubling_sum(second_rows, "tp", tp_count, going_w1) / full_width
    second_slots, second_means = tie(
        [slots_of(1, second_gained, second_means), second_means], arrived_w1[0] + arrived_w2
    )
    outgoing.append(second_slots)
    received = [
        lax.all_to_all(part, "tp", split_axis=0, concat_axis=0, tiled=True) for part in outgoing
    ]
    ln_sum = (first_ln + second_ln)[:, :2]
    small = jnp.concatenate(
        [jnp.sum(out_grad.astype(jnp.float32), axis=0), back_sum, ln_sum.T.reshape(-1)]
    )
    (small,) = tie([small], sum(arrived_w1, []))
    small = doubling_sum(small, "ctx", ctx_count) * grad_scale
    grad_w2 = add_arrived(grad_w2_share(member, None, jnp.float32, [second_means]), 0, arrived_w2)
    grad_w1_t = grad_w1_share(member, (0, w1_tiles), jnp.float32, [second_means])
    for (first, _), parts in zip(spans, arrived_w1):
        grad_w1_t = add_arrived(grad_w1_t, first * w1_tile, parts)
    assert capacity == 1
    vit_grad = None
    for chunk in range(CHUNKS):
        columns = received[chunk].reshape(tp_count * width, part_rows)
        after = [grad_w1_t, grad_w2] if chunk + 1 == CHUNKS else []
        vit_grad = turn_rows(columns, chunk, image_rows, vit_grad, after)

    features_in = out_grad.shape[1]
    hidden_in = pre_act.shape[1]
    bias_down = small[:features_in]
    bias_up = small[features_in : features_in + hidden_in]
    ln_grads = small[features_in + hidden_in :].reshape(2, width)
    return (grad_w2, grad_w1_t.T, bias_up, bias_down, ln_grads, vit_grad)


def solution(mesh):
    return jax.shard_map(
        per_device,
        mesh=mesh,
        in_specs=(
            P("ctx", "tp"),
            P("ctx", "tp"),
            P("ctx", "tp"),
            P("ctx"),
            P(None, "tp"),
            P(None, "tp"),
            P("tp"),
            P("ctx", None),
        ),
        out_specs=(
            P("ctx", "tp"),
            P("ctx", "tp"),
            P("tp"),
            P("tp"),
            P(None, "tp"),
            P(("ctx", "tp"), None),
        ),
        check_vma=False,
    )
```

```python
import functools
import math

import jax
import jax.numpy as jnp
from jax import lax
from jax.experimental import pallas as pl
from jax.experimental.pallas import tpu as pltpu
from jax.sharding import PartitionSpec as P

CHUNKS = 2
VMEM_LIMIT = 48 * 1024 * 1024
NORM_VMEM_LIMIT = 32 * 1024 * 1024


def gelu_parts(linear):
    normal_cdf = 0.5 * (1.0 + jax.scipy.special.erf(linear * 2.0 ** (-0.5)))
    density = jnp.exp(-0.5 * linear * linear) * (2.0 * math.pi) ** (-0.5)
    return (linear * normal_cdf, normal_cdf + linear * density)


def slot_numbers(owners, capacity):
    position = jnp.arange(owners.shape[0])
    earlier = (owners[None, :] == owners[:, None]) & (position[None, :] < position[:, None])
    return owners * capacity + jnp.sum(earlier.astype(jnp.int32), axis=1)


def divisor(extent, most, unit):
    return max(d for d in range(unit, most + 1, unit) if extent % d == 0)


def ring_order(count):
    depth = 4 if count % 4 == 0 else count
    width = count // depth
    walk = [(z, 0) for z in range(depth)]
    if width > 1:
        for turn, z in enumerate(reversed(range(depth))):
            ys = list(range(1, width))
            walk += [(z, y) for y in (ys if turn % 2 == 0 else ys[::-1])]
    return [z * width + y for z, y in walk]


def ring_owners(count):
    order = ring_order(count)
    table = []
    for j in range(count):
        at = order.index(j)
        steps = [0]
        for step in range(1, count // 2):
            steps += [-step, step]
        steps += [count // 2]
        table.append([order[(at + s) % count] for s in steps])
    core = (lax.axis_index("ctx") % 2).astype(jnp.int32)
    return jnp.concatenate([jnp.array(table, jnp.int32)[lax.axis_index("tp")], core[None]])


def ring_blocks(block, count):
    order = ring_order(count)
    ahead = [(order[p], order[(p + 1) % count]) for p in range(count)]
    behind = [(order[p], order[(p - 1) % count]) for p in range(count)]
    up, down = block, block
    blocks = [block]
    for _ in range(1, count // 2):
        up = lax.ppermute(up, "tp", ahead)
        down = lax.ppermute(down, "tp", behind)
        blocks += [up, down]
    half = block.shape[0] // 2
    blocks.append(lax.ppermute(up[:half], "tp", ahead))
    blocks.append(lax.ppermute(down[half:], "tp", behind))
    return blocks


def assemble(owners_ref, block_refs, held, sems):
    rows, width = block_refs[0].shape
    half = rows // 2
    last = len(block_refs) - 2
    copies = []
    for k, ref in enumerate(block_refs):
        columns = pl.ds(pl.multiple_of(owners_ref[min(k, last)] * width, width), width)
        if k < last:
            target = held.at[:, columns]
        else:
            target = held.at[pl.ds((k - last) * half, half), columns]
        copies.append(pltpu.make_async_copy(ref, target, sems.at[k]))
    return copies


def spread(ring_ref, held, full_ref, swap_ref, chunk, image_rows, sems):
    rows, part_rows = held.shape[0], image_rows // CHUNKS
    all_rows, member_width = full_ref.shape[0], swap_ref.shape[1]
    other = 1 - ring_ref[ring_ref.shape[0] - 1]
    copies = []
    for i in range(rows // part_rows):
        source = pl.ds(i * part_rows, part_rows)
        place = i * image_rows + chunk * part_rows
        copies.append((held.at[source, :], full_ref.at[pl.ds(place, part_rows), :]))
        for chip in range(swap_ref.shape[0] // all_rows):
            columns = pl.ds(
                pl.multiple_of((2 * chip + other) * member_width, member_width), member_width
            )
            target = swap_ref.at[pl.ds(chip * all_rows + place, part_rows), :]
            copies.append((held.at[source, columns], target))
    return [
        pltpu.make_async_copy(source, target, sems.at[n])
        for n, (source, target) in enumerate(copies)
    ]


def spread_shapes(rows, chunk_rows, full, ctx_count, images):
    shapes = (
        jax.ShapeDtypeStruct((rows, full), jnp.bfloat16),
        jax.ShapeDtypeStruct((rows * (ctx_count // 2), full // ctx_count), jnp.bfloat16),
    )
    scratch = [
        pltpu.VMEM((chunk_rows, full), jnp.bfloat16),
        pltpu.SemaphoreType.DMA((2 * tp_most(),)),
        pltpu.SemaphoreType.DMA((images * (1 + ctx_count // 2),)),
    ]
    return shapes, scratch


def tp_most():
    return lax.axis_size("tp")


def back_kernel(chunk, image_rows, blocks, carried, ring_ref, *refs):
    block_refs, refs = refs[:blocks], refs[blocks:]
    w_ref, slope_ref, *refs = refs
    back_ref, sum_ref, full_ref, swap_ref, held, sems, out_sems = refs[carried:]
    copies = assemble(ring_ref, block_refs, held, sems)
    for copy in copies:
        copy.start()
    for copy in copies:
        copy.wait()
    outs = spread(ring_ref, held, full_ref, swap_ref, chunk, image_rows, out_sems)
    for copy in outs:
        copy.start()
    rows, part_rows = held.shape[0], image_rows // CHUNKS
    tile = divisor(rows, 256, part_rows)
    sums = jnp.zeros(sum_ref.shape, jnp.float32)
    for start in range(0, rows, tile):
        total = jnp.dot(
            held[start : start + tile, :], w_ref[...], preferred_element_type=jnp.float32
        )
        for n in range(tile // part_rows):
            image = start // part_rows + n
            place = image * image_rows + chunk * part_rows
            part = (
                total[n * part_rows : (n + 1) * part_rows]
                * slope_ref[place : place + part_rows, :]
            ).astype(back_ref.dtype)
            back_ref[image * part_rows : (image + 1) * part_rows, :] = part
            sums += jnp.sum(part.astype(jnp.float32), axis=0, keepdims=True)
    sum_ref[...] = sums
    for copy in outs:
        copy.wait()


def back_part(ring, blocks, w_down, slope, chunk, image_rows, ctx_count, so_far, after):
    rows = blocks[0].shape[0]
    full, width = w_down.shape
    images = slope.shape[0] // image_rows
    shapes, scratch = spread_shapes(slope.shape[0], rows, full, ctx_count, images)
    first = 1 + len(blocks) + 2
    return pl.pallas_call(
        functools.partial(
            back_kernel, chunk, image_rows, len(blocks), len(so_far) + len(after)
        ),
        out_shape=(
            jax.ShapeDtypeStruct((rows, width), jnp.bfloat16),
            jax.ShapeDtypeStruct((1, width), jnp.float32),
        )
        + shapes,
        in_specs=[pl.BlockSpec(memory_space=pltpu.SMEM)]
        + [pl.BlockSpec(memory_space=pl.ANY)] * len(blocks)
        + [pl.BlockSpec(memory_space=pltpu.VMEM)] * 2
        + [pl.BlockSpec(memory_space=pltpu.HBM)] * (len(so_far) + len(after)),
        out_specs=(pl.BlockSpec(memory_space=pltpu.VMEM),) * 2
        + (pl.BlockSpec(memory_space=pltpu.HBM),) * 2,
        scratch_shapes=scratch,
        input_output_aliases={first + n: 2 + n for n in range(len(so_far))},
        compiler_params=pltpu.CompilerParams(vmem_limit_bytes=VMEM_LIMIT),
        cost_estimate=pl.CostEstimate(
            flops=2 * rows * full * width,
            bytes_accessed=2 * (2 * rows * full + full * width),
            transcendentals=0,
        ),
    )(ring, *blocks, w_down, slope, *so_far, *after)


def norm_kernel(chunk, image_rows, blocks, images, carried, ring_ref, *refs):
    block_refs, refs = refs[:blocks], refs[blocks:]
    w_ref, gain_ref, *refs = refs
    normed_refs, refs = refs[:images], refs[images:]
    gained_ref, sums_ref, ln_ref, full_ref, swap_ref, held, sems, out_sems = refs[carried:]
    step = pl.program_id(0)
    outs = spread(ring_ref, held, full_ref, swap_ref, chunk, image_rows, out_sems)

    @pl.when(step == 0)
    def _():
        copies = assemble(ring_ref, block_refs, held, sems)
        for copy in copies:
            copy.start()
        for copy in copies:
            copy.wait()
        for copy in outs:
            copy.start()
        sums_ref[...] = jnp.zeros_like(sums_ref)

    grad = lax.dot_general(
        w_ref[...], held[...], (((1,), (1,)), ((), ())), preferred_element_type=jnp.float32
    )
    features = jnp.concatenate([ref[...] for ref in normed_refs], axis=1).astype(jnp.float32)
    gained = gain_ref[...] * grad
    gained_ref[...] = gained
    sums_ref[0:1, :] += jnp.sum(gained, axis=0, keepdims=True)
    sums_ref[1:2, :] += jnp.sum(gained * features, axis=0, keepdims=True)
    gains = jnp.sum(grad * features, axis=1, keepdims=True)
    biases = jnp.sum(grad, axis=1, keepdims=True)
    lane = lax.broadcasted_iota(jnp.int32, ln_ref.shape, 1)
    ln_ref[...] = jnp.where(lane == 0, gains, biases)

    @pl.when(step == pl.num_programs(0) - 1)
    def _():
        for copy in outs:
            copy.wait()


def norm_part(ring, blocks, w_up_t, gain, normed_t, chunk, image_rows, ctx_count, so_far, after):
    rows = blocks[0].shape[0]
    width, full = w_up_t.shape
    part_rows = image_rows // CHUNKS
    images = rows // part_rows
    tile = divisor(width, 400, 16)
    shapes, scratch = spread_shapes(normed_t.shape[1], rows, full, ctx_count, images)
    first = 1 + len(blocks) + 2 + images
    return pl.pallas_call(
        functools.partial(
            norm_kernel, chunk, image_rows, len(blocks), images, len(so_far) + len(after)
        ),
        grid=(width // tile,),
        out_shape=(
            jax.ShapeDtypeStruct((width, rows), jnp.float32),
            jax.ShapeDtypeStruct((2, rows), jnp.float32),
            jax.ShapeDtypeStruct((width, 128), jnp.float32),
        )
        + shapes,
        in_specs=[pl.BlockSpec(memory_space=pltpu.SMEM)]
        + [pl.BlockSpec(memory_space=pl.ANY)] * len(blocks)
        + [
            pl.BlockSpec((tile, full), lambda t: (t, 0)),
            pl.BlockSpec((tile, 1), lambda t: (t, 0)),
        ]
        + [
            pl.BlockSpec((tile, part_rows), lambda t, i=i: (t, i * CHUNKS + chunk))
            for i in range(images)
        ]
        + [pl.BlockSpec(memory_space=pltpu.HBM)] * (len(so_far) + len(after)),
        out_specs=(
            pl.BlockSpec((tile, rows), lambda t: (t, 0)),
            pl.BlockSpec((2, rows), lambda t: (0, 0)),
            pl.BlockSpec((tile, 128), lambda t: (t, 0)),
        )
        + (pl.BlockSpec(memory_space=pltpu.HBM),) * 2,
        scratch_shapes=scratch,
        input_output_aliases={first + n: 3 + n for n in range(len(so_far))},
        compiler_params=pltpu.CompilerParams(vmem_limit_bytes=NORM_VMEM_LIMIT),
        cost_estimate=pl.CostEstimate(
            flops=2 * rows * full * width,
            bytes_accessed=2 * (full * width + 2 * rows * full) + 6 * rows * width,
            transcendentals=0,
        ),
    )(ring, *blocks, w_up_t, gain, *[normed_t] * images, *so_far, *after)


def pair_kernel(contract, scale, members_ref, a_ref, a_other_ref, b_ref, b_other_ref, *refs):
    *send_refs, own_ref = refs[-3:]
    dims = (contract, ((), ()))
    total = lax.dot_general(a_ref[...], b_ref[...], dims, preferred_element_type=jnp.float32)
    total += lax.dot_general(
        a_other_ref[...], b_other_ref[...], dims, preferred_element_type=jnp.float32
    )
    total *= scale
    own = pl.program_id(0) == pl.num_programs(0) - 1
    early = pl.program_id(1) == 0

    @pl.when(own)
    def _():
        own_ref[...] = total

    @pl.when(jnp.logical_not(own) & early)
    def _():
        send_refs[0][...] = total.astype(jnp.bfloat16)

    @pl.when(jnp.logical_not(own) & jnp.logical_not(early))
    def _():
        send_refs[1][...] = total.astype(jnp.bfloat16)


def pair_product(operands, specs, contract, shape, tile, depth, scale, after):
    index, pairs = lax.axis_index("ctx"), lax.axis_size("ctx") // 2
    members = jnp.stack([(index + 2 * s) % (2 * pairs) for s in range(1, pairs + 1)])
    steps, others = shape[0] // tile, pairs - 1
    rest = steps - 1
    block = (tile, shape[1])
    return pl.pallas_call(
        functools.partial(pair_kernel, contract, scale),
        grid_spec=pltpu.PrefetchScalarGridSpec(
            num_scalar_prefetch=1,
            grid=(pairs, steps),
            in_specs=specs + [pl.BlockSpec(memory_space=pltpu.HBM)] * len(after),
            out_specs=(
                pl.BlockSpec(block, lambda s, t, m: (jnp.minimum(s, others - 1), 0)),
                pl.BlockSpec(
                    block,
                    lambda s, t, m: (
                        jnp.where(s < others, s * rest + jnp.maximum(t - 1, 0), others * rest - 1),
                        0,
                    ),
                ),
                pl.BlockSpec(block, lambda s, t, m: (jnp.where(s < others, 0, t), 0)),
            ),
        ),
        out_shape=(
            jax.ShapeDtypeStruct((others * tile, shape[1]), jnp.bfloat16),
            jax.ShapeDtypeStruct((others * rest * tile, shape[1]), jnp.bfloat16),
            jax.ShapeDtypeStruct(shape, jnp.float32),
        ),
        compiler_params=pltpu.CompilerParams(vmem_limit_bytes=VMEM_LIMIT),
        cost_estimate=pl.CostEstimate(
            flops=4 * pairs * shape[0] * shape[1] * depth,
            bytes_accessed=4 * depth * (shape[0] + shape[1]) + 4 * pairs * shape[0] * shape[1],
            transcendentals=0,
        ),
    )(members.astype(jnp.int32), *operands, *after)


def add_kernel(own_ref, *refs):
    total = own_ref[...]
    for ref in refs[:-1]:
        total += ref[...].astype(jnp.float32)
    refs[-1][...] = total


def add_arrived(own, first_row, arrived):
    rows, width = arrived[0].shape
    tile = divisor(math.gcd(rows, first_row), 512, 16)
    place = lambda t: (first_row // tile + t, 0)
    return pl.pallas_call(
        add_kernel,
        grid=(rows // tile,),
        in_specs=[pl.BlockSpec((tile, width), place)]
        + [pl.BlockSpec((tile, width), lambda t: (t, 0))] * len(arrived),
        out_specs=pl.BlockSpec((tile, width), place),
        out_shape=jax.ShapeDtypeStruct(own.shape, own.dtype),
        input_output_aliases={0: 0},
        compiler_params=pltpu.CompilerParams(vmem_limit_bytes=VMEM_LIMIT),
        cost_estimate=pl.CostEstimate(
            flops=rows * width * len(arrived),
            bytes_accessed=rows * width * (8 + 2 * len(arrived)),
            transcendentals=0,
        ),
    )(own, *arrived)


def chip_exchange(going, ctx_count):
    others = ctx_count // 2 - 1
    rows = going.shape[0] // others
    arrived = []
    for shift in range(1, others + 1):
        part = going[(shift - 1) * rows : shift * rows] if others > 1 else going
        route = [(c, (c + 2 * shift) % ctx_count) for c in range(ctx_count)]
        arrived.append(lax.ppermute(part, "ctx", route))
    return arrived


def tie_kernel(*refs):
    del refs


def tie(values, others):
    return pl.pallas_call(
        tie_kernel,
        in_specs=[pl.BlockSpec(memory_space=pl.ANY)] * (len(values) + len(others)),
        out_specs=[pl.BlockSpec(memory_space=pl.ANY)] * len(values),
        out_shape=[jax.ShapeDtypeStruct(value.shape, value.dtype) for value in values],
        input_output_aliases={n: n for n in range(len(values))},
        compiler_params=pltpu.CompilerParams(vmem_limit_bytes=VMEM_LIMIT),
    )(*values, *others)


def visual_kernel(
    source_ref, present_ref, gained_ref, normed_ref, means_ref, inverse_ref, out_ref
):
    slot = pl.program_id(0)

    @pl.when(present_ref[slot] == 0)
    def _():
        out_ref[...] = jnp.zeros_like(out_ref)

    @pl.when(present_ref[slot] != 0)
    def _():
        gained = gained_ref[...]
        features = normed_ref[...].astype(jnp.float32)
        first, second = means_ref[0:1, :], means_ref[1:2, :]
        out_ref[0] = (inverse_ref[...] * (gained - first - features * second)).astype(
            out_ref.dtype
        )


def visual_slots(source, present, gained_t, normed_t, means, inverse, chunk, part_rows):
    width = gained_t.shape[0]
    slots = source.shape[0]
    picked = lambda s, source, present: (0, source[s])
    natural = lambda s, source, present: (0, source[s] * CHUNKS + chunk)
    return pl.pallas_call(
        visual_kernel,
        grid_spec=pltpu.PrefetchScalarGridSpec(
            num_scalar_prefetch=2,
            grid=(slots,),
            in_specs=[
                pl.BlockSpec((width, part_rows), picked),
                pl.BlockSpec((width, part_rows), natural),
                pl.BlockSpec((2, part_rows), picked),
                pl.BlockSpec((1, part_rows), natural),
            ],
            out_specs=pl.BlockSpec((1, width, part_rows), lambda s, source, present: (s, 0, 0)),
        ),
        out_shape=jax.ShapeDtypeStruct((slots, width, part_rows), jnp.bfloat16),
        compiler_params=pltpu.CompilerParams(vmem_limit_bytes=VMEM_LIMIT),
        cost_estimate=pl.CostEstimate(
            flops=6 * slots * width * part_rows,
            bytes_accessed=8 * slots * width * part_rows,
            transcendentals=0,
        ),
    )(source, present, gained_t, normed_t, means, inverse)


def turn_kernel(in_ref, *refs):
    refs[-1][...] = in_ref[...].T


def turn_rows(received, chunk, rows, so_far, after):
    full, part_rows = received.shape
    tile = divisor(full, 2560, 128)
    operands, aliases = [received], {}
    if so_far is not None:
        operands.append(so_far)
        aliases = {1: 0}
    operands += after
    specs = [pl.BlockSpec((tile, part_rows), lambda t: (t, 0))]
    specs += [pl.BlockSpec(memory_space=pltpu.HBM)] * (len(operands) - 1)
    return pl.pallas_call(
        turn_kernel,
        grid=(full // tile,),
        in_specs=specs,
        out_specs=pl.BlockSpec((part_rows, tile), lambda t: (chunk, t)),
        out_shape=jax.ShapeDtypeStruct((rows, full), received.dtype),
        input_output_aliases=aliases,
        compiler_params=pltpu.CompilerParams(vmem_limit_bytes=VMEM_LIMIT),
        cost_estimate=pl.CostEstimate(
            flops=0, bytes_accessed=4 * part_rows * full, transcendentals=0
        ),
    )(*operands)


def core_swap(value, ctx_count):
    return lax.ppermute(value, "ctx", [(c, c ^ 1) for c in range(ctx_count)])


def doubling_sum(value, axis, count, after=()):
    bit = 1
    while bit < count:
        if after and 2 * bit >= count:
            (value,) = tie([value], after)
        value = value + lax.ppermute(value, axis, [(t, t ^ bit) for t in range(count)])
        bit *= 2
    return value


def per_device(out_grad, pre_act, normed, inverse_std, w_up, w_down, ln_gain, owner_map):
    ctx_count = lax.axis_size("ctx")
    tp_count = lax.axis_size("tp")
    row_count = out_grad.shape[0]
    width = normed.shape[1]
    grad_scale = float(row_count * ctx_count) ** (-0.5)
    full_width = float(width * tp_count)

    owners = owner_map[0]
    image_count = owners.shape[0]
    image_rows = row_count // image_count
    part_rows = image_rows // CHUNKS
    chunk_rows = row_count // CHUNKS
    capacity = max(1, 2 * image_count // tp_count)
    slot_of = slot_numbers(owners, capacity)
    slot_ids = jnp.arange(tp_count * capacity)
    matches = slot_of[None, :] == slot_ids[:, None]
    present = jnp.any(matches, axis=1).astype(jnp.int32)
    source = jnp.sum(jnp.where(matches, jnp.arange(image_count)[None, :], 0), axis=1).astype(
        jnp.int32
    )

    def chunk_of(array, chunk):
        images = array.reshape((image_count, image_rows) + array.shape[1:])
        piece = images[:, chunk * part_rows : (chunk + 1) * part_rows]
        return piece.reshape((chunk_rows,) + array.shape[1:])

    ring = ring_owners(tp_count)
    gelu_value, slope = gelu_parts(pre_act.astype(jnp.float32))
    hidden = gelu_value.astype(jnp.bfloat16)
    hidden_other = core_swap(hidden, ctx_count)
    normed_t = normed.T
    normed_other = core_swap(normed_t, ctx_count)
    gain = ln_gain[:, None]
    w_up_t = w_up.T

    def back_of(chunk, blocks, so_far, after):
        return back_part(
            ring, blocks, w_down, slope, chunk, image_rows, ctx_count, so_far, after
        )

    first_grads, second_grads = [
        ring_blocks(chunk_of(out_grad, chunk), tp_count) for chunk in range(CHUNKS)
    ]
    first_back, first_sum, *so_far = back_of(0, first_grads, (), [])
    first_backs = ring_blocks(first_back, tp_count)
    second_back, second_sum, grads, grads_swap = back_of(1, second_grads, so_far, [])
    second_backs = ring_blocks(second_back, tp_count)
    grads_other = core_swap(grads_swap, ctx_count)
    back_sum = first_sum[0] + second_sum[0]

    w2_share, w2_width = grads.shape[1] // ctx_count, hidden.shape[1]
    w2_tile = divisor(w2_share, 256, 128)
    w2_steps = w2_share // w2_tile
    going_w2, rest_w2, own_w2 = pair_product(
        (grads, grads_other, hidden, hidden_other),
        [
            pl.BlockSpec((row_count, w2_tile), lambda s, t, m: (0, m[s] * w2_steps + t)),
            pl.BlockSpec((row_count, w2_tile), lambda s, t, m: (m[s] // 2, t)),
            pl.BlockSpec((row_count, w2_width), lambda s, t, m: (0, 0)),
            pl.BlockSpec((row_count, w2_width), lambda s, t, m: (0, 0)),
        ],
        ((0,), (0,)), (w2_share, w2_width), w2_tile, row_count, grad_scale, [],
    )
    arrived_w2 = [chip_exchange(going, ctx_count) for going in (going_w2, rest_w2)]


    def norm_of(chunk, blocks, so_far, after):
        return norm_part(
            ring, blocks, w_up_t, gain, normed_t, chunk, image_rows, ctx_count, so_far, after
        )

    def slots_of(chunk, gained_t, means):
        return visual_slots(
            source, present, gained_t, normed_t, means, inverse_std[None, :], chunk, part_rows
        )

    first_gained, first_rows, first_ln, *so_far = norm_of(0, first_backs, (), [])
    first_means = doubling_sum(first_rows, "tp", tp_count) / full_width
    first_slots, first_means = tie(
        [slots_of(0, first_gained, first_means), first_means], second_backs[-2:]
    )
    outgoing = [first_slots]
    second_gained, second_rows, second_ln, backs, backs_swap = norm_of(
        1, second_backs, so_far, [first_means, grads_other, normed_other, hidden_other]
    )
    backs_other = core_swap(backs_swap, ctx_count)

    w1_tile = divisor(width, 400, 16)

    w1_share = backs.shape[1] // ctx_count
    going_w1, rest_w1, own_w1 = pair_product(
        (normed_t, normed_other, backs, backs_other),
        [
            pl.BlockSpec((w1_tile, row_count), lambda s, t, m: (t, 0)),
            pl.BlockSpec((w1_tile, row_count), lambda s, t, m: (t, 0)),
            pl.BlockSpec((row_count, w1_share), lambda s, t, m: (0, m[s])),
            pl.BlockSpec((row_count, w1_share), lambda s, t, m: (m[s] // 2, 0)),
        ],
        ((1,), (0,)), (width, w1_share), w1_tile, row_count, grad_scale, [going_w2],
    )
    arrived_w1 = [chip_exchange(going, ctx_count) for going in (going_w1, rest_w1)]

    second_means = doubling_sum(second_rows, "tp", tp_count, [going_w1]) / full_width
    outgoing += tie(
        [slots_of(1, second_gained, second_means)], arrived_w1[0] + sum(arrived_w2, [])
    )
    received = [
        lax.all_to_all(part, "tp", split_axis=0, concat_axis=0, tiled=True) for part in outgoing
    ]
    ln_sum = (first_ln + second_ln)[:, :2]
    small = jnp.concatenate(
        [jnp.sum(out_grad.astype(jnp.float32), axis=0), back_sum, ln_sum.T.reshape(-1)]
    )
    (small,) = tie([small], sum(arrived_w1, []))
    small = doubling_sum(small, "ctx", ctx_count) * grad_scale
    grad_w2 = add_arrived(own_w2, 0, arrived_w2[0])
    grad_w2 = add_arrived(grad_w2, w2_tile, arrived_w2[1])
    grad_w1_t = add_arrived(own_w1, 0, arrived_w1[0])
    grad_w1_t = add_arrived(grad_w1_t, w1_tile, arrived_w1[1])
    assert capacity == 1
    vit_grad = None
    for chunk in range(CHUNKS):
        columns = received[chunk].reshape(tp_count * width, part_rows)
        after = [grad_w1_t, grad_w2] if chunk + 1 == CHUNKS else []
        vit_grad = turn_rows(columns, chunk, image_rows, vit_grad, after)

    features_in = out_grad.shape[1]
    hidden_in = pre_act.shape[1]
    bias_down = small[:features_in]
    bias_up = small[features_in : features_in + hidden_in]
    ln_grads = small[features_in + hidden_in :].reshape(2, width)
    return (grad_w2, grad_w1_t.T, bias_up, bias_down, ln_grads, vit_grad)


def solution(mesh):
    return jax.shard_map(
        per_device,
        mesh=mesh,
        in_specs=(
            P("ctx", "tp"),
            P("ctx", "tp"),
            P("ctx", "tp"),
            P("ctx"),
            P(None, "tp"),
            P(None, "tp"),
            P("tp"),
            P("ctx", None),
        ),
        out_specs=(
            P("ctx", "tp"),
            P("ctx", "tp"),
            P("tp"),
            P("tp"),
            P(None, "tp"),
            P(("ctx", "tp"), None),
        ),
        check_vma=False,
    )
```

```python
import functools
import math

import jax
import jax.numpy as jnp
from jax import lax
from jax.experimental import pallas as pl
from jax.experimental.pallas import tpu as pltpu
from jax.sharding import PartitionSpec as P

CHUNKS = 2
VMEM_LIMIT = 48 * 1024 * 1024


def gelu_parts(linear):
    normal_cdf = 0.5 * (1.0 + jax.scipy.special.erf(linear * 2.0 ** (-0.5)))
    density = jnp.exp(-0.5 * linear * linear) * (2.0 * math.pi) ** (-0.5)
    return (linear * normal_cdf, normal_cdf + linear * density)


def slot_numbers(owners, capacity):
    position = jnp.arange(owners.shape[0])
    earlier = (owners[None, :] == owners[:, None]) & (position[None, :] < position[:, None])
    return owners * capacity + jnp.sum(earlier.astype(jnp.int32), axis=1)


def divisor(extent, most, unit):
    return max(d for d in range(unit, most + 1, unit) if extent % d == 0)


def ring_order(count):
    depth = 4 if count % 4 == 0 else count
    width = count // depth
    walk = [(z, 0) for z in range(depth)]
    if width > 1:
        for turn, z in enumerate(reversed(range(depth))):
            ys = list(range(1, width))
            walk += [(z, y) for y in (ys if turn % 2 == 0 else ys[::-1])]
    return [z * width + y for z, y in walk]


def ring_owners(count):
    order = ring_order(count)
    table = []
    for j in range(count):
        at = order.index(j)
        steps = [0]
        for step in range(1, count // 2):
            steps += [-step, step]
        steps += [count // 2]
        table.append([order[(at + s) % count] for s in steps])
    core = (lax.axis_index("ctx") % 2).astype(jnp.int32)
    return jnp.concatenate([jnp.array(table, jnp.int32)[lax.axis_index("tp")], core[None]])


def ring_blocks(block, count):
    order = ring_order(count)
    ahead = [(order[p], order[(p + 1) % count]) for p in range(count)]
    behind = [(order[p], order[(p - 1) % count]) for p in range(count)]
    up, down = block, block
    blocks = [block]
    for _ in range(1, count // 2):
        up = lax.ppermute(up, "tp", ahead)
        down = lax.ppermute(down, "tp", behind)
        blocks += [up, down]
    half = block.shape[0] // 2
    blocks.append(lax.ppermute(up[:half], "tp", ahead))
    blocks.append(lax.ppermute(down[half:], "tp", behind))
    return blocks


def assemble(owners_ref, block_refs, held, sems):
    rows, width = block_refs[0].shape
    half = rows // 2
    last = len(block_refs) - 2
    copies = []
    for k, ref in enumerate(block_refs):
        columns = pl.ds(pl.multiple_of(owners_ref[min(k, last)] * width, width), width)
        if k < last:
            target = held.at[:, columns]
        else:
            target = held.at[pl.ds((k - last) * half, half), columns]
        copies.append(pltpu.make_async_copy(ref, target, sems.at[k]))
    return copies


def spread(ring_ref, held, full_ref, swap_ref, chunk, image_rows, sems):
    rows, part_rows = held.shape[0], image_rows // CHUNKS
    all_rows, member_width = full_ref.shape[0], swap_ref.shape[1]
    other = 1 - ring_ref[ring_ref.shape[0] - 1]
    copies = []
    for i in range(rows // part_rows):
        source = pl.ds(i * part_rows, part_rows)
        place = i * image_rows + chunk * part_rows
        copies.append((held.at[source, :], full_ref.at[pl.ds(place, part_rows), :]))
        for chip in range(swap_ref.shape[0] // all_rows):
            columns = pl.ds(
                pl.multiple_of((2 * chip + other) * member_width, member_width), member_width
            )
            target = swap_ref.at[pl.ds(chip * all_rows + place, part_rows), :]
            copies.append((held.at[source, columns], target))
    return [
        pltpu.make_async_copy(source, target, sems.at[n])
        for n, (source, target) in enumerate(copies)
    ]


def spread_shapes(rows, chunk_rows, full, ctx_count, images):
    shapes = (
        jax.ShapeDtypeStruct((rows, full), jnp.bfloat16),
        jax.ShapeDtypeStruct((rows * (ctx_count // 2), full // ctx_count), jnp.bfloat16),
    )
    scratch = [
        pltpu.VMEM((chunk_rows, full), jnp.bfloat16),
        pltpu.SemaphoreType.DMA((2 * tp_most(),)),
        pltpu.SemaphoreType.DMA((images * (1 + ctx_count // 2),)),
    ]
    return shapes, scratch


def tp_most():
    return lax.axis_size("tp")


def back_kernel(chunk, image_rows, blocks, carried, ring_ref, *refs):
    block_refs, refs = refs[:blocks], refs[blocks:]
    w_ref, slope_ref, *refs = refs
    back_ref, sum_ref, full_ref, swap_ref, held, sems, out_sems = refs[carried:]
    copies = assemble(ring_ref, block_refs, held, sems)
    for copy in copies:
        copy.start()
    for copy in copies:
        copy.wait()
    outs = spread(ring_ref, held, full_ref, swap_ref, chunk, image_rows, out_sems)
    for copy in outs:
        copy.start()
    rows, part_rows = held.shape[0], image_rows // CHUNKS
    tile = divisor(rows, 256, part_rows)
    sums = jnp.zeros(sum_ref.shape, jnp.float32)
    for start in range(0, rows, tile):
        total = jnp.dot(
            held[start : start + tile, :], w_ref[...], preferred_element_type=jnp.float32
        )
        for n in range(tile // part_rows):
            image = start // part_rows + n
            place = image * image_rows + chunk * part_rows
            part = (
                total[n * part_rows : (n + 1) * part_rows]
                * slope_ref[place : place + part_rows, :]
            ).astype(back_ref.dtype)
            back_ref[image * part_rows : (image + 1) * part_rows, :] = part
            sums += jnp.sum(part.astype(jnp.float32), axis=0, keepdims=True)
    sum_ref[...] = sums
    for copy in outs:
        copy.wait()


def back_part(ring, blocks, w_down, slope, chunk, image_rows, ctx_count, so_far):
    rows = blocks[0].shape[0]
    full, width = w_down.shape
    images = slope.shape[0] // image_rows
    shapes, scratch = spread_shapes(slope.shape[0], rows, full, ctx_count, images)
    first = 1 + len(blocks) + 2
    return pl.pallas_call(
        functools.partial(back_kernel, chunk, image_rows, len(blocks), len(so_far)),
        out_shape=(
            jax.ShapeDtypeStruct((rows, width), jnp.bfloat16),
            jax.ShapeDtypeStruct((1, width), jnp.float32),
        )
        + shapes,
        in_specs=[pl.BlockSpec(memory_space=pltpu.SMEM)]
        + [pl.BlockSpec(memory_space=pl.ANY)] * len(blocks)
        + [pl.BlockSpec(memory_space=pltpu.VMEM)] * 2
        + [pl.BlockSpec(memory_space=pltpu.HBM)] * len(so_far),
        out_specs=(pl.BlockSpec(memory_space=pltpu.VMEM),) * 2
        + (pl.BlockSpec(memory_space=pltpu.HBM),) * 2,
        scratch_shapes=scratch,
        input_output_aliases={first + n: 2 + n for n in range(len(so_far))},
        compiler_params=pltpu.CompilerParams(vmem_limit_bytes=VMEM_LIMIT),
        cost_estimate=pl.CostEstimate(
            flops=2 * rows * full * width,
            bytes_accessed=2 * (2 * rows * full + full * width),
            transcendentals=0,
        ),
    )(ring, *blocks, w_down, slope, *so_far)


def norm_kernel(chunk, image_rows, blocks, images, carried, ring_ref, *refs):
    block_refs, refs = refs[:blocks], refs[blocks:]
    w_ref, gain_ref, *refs = refs
    normed_refs, refs = refs[:images], refs[images:]
    gained_ref, sums_ref, ln_ref, full_ref, swap_ref, held, sems, out_sems = refs[carried:]
    step = pl.program_id(0)
    outs = spread(ring_ref, held, full_ref, swap_ref, chunk, image_rows, out_sems)

    @pl.when(step == 0)
    def _():
        copies = assemble(ring_ref, block_refs, held, sems)
        for copy in copies:
            copy.start()
        for copy in copies:
            copy.wait()
        for copy in outs:
            copy.start()
        sums_ref[...] = jnp.zeros_like(sums_ref)

    grad = lax.dot_general(
        w_ref[...], held[...], (((1,), (1,)), ((), ())), preferred_element_type=jnp.float32
    )
    features = jnp.concatenate([ref[...] for ref in normed_refs], axis=1).astype(jnp.float32)
    gained = gain_ref[...] * grad
    gained_ref[...] = gained
    sums_ref[0:1, :] += jnp.sum(gained, axis=0, keepdims=True)
    sums_ref[1:2, :] += jnp.sum(gained * features, axis=0, keepdims=True)
    gains = jnp.sum(grad * features, axis=1, keepdims=True)
    biases = jnp.sum(grad, axis=1, keepdims=True)
    lane = lax.broadcasted_iota(jnp.int32, ln_ref.shape, 1)
    ln_ref[...] = jnp.where(lane == 0, gains, biases)

    @pl.when(step == pl.num_programs(0) - 1)
    def _():
        for copy in outs:
            copy.wait()


def norm_part(ring, blocks, w_up_t, gain, normed_t, chunk, image_rows, ctx_count, so_far, after):
    rows = blocks[0].shape[0]
    width, full = w_up_t.shape
    part_rows = image_rows // CHUNKS
    images = rows // part_rows
    tile = divisor(width, 400, 16)
    shapes, scratch = spread_shapes(normed_t.shape[1], rows, full, ctx_count, images)
    first = 1 + len(blocks) + 2 + images
    return pl.pallas_call(
        functools.partial(
            norm_kernel, chunk, image_rows, len(blocks), images, len(so_far) + len(after)
        ),
        grid=(width // tile,),
        out_shape=(
            jax.ShapeDtypeStruct((width, rows), jnp.float32),
            jax.ShapeDtypeStruct((2, rows), jnp.float32),
            jax.ShapeDtypeStruct((width, 128), jnp.float32),
        )
        + shapes,
        in_specs=[pl.BlockSpec(memory_space=pltpu.SMEM)]
        + [pl.BlockSpec(memory_space=pl.ANY)] * len(blocks)
        + [
            pl.BlockSpec((tile, full), lambda t: (t, 0)),
            pl.BlockSpec((tile, 1), lambda t: (t, 0)),
        ]
        + [
            pl.BlockSpec((tile, part_rows), lambda t, i=i: (t, i * CHUNKS + chunk))
            for i in range(images)
        ]
        + [pl.BlockSpec(memory_space=pltpu.HBM)] * (len(so_far) + len(after)),
        out_specs=(
            pl.BlockSpec((tile, rows), lambda t: (t, 0)),
            pl.BlockSpec((2, rows), lambda t: (0, 0)),
            pl.BlockSpec((tile, 128), lambda t: (t, 0)),
        )
        + (pl.BlockSpec(memory_space=pltpu.HBM),) * 2,
        scratch_shapes=scratch,
        input_output_aliases={first + n: 3 + n for n in range(len(so_far))},
        compiler_params=pltpu.CompilerParams(vmem_limit_bytes=VMEM_LIMIT),
        cost_estimate=pl.CostEstimate(
            flops=2 * rows * full * width,
            bytes_accessed=2 * (full * width + 2 * rows * full) + 6 * rows * width,
            transcendentals=0,
        ),
    )(ring, *blocks, w_up_t, gain, *[normed_t] * images, *so_far, *after)


def pair_kernel(
    contract, scale, ranges, member_ref, a_ref, a_other_ref, b_ref, b_other_ref, *refs
):
    arrived, out_ref = refs[: len(ranges)], refs[-1]
    dims = (contract, ((), ()))
    total = lax.dot_general(a_ref[...], b_ref[...], dims, preferred_element_type=jnp.float32)
    total += lax.dot_general(
        a_other_ref[...], b_other_ref[...], dims, preferred_element_type=jnp.float32
    )
    total *= scale
    step = pl.program_id(0)
    for (first, last), ref in zip(ranges, arrived):
        part = ref[...].astype(jnp.float32)
        total += jnp.where((step >= first) & (step < last), part, 0.0)
    out_ref[...] = total.astype(out_ref.dtype)


def pair_product(
    operands, specs, contract, shape, tile, depth, member, scale, arrived, dtype, after
):
    row_spec = lambda first, last: pl.BlockSpec(
        (tile, shape[1]), lambda t, m: (jnp.clip(t - first, 0, last - first - 1), 0)
    )
    steps = shape[0] // tile
    return pl.pallas_call(
        functools.partial(pair_kernel, contract, scale, [span for span, _ in arrived]),
        grid_spec=pltpu.PrefetchScalarGridSpec(
            num_scalar_prefetch=1,
            grid=(steps,),
            in_specs=specs
            + [row_spec(*span) for span, _ in arrived]
            + [pl.BlockSpec(memory_space=pltpu.HBM)] * len(after),
            out_specs=row_spec(0, steps),
        ),
        out_shape=jax.ShapeDtypeStruct(shape, dtype),
        compiler_params=pltpu.CompilerParams(vmem_limit_bytes=VMEM_LIMIT),
        cost_estimate=pl.CostEstimate(
            flops=4 * shape[0] * shape[1] * depth,
            bytes_accessed=4 * depth * (shape[0] + shape[1]) + 4 * shape[0] * shape[1],
            transcendentals=0,
        ),
    )(
        member.reshape(1).astype(jnp.int32),
        *operands,
        *[part for _, part in arrived],
        *after,
    )


def chip_products(product, spans, ctx_count, after):
    index = lax.axis_index("ctx")
    going, arrived = [], []
    for span in spans:
        for shift in range(1, ctx_count // 2):
            member = (index + 2 * shift) % ctx_count
            going.append(product(member, span, [], jnp.bfloat16, after))
            route = [(c, (c + 2 * shift) % ctx_count) for c in range(ctx_count)]
            arrived.append((span, lax.ppermute(going[-1], "ctx", route)))
    return going, arrived


def tie_kernel(*refs):
    del refs


def tie(values, others):
    return pl.pallas_call(
        tie_kernel,
        in_specs=[pl.BlockSpec(memory_space=pl.ANY)] * (len(values) + len(others)),
        out_specs=[pl.BlockSpec(memory_space=pl.ANY)] * len(values),
        out_shape=[jax.ShapeDtypeStruct(value.shape, value.dtype) for value in values],
        input_output_aliases={n: n for n in range(len(values))},
        compiler_params=pltpu.CompilerParams(vmem_limit_bytes=VMEM_LIMIT),
    )(*values, *others)


def visual_kernel(
    source_ref, present_ref, gained_ref, normed_ref, means_ref, inverse_ref, out_ref
):
    slot = pl.program_id(0)

    @pl.when(present_ref[slot] == 0)
    def _():
        out_ref[...] = jnp.zeros_like(out_ref)

    @pl.when(present_ref[slot] != 0)
    def _():
        gained = gained_ref[...]
        features = normed_ref[...].astype(jnp.float32)
        first, second = means_ref[0:1, :], means_ref[1:2, :]
        out_ref[0] = (inverse_ref[...] * (gained - first - features * second)).astype(
            out_ref.dtype
        )


def visual_slots(source, present, gained_t, normed_t, means, inverse, chunk, part_rows):
    width = gained_t.shape[0]
    slots = source.shape[0]
    picked = lambda s, source, present: (0, source[s])
    natural = lambda s, source, present: (0, source[s] * CHUNKS + chunk)
    return pl.pallas_call(
        visual_kernel,
        grid_spec=pltpu.PrefetchScalarGridSpec(
            num_scalar_prefetch=2,
            grid=(slots,),
            in_specs=[
                pl.BlockSpec((width, part_rows), picked),
                pl.BlockSpec((width, part_rows), natural),
                pl.BlockSpec((2, part_rows), picked),
                pl.BlockSpec((1, part_rows), natural),
            ],
            out_specs=pl.BlockSpec((1, width, part_rows), lambda s, source, present: (s, 0, 0)),
        ),
        out_shape=jax.ShapeDtypeStruct((slots, width, part_rows), jnp.bfloat16),
        compiler_params=pltpu.CompilerParams(vmem_limit_bytes=VMEM_LIMIT),
        cost_estimate=pl.CostEstimate(
            flops=6 * slots * width * part_rows,
            bytes_accessed=8 * slots * width * part_rows,
            transcendentals=0,
        ),
    )(source, present, gained_t, normed_t, means, inverse)


def turn_kernel(in_ref, *refs):
    refs[-1][...] = in_ref[...].T


def turn_rows(received, chunk, rows, so_far, after):
    full, part_rows = received.shape
    tile = divisor(full, 2560, 128)
    operands, aliases = [received], {}
    if so_far is not None:
        operands.append(so_far)
        aliases = {1: 0}
    operands += after
    specs = [pl.BlockSpec((tile, part_rows), lambda t: (t, 0))]
    specs += [pl.BlockSpec(memory_space=pltpu.HBM)] * (len(operands) - 1)
    return pl.pallas_call(
        turn_kernel,
        grid=(full // tile,),
        in_specs=specs,
        out_specs=pl.BlockSpec((part_rows, tile), lambda t: (chunk, t)),
        out_shape=jax.ShapeDtypeStruct((rows, full), received.dtype),
        input_output_aliases=aliases,
        compiler_params=pltpu.CompilerParams(vmem_limit_bytes=VMEM_LIMIT),
        cost_estimate=pl.CostEstimate(
            flops=0, bytes_accessed=4 * part_rows * full, transcendentals=0
        ),
    )(*operands)


def core_swap(value, ctx_count):
    return lax.ppermute(value, "ctx", [(c, c ^ 1) for c in range(ctx_count)])


def doubling_sum(value, axis, count, after=()):
    bit = 1
    while bit < count:
        if after and 2 * bit >= count:
            (value,) = tie([value], after)
        value = value + lax.ppermute(value, axis, [(t, t ^ bit) for t in range(count)])
        bit *= 2
    return value


def per_device(out_grad, pre_act, normed, inverse_std, w_up, w_down, ln_gain, owner_map):
    ctx_count = lax.axis_size("ctx")
    tp_count = lax.axis_size("tp")
    row_count = out_grad.shape[0]
    width = normed.shape[1]
    grad_scale = float(row_count * ctx_count) ** (-0.5)
    full_width = float(width * tp_count)

    owners = owner_map[0]
    image_count = owners.shape[0]
    image_rows = row_count // image_count
    part_rows = image_rows // CHUNKS
    chunk_rows = row_count // CHUNKS
    capacity = max(1, 2 * image_count // tp_count)
    slot_of = slot_numbers(owners, capacity)
    slot_ids = jnp.arange(tp_count * capacity)
    matches = slot_of[None, :] == slot_ids[:, None]
    present = jnp.any(matches, axis=1).astype(jnp.int32)
    source = jnp.sum(jnp.where(matches, jnp.arange(image_count)[None, :], 0), axis=1).astype(
        jnp.int32
    )

    def chunk_of(array, chunk):
        images = array.reshape((image_count, image_rows) + array.shape[1:])
        piece = images[:, chunk * part_rows : (chunk + 1) * part_rows]
        return piece.reshape((chunk_rows,) + array.shape[1:])

    ring = ring_owners(tp_count)
    gelu_value, slope = gelu_parts(pre_act.astype(jnp.float32))
    hidden = gelu_value.astype(jnp.bfloat16)
    hidden_other = core_swap(hidden, ctx_count)
    normed_t = normed.T
    normed_other = core_swap(normed_t, ctx_count)
    gain = ln_gain[:, None]
    w_up_t = w_up.T

    def back_of(chunk, blocks, so_far):
        return back_part(ring, blocks, w_down, slope, chunk, image_rows, ctx_count, so_far)

    first_grads, second_grads = [
        ring_blocks(chunk_of(out_grad, chunk), tp_count) for chunk in range(CHUNKS)
    ]
    first_back, first_sum, *so_far = back_of(0, first_grads, ())
    first_backs = ring_blocks(first_back, tp_count)
    second_back, second_sum, grads, grads_swap = back_of(1, second_grads, so_far)
    second_backs = ring_blocks(second_back, tp_count)
    grads_other = core_swap(grads_swap, ctx_count)
    back_sum = first_sum[0] + second_sum[0]

    def grad_w2_share(member, span, arrived, dtype, after):
        share, local = grads.shape[1] // ctx_count, hidden.shape[1]
        tile = divisor(share, 256, 128)
        steps = share // tile
        return pair_product(
            (grads, grads_other, hidden, hidden_other),
            [
                pl.BlockSpec((row_count, tile), lambda t, m: (0, m[0] * steps + t)),
                pl.BlockSpec((row_count, tile), lambda t, m: (m[0] // 2, t)),
                pl.BlockSpec((row_count, local), lambda t, m: (0, 0)),
                pl.BlockSpec((row_count, local), lambda t, m: (0, 0)),
            ],
            ((0,), (0,)), (share, local), tile, row_count, member, grad_scale, arrived, dtype,
            after,
        )

    w2_span = (0, grads.shape[1] // ctx_count // divisor(grads.shape[1] // ctx_count, 256, 128))
    going_w2, arrived_w2 = chip_products(grad_w2_share, [w2_span], ctx_count, [])
    member = lax.axis_index("ctx")

    def norm_of(chunk, blocks, so_far, after):
        return norm_part(
            ring, blocks, w_up_t, gain, normed_t, chunk, image_rows, ctx_count, so_far, after
        )

    def slots_of(chunk, gained_t, means):
        return visual_slots(
            source, present, gained_t, normed_t, means, inverse_std[None, :], chunk, part_rows
        )

    first_gained, first_rows, first_ln, *so_far = norm_of(0, first_backs, (), [])
    first_means = doubling_sum(first_rows, "tp", tp_count) / full_width
    first_slots, first_means = tie(
        [slots_of(0, first_gained, first_means), first_means], second_backs[-2:]
    )
    outgoing = [first_slots]
    second_gained, second_rows, second_ln, backs, backs_swap = norm_of(
        1, second_backs, so_far, [first_means]
    )
    backs_other = core_swap(backs_swap, ctx_count)

    w1_tile = divisor(width, 400, 16)
    w1_tiles = width // w1_tile

    def grad_w1_share(member, span, arrived, dtype, after):
        share = backs.shape[1] // ctx_count
        first, last = span
        return pair_product(
            (normed_t, normed_other, backs, backs_other),
            [
                pl.BlockSpec((w1_tile, row_count), lambda t, m: (first + t, 0)),
                pl.BlockSpec((w1_tile, row_count), lambda t, m: (first + t, 0)),
                pl.BlockSpec((row_count, share), lambda t, m: (0, m[0])),
                pl.BlockSpec((row_count, share), lambda t, m: (m[0] // 2, 0)),
            ],
            ((1,), (0,)), ((last - first) * w1_tile, share), w1_tile, row_count, member,
            grad_scale, arrived, dtype, after,
        )

    cut = w1_tiles // 2
    spans = [(0, cut), (cut, w1_tiles)] if cut else [(0, w1_tiles)]
    going_w1, arrived_w1 = chip_products(grad_w1_share, spans, ctx_count, going_w2)

    second_means = doubling_sum(second_rows, "tp", tp_count, going_w1) / full_width
    early = [part for span, part in arrived_w1 if span == spans[0]]
    outgoing += tie([slots_of(1, second_gained, second_means)], early)
    received = [
        lax.all_to_all(part, "tp", split_axis=0, concat_axis=0, tiled=True) for part in outgoing
    ]
    ln_sum = (first_ln + second_ln)[:, :2]
    small = jnp.concatenate(
        [jnp.sum(out_grad.astype(jnp.float32), axis=0), back_sum, ln_sum.T.reshape(-1)]
    )
    (small,) = tie([small], [part for _, part in arrived_w1])
    grad_w2 = grad_w2_share(member, w2_span, arrived_w2, jnp.float32, [small])
    small = doubling_sum(small, "ctx", ctx_count) * grad_scale
    grad_w1_t = grad_w1_share(member, (0, w1_tiles), arrived_w1, jnp.float32, [])
    assert capacity == 1
    vit_grad = None
    for chunk in range(CHUNKS):
        columns = received[chunk].reshape(tp_count * width, part_rows)
        after = [grad_w1_t, grad_w2] if chunk + 1 == CHUNKS else []
        vit_grad = turn_rows(columns, chunk, image_rows, vit_grad, after)

    features_in = out_grad.shape[1]
    hidden_in = pre_act.shape[1]
    bias_down = small[:features_in]
    bias_up = small[features_in : features_in + hidden_in]
    ln_grads = small[features_in + hidden_in :].reshape(2, width)
    return (grad_w2, grad_w1_t.T, bias_up, bias_down, ln_grads, vit_grad)


def solution(mesh):
    return jax.shard_map(
        per_device,
        mesh=mesh,
        in_specs=(
            P("ctx", "tp"),
            P("ctx", "tp"),
            P("ctx", "tp"),
            P("ctx"),
            P(None, "tp"),
            P(None, "tp"),
            P("tp"),
            P("ctx", None),
        ),
        out_specs=(
            P("ctx", "tp"),
            P("ctx", "tp"),
            P("tp"),
            P("tp"),
            P(None, "tp"),
            P(("ctx", "tp"), None),
        ),
        check_vma=False,
    )
```

```python
import functools
import math

import jax
import jax.numpy as jnp
from jax import lax
from jax.experimental import pallas as pl
from jax.experimental.pallas import tpu as pltpu
from jax.sharding import PartitionSpec as P

CHUNKS = 2
VMEM_LIMIT = 48 * 1024 * 1024


def gelu_parts(linear):
    normal_cdf = 0.5 * (1.0 + jax.scipy.special.erf(linear * 2.0 ** (-0.5)))
    density = jnp.exp(-0.5 * linear * linear) * (2.0 * math.pi) ** (-0.5)
    return (linear * normal_cdf, normal_cdf + linear * density)


def slot_numbers(owners, capacity):
    position = jnp.arange(owners.shape[0])
    earlier = (owners[None, :] == owners[:, None]) & (position[None, :] < position[:, None])
    return owners * capacity + jnp.sum(earlier.astype(jnp.int32), axis=1)


def divisor(extent, most, unit):
    return max(d for d in range(unit, most + 1, unit) if extent % d == 0)


def ring_order(count):
    depth = 4 if count % 4 == 0 else count
    width = count // depth
    walk = [(z, 0) for z in range(depth)]
    if width > 1:
        for turn, z in enumerate(reversed(range(depth))):
            ys = list(range(1, width))
            walk += [(z, y) for y in (ys if turn % 2 == 0 else ys[::-1])]
    return [z * width + y for z, y in walk]


def ring_owners(count):
    order = ring_order(count)
    table = []
    for j in range(count):
        at = order.index(j)
        steps = [0]
        for step in range(1, count // 2):
            steps += [-step, step]
        steps += [count // 2]
        table.append([order[(at + s) % count] for s in steps])
    core = (lax.axis_index("ctx") % 2).astype(jnp.int32)
    return jnp.concatenate([jnp.array(table, jnp.int32)[lax.axis_index("tp")], core[None]])


def ring_blocks(block, count):
    order = ring_order(count)
    ahead = [(order[p], order[(p + 1) % count]) for p in range(count)]
    behind = [(order[p], order[(p - 1) % count]) for p in range(count)]
    up, down = block, block
    blocks = [block]
    for _ in range(1, count // 2):
        up = lax.ppermute(up, "tp", ahead)
        down = lax.ppermute(down, "tp", behind)
        blocks += [up, down]
    half = block.shape[0] // 2
    blocks.append(lax.ppermute(up[:half], "tp", ahead))
    blocks.append(lax.ppermute(down[half:], "tp", behind))
    return blocks


def assemble(owners_ref, block_refs, held, sems):
    rows, width = block_refs[0].shape
    half = rows // 2
    last = len(block_refs) - 2
    copies = []
    for k, ref in enumerate(block_refs):
        columns = pl.ds(pl.multiple_of(owners_ref[min(k, last)] * width, width), width)
        if k < last:
            target = held.at[:, columns]
        else:
            target = held.at[pl.ds((k - last) * half, half), columns]
        copies.append(pltpu.make_async_copy(ref, target, sems.at[k]))
    return copies


def spread(ring_ref, held, full_ref, swap_ref, chunk, image_rows, sems):
    rows, part_rows = held.shape[0], image_rows // CHUNKS
    all_rows, member_width = full_ref.shape[0], swap_ref.shape[1]
    other = 1 - ring_ref[ring_ref.shape[0] - 1]
    copies = []
    for i in range(rows // part_rows):
        source = pl.ds(i * part_rows, part_rows)
        place = i * image_rows + chunk * part_rows
        copies.append((held.at[source, :], full_ref.at[pl.ds(place, part_rows), :]))
        for chip in range(swap_ref.shape[0] // all_rows):
            columns = pl.ds(
                pl.multiple_of((2 * chip + other) * member_width, member_width), member_width
            )
            target = swap_ref.at[pl.ds(chip * all_rows + place, part_rows), :]
            copies.append((held.at[source, columns], target))
    return [
        pltpu.make_async_copy(source, target, sems.at[n])
        for n, (source, target) in enumerate(copies)
    ]


def spread_shapes(rows, chunk_rows, full, ctx_count, images):
    shapes = (
        jax.ShapeDtypeStruct((rows, full), jnp.bfloat16),
        jax.ShapeDtypeStruct((rows * (ctx_count // 2), full // ctx_count), jnp.bfloat16),
    )
    scratch = [
        pltpu.VMEM((chunk_rows, full), jnp.bfloat16),
        pltpu.SemaphoreType.DMA((2 * tp_most(),)),
        pltpu.SemaphoreType.DMA((images * (1 + ctx_count // 2),)),
    ]
    return shapes, scratch


def tp_most():
    return lax.axis_size("tp")


def back_kernel(chunk, image_rows, blocks, carried, ring_ref, *refs):
    block_refs, refs = refs[:blocks], refs[blocks:]
    w_ref, slope_ref, *refs = refs
    back_ref, sum_ref, full_ref, swap_ref, held, sems, out_sems = refs[carried:]
    copies = assemble(ring_ref, block_refs, held, sems)
    for copy in copies:
        copy.start()
    for copy in copies:
        copy.wait()
    outs = spread(ring_ref, held, full_ref, swap_ref, chunk, image_rows, out_sems)
    for copy in outs:
        copy.start()
    rows, part_rows = held.shape[0], image_rows // CHUNKS
    tile = divisor(rows, 256, part_rows)
    sums = jnp.zeros(sum_ref.shape, jnp.float32)
    for start in range(0, rows, tile):
        total = jnp.dot(
            held[start : start + tile, :], w_ref[...], preferred_element_type=jnp.float32
        )
        for n in range(tile // part_rows):
            image = start // part_rows + n
            place = image * image_rows + chunk * part_rows
            part = (
                total[n * part_rows : (n + 1) * part_rows]
                * slope_ref[place : place + part_rows, :]
            ).astype(back_ref.dtype)
            back_ref[image * part_rows : (image + 1) * part_rows, :] = part
            sums += jnp.sum(part.astype(jnp.float32), axis=0, keepdims=True)
    sum_ref[...] = sums
    for copy in outs:
        copy.wait()


def back_part(ring, blocks, w_down, slope, chunk, image_rows, ctx_count, so_far):
    rows = blocks[0].shape[0]
    full, width = w_down.shape
    images = slope.shape[0] // image_rows
    shapes, scratch = spread_shapes(slope.shape[0], rows, full, ctx_count, images)
    first = 1 + len(blocks) + 2
    return pl.pallas_call(
        functools.partial(back_kernel, chunk, image_rows, len(blocks), len(so_far)),
        out_shape=(
            jax.ShapeDtypeStruct((rows, width), jnp.bfloat16),
            jax.ShapeDtypeStruct((1, width), jnp.float32),
        )
        + shapes,
        in_specs=[pl.BlockSpec(memory_space=pltpu.SMEM)]
        + [pl.BlockSpec(memory_space=pl.ANY)] * len(blocks)
        + [pl.BlockSpec(memory_space=pltpu.VMEM)] * 2
        + [pl.BlockSpec(memory_space=pltpu.HBM)] * len(so_far),
        out_specs=(pl.BlockSpec(memory_space=pltpu.VMEM),) * 2
        + (pl.BlockSpec(memory_space=pltpu.HBM),) * 2,
        scratch_shapes=scratch,
        input_output_aliases={first + n: 2 + n for n in range(len(so_far))},
        compiler_params=pltpu.CompilerParams(vmem_limit_bytes=VMEM_LIMIT),
        cost_estimate=pl.CostEstimate(
            flops=2 * rows * full * width,
            bytes_accessed=2 * (2 * rows * full + full * width),
            transcendentals=0,
        ),
    )(ring, *blocks, w_down, slope, *so_far)


def norm_kernel(chunk, image_rows, blocks, images, carried, ring_ref, *refs):
    block_refs, refs = refs[:blocks], refs[blocks:]
    w_ref, gain_ref, *refs = refs
    normed_refs, refs = refs[:images], refs[images:]
    gained_ref, sums_ref, ln_ref, full_ref, swap_ref, held, sems, out_sems = refs[carried:]
    step = pl.program_id(0)
    outs = spread(ring_ref, held, full_ref, swap_ref, chunk, image_rows, out_sems)

    @pl.when(step == 0)
    def _():
        copies = assemble(ring_ref, block_refs, held, sems)
        for copy in copies:
            copy.start()
        for copy in copies:
            copy.wait()
        for copy in outs:
            copy.start()
        sums_ref[...] = jnp.zeros_like(sums_ref)

    grad = lax.dot_general(
        w_ref[...], held[...], (((1,), (1,)), ((), ())), preferred_element_type=jnp.float32
    )
    features = jnp.concatenate([ref[...] for ref in normed_refs], axis=1).astype(jnp.float32)
    gained = gain_ref[...] * grad
    gained_ref[...] = gained
    sums_ref[0:1, :] += jnp.sum(gained, axis=0, keepdims=True)
    sums_ref[1:2, :] += jnp.sum(gained * features, axis=0, keepdims=True)
    gains = jnp.sum(grad * features, axis=1, keepdims=True)
    biases = jnp.sum(grad, axis=1, keepdims=True)
    lane = lax.broadcasted_iota(jnp.int32, ln_ref.shape, 1)
    ln_ref[...] = jnp.where(lane == 0, gains, biases)

    @pl.when(step == pl.num_programs(0) - 1)
    def _():
        for copy in outs:
            copy.wait()


def norm_part(ring, blocks, w_up_t, gain, normed_t, chunk, image_rows, ctx_count, so_far, after):
    rows = blocks[0].shape[0]
    width, full = w_up_t.shape
    part_rows = image_rows // CHUNKS
    images = rows // part_rows
    tile = divisor(width, 400, 16)
    shapes, scratch = spread_shapes(normed_t.shape[1], rows, full, ctx_count, images)
    first = 1 + len(blocks) + 2 + images
    return pl.pallas_call(
        functools.partial(
            norm_kernel, chunk, image_rows, len(blocks), images, len(so_far) + len(after)
        ),
        grid=(width // tile,),
        out_shape=(
            jax.ShapeDtypeStruct((width, rows), jnp.float32),
            jax.ShapeDtypeStruct((2, rows), jnp.float32),
            jax.ShapeDtypeStruct((width, 128), jnp.float32),
        )
        + shapes,
        in_specs=[pl.BlockSpec(memory_space=pltpu.SMEM)]
        + [pl.BlockSpec(memory_space=pl.ANY)] * len(blocks)
        + [
            pl.BlockSpec((tile, full), lambda t: (t, 0)),
            pl.BlockSpec((tile, 1), lambda t: (t, 0)),
        ]
        + [
            pl.BlockSpec((tile, part_rows), lambda t, i=i: (t, i * CHUNKS + chunk))
            for i in range(images)
        ]
        + [pl.BlockSpec(memory_space=pltpu.HBM)] * (len(so_far) + len(after)),
        out_specs=(
            pl.BlockSpec((tile, rows), lambda t: (t, 0)),
            pl.BlockSpec((2, rows), lambda t: (0, 0)),
            pl.BlockSpec((tile, 128), lambda t: (t, 0)),
        )
        + (pl.BlockSpec(memory_space=pltpu.HBM),) * 2,
        scratch_shapes=scratch,
        input_output_aliases={first + n: 3 + n for n in range(len(so_far))},
        compiler_params=pltpu.CompilerParams(vmem_limit_bytes=VMEM_LIMIT),
        cost_estimate=pl.CostEstimate(
            flops=2 * rows * full * width,
            bytes_accessed=2 * (full * width + 2 * rows * full) + 6 * rows * width,
            transcendentals=0,
        ),
    )(ring, *blocks, w_up_t, gain, *[normed_t] * images, *so_far, *after)


def pair_kernel(
    contract, scale, ranges, member_ref, a_ref, a_other_ref, b_ref, b_other_ref, *refs
):
    arrived, out_ref = refs[: len(ranges)], refs[-1]
    dims = (contract, ((), ()))
    total = lax.dot_general(a_ref[...], b_ref[...], dims, preferred_element_type=jnp.float32)
    total += lax.dot_general(
        a_other_ref[...], b_other_ref[...], dims, preferred_element_type=jnp.float32
    )
    total *= scale
    step = pl.program_id(0)
    for (first, last), ref in zip(ranges, arrived):
        part = ref[...].astype(jnp.float32)
        total += jnp.where((step >= first) & (step < last), part, 0.0)
    out_ref[...] = total.astype(out_ref.dtype)


def pair_product(
    operands, specs, contract, shape, tile, depth, member, scale, arrived, dtype, after
):
    row_spec = lambda first, last: pl.BlockSpec(
        (tile, shape[1]), lambda t, m: (jnp.clip(t - first, 0, last - first - 1), 0)
    )
    steps = shape[0] // tile
    return pl.pallas_call(
        functools.partial(pair_kernel, contract, scale, [span for span, _ in arrived]),
        grid_spec=pltpu.PrefetchScalarGridSpec(
            num_scalar_prefetch=1,
            grid=(steps,),
            in_specs=specs
            + [row_spec(*span) for span, _ in arrived]
            + [pl.BlockSpec(memory_space=pltpu.HBM)] * len(after),
            out_specs=row_spec(0, steps),
        ),
        out_shape=jax.ShapeDtypeStruct(shape, dtype),
        compiler_params=pltpu.CompilerParams(vmem_limit_bytes=VMEM_LIMIT),
        cost_estimate=pl.CostEstimate(
            flops=4 * shape[0] * shape[1] * depth,
            bytes_accessed=4 * depth * (shape[0] + shape[1]) + 4 * shape[0] * shape[1],
            transcendentals=0,
        ),
    )(
        member.reshape(1).astype(jnp.int32),
        *operands,
        *[part for _, part in arrived],
        *after,
    )


def chip_products(product, spans, ctx_count, after):
    index = lax.axis_index("ctx")
    going, arrived = [], []
    for span in spans:
        for shift in range(1, ctx_count // 2):
            member = (index + 2 * shift) % ctx_count
            going.append(product(member, span, [], jnp.bfloat16, after))
            route = [(c, (c + 2 * shift) % ctx_count) for c in range(ctx_count)]
            arrived.append((span, lax.ppermute(going[-1], "ctx", route)))
    return going, arrived


def tie_kernel(*refs):
    del refs


def tie(values, others, place=pl.ANY):
    spaces = [place] + [pl.ANY] * (len(values) + len(others) - 1)
    return pl.pallas_call(
        tie_kernel,
        in_specs=[pl.BlockSpec(memory_space=space) for space in spaces],
        out_specs=[pl.BlockSpec(memory_space=space) for space in spaces[: len(values)]],
        out_shape=[jax.ShapeDtypeStruct(value.shape, value.dtype) for value in values],
        input_output_aliases={n: n for n in range(len(values))},
        compiler_params=pltpu.CompilerParams(vmem_limit_bytes=VMEM_LIMIT),
    )(*values, *others)


def visual_kernel(
    source_ref, present_ref, gained_ref, normed_ref, means_ref, inverse_ref, out_ref
):
    slot = pl.program_id(0)

    @pl.when(present_ref[slot] == 0)
    def _():
        out_ref[...] = jnp.zeros_like(out_ref)

    @pl.when(present_ref[slot] != 0)
    def _():
        gained = gained_ref[...]
        features = normed_ref[...].astype(jnp.float32)
        first, second = means_ref[0:1, :], means_ref[1:2, :]
        out_ref[0] = (inverse_ref[...] * (gained - first - features * second)).astype(
            out_ref.dtype
        )


def visual_slots(source, present, gained_t, normed_t, means, inverse, chunk, part_rows):
    width = gained_t.shape[0]
    slots = source.shape[0]
    picked = lambda s, source, present: (0, source[s])
    natural = lambda s, source, present: (0, source[s] * CHUNKS + chunk)
    return pl.pallas_call(
        visual_kernel,
        grid_spec=pltpu.PrefetchScalarGridSpec(
            num_scalar_prefetch=2,
            grid=(slots,),
            in_specs=[
                pl.BlockSpec((width, part_rows), picked),
                pl.BlockSpec((width, part_rows), natural),
                pl.BlockSpec((2, part_rows), picked),
                pl.BlockSpec((1, part_rows), natural),
            ],
            out_specs=pl.BlockSpec((1, width, part_rows), lambda s, source, present: (s, 0, 0)),
        ),
        out_shape=jax.ShapeDtypeStruct((slots, width, part_rows), jnp.bfloat16),
        compiler_params=pltpu.CompilerParams(vmem_limit_bytes=VMEM_LIMIT),
        cost_estimate=pl.CostEstimate(
            flops=6 * slots * width * part_rows,
            bytes_accessed=8 * slots * width * part_rows,
            transcendentals=0,
        ),
    )(source, present, gained_t, normed_t, means, inverse)


def turn_kernel(in_ref, *refs):
    refs[-1][...] = in_ref[...].T


def turn_rows(received, chunk, rows, so_far, after):
    full, part_rows = received.shape
    tile = divisor(full, 2560, 128)
    operands, aliases = [received], {}
    if so_far is not None:
        operands.append(so_far)
        aliases = {1: 0}
    operands += after
    specs = [pl.BlockSpec((tile, part_rows), lambda t: (t, 0))]
    specs += [pl.BlockSpec(memory_space=pltpu.HBM)] * (len(operands) - 1)
    return pl.pallas_call(
        turn_kernel,
        grid=(full // tile,),
        in_specs=specs,
        out_specs=pl.BlockSpec((part_rows, tile), lambda t: (chunk, t)),
        out_shape=jax.ShapeDtypeStruct((rows, full), received.dtype),
        input_output_aliases=aliases,
        compiler_params=pltpu.CompilerParams(vmem_limit_bytes=VMEM_LIMIT),
        cost_estimate=pl.CostEstimate(
            flops=0, bytes_accessed=4 * part_rows * full, transcendentals=0
        ),
    )(*operands)


def core_swap(value, ctx_count):
    return lax.ppermute(value, "ctx", [(c, c ^ 1) for c in range(ctx_count)])


def doubling_sum(value, axis, count, after=()):
    bit = 1
    while bit < count:
        if after and 2 * bit >= count:
            (value,) = tie([value], after)
        value = value + lax.ppermute(value, axis, [(t, t ^ bit) for t in range(count)])
        bit *= 2
    return value


def per_device(out_grad, pre_act, normed, inverse_std, w_up, w_down, ln_gain, owner_map):
    ctx_count = lax.axis_size("ctx")
    tp_count = lax.axis_size("tp")
    row_count = out_grad.shape[0]
    width = normed.shape[1]
    grad_scale = float(row_count * ctx_count) ** (-0.5)
    full_width = float(width * tp_count)

    owners = owner_map[0]
    image_count = owners.shape[0]
    image_rows = row_count // image_count
    part_rows = image_rows // CHUNKS
    chunk_rows = row_count // CHUNKS
    capacity = max(1, 2 * image_count // tp_count)
    slot_of = slot_numbers(owners, capacity)
    slot_ids = jnp.arange(tp_count * capacity)
    matches = slot_of[None, :] == slot_ids[:, None]
    present = jnp.any(matches, axis=1).astype(jnp.int32)
    source = jnp.sum(jnp.where(matches, jnp.arange(image_count)[None, :], 0), axis=1).astype(
        jnp.int32
    )

    def chunk_of(array, chunk):
        images = array.reshape((image_count, image_rows) + array.shape[1:])
        piece = images[:, chunk * part_rows : (chunk + 1) * part_rows]
        return piece.reshape((chunk_rows,) + array.shape[1:])

    ring = ring_owners(tp_count)
    gelu_value, slope = gelu_parts(pre_act.astype(jnp.float32))
    hidden = gelu_value.astype(jnp.bfloat16)
    hidden_other = core_swap(hidden, ctx_count)
    normed_t = normed.T
    normed_other = core_swap(normed_t, ctx_count)
    gain = ln_gain[:, None]
    w_up_t = w_up.T

    def back_of(chunk, blocks, so_far):
        return back_part(ring, blocks, w_down, slope, chunk, image_rows, ctx_count, so_far)

    first_grads, second_grads = [
        ring_blocks(chunk_of(out_grad, chunk), tp_count) for chunk in range(CHUNKS)
    ]
    first_back, first_sum, *so_far = back_of(0, first_grads, ())
    first_backs = ring_blocks(first_back, tp_count)
    second_back, second_sum, grads, grads_swap = back_of(1, second_grads, so_far)
    second_backs = ring_blocks(second_back, tp_count)
    grads_other = core_swap(grads_swap, ctx_count)
    back_sum = first_sum[0] + second_sum[0]

    def grad_w2_share(member, span, arrived, dtype, after):
        share, local = grads.shape[1] // ctx_count, hidden.shape[1]
        tile = divisor(share, 256, 128)
        steps = share // tile
        return pair_product(
            (grads, grads_other, hidden, hidden_other),
            [
                pl.BlockSpec((row_count, tile), lambda t, m: (0, m[0] * steps + t)),
                pl.BlockSpec((row_count, tile), lambda t, m: (m[0] // 2, t)),
                pl.BlockSpec((row_count, local), lambda t, m: (0, 0)),
                pl.BlockSpec((row_count, local), lambda t, m: (0, 0)),
            ],
            ((0,), (0,)), (share, local), tile, row_count, member, grad_scale, arrived, dtype,
            after,
        )

    w2_span = (0, grads.shape[1] // ctx_count // divisor(grads.shape[1] // ctx_count, 256, 128))
    going_w2, arrived_w2 = chip_products(grad_w2_share, [w2_span], ctx_count, [])
    member = lax.axis_index("ctx")

    def norm_of(chunk, blocks, so_far, after):
        return norm_part(
            ring, blocks, w_up_t, gain, normed_t, chunk, image_rows, ctx_count, so_far, after
        )

    def slots_of(chunk, gained_t, means):
        return visual_slots(
            source, present, gained_t, normed_t, means, inverse_std[None, :], chunk, part_rows
        )

    first_gained, first_rows, first_ln, *so_far = norm_of(0, first_backs, (), [])
    first_means = doubling_sum(first_rows, "tp", tp_count) / full_width
    first_slots, first_means = tie(
        [slots_of(0, first_gained, first_means), first_means], second_backs[-2:], pltpu.HBM
    )
    outgoing = [first_slots]
    second_gained, second_rows, second_ln, backs, backs_swap = norm_of(
        1, second_backs, so_far, [first_means]
    )
    backs_other = core_swap(backs_swap, ctx_count)

    w1_tile = divisor(width, 400, 16)
    w1_tiles = width // w1_tile

    def grad_w1_share(member, span, arrived, dtype, after):
        share = backs.shape[1] // ctx_count
        first, last = span
        return pair_product(
            (normed_t, normed_other, backs, backs_other),
            [
                pl.BlockSpec((w1_tile, row_count), lambda t, m: (first + t, 0)),
                pl.BlockSpec((w1_tile, row_count), lambda t, m: (first + t, 0)),
                pl.BlockSpec((row_count, share), lambda t, m: (0, m[0])),
                pl.BlockSpec((row_count, share), lambda t, m: (m[0] // 2, 0)),
            ],
            ((1,), (0,)), ((last - first) * w1_tile, share), w1_tile, row_count, member,
            grad_scale, arrived, dtype, after,
        )

    cut = w1_tiles // 2
    spans = [(0, cut), (cut, w1_tiles)] if cut else [(0, w1_tiles)]
    going_w1, arrived_w1 = chip_products(grad_w1_share, spans, ctx_count, [])

    second_means = doubling_sum(second_rows, "tp", tp_count, going_w1) / full_width
    early = [part for span, part in arrived_w1 if span == spans[0]]
    outgoing += tie([slots_of(1, second_gained, second_means)], early, pltpu.HBM)
    received = [
        lax.all_to_all(part, "tp", split_axis=0, concat_axis=0, tiled=True) for part in outgoing
    ]
    ln_sum = (first_ln + second_ln)[:, :2]
    small = jnp.concatenate(
        [jnp.sum(out_grad.astype(jnp.float32), axis=0), back_sum, ln_sum.T.reshape(-1)]
    )
    (small,) = tie([small], [part for _, part in arrived_w1])
    grad_w2 = grad_w2_share(member, w2_span, arrived_w2, jnp.float32, [small])
    small = doubling_sum(small, "ctx", ctx_count) * grad_scale
    grad_w1_t = grad_w1_share(member, (0, w1_tiles), arrived_w1, jnp.float32, [])
    assert capacity == 1
    vit_grad = None
    for chunk in range(CHUNKS):
        columns = received[chunk].reshape(tp_count * width, part_rows)
        after = [grad_w1_t, grad_w2] if chunk + 1 == CHUNKS else []
        vit_grad = turn_rows(columns, chunk, image_rows, vit_grad, after)

    features_in = out_grad.shape[1]
    hidden_in = pre_act.shape[1]
    bias_down = small[:features_in]
    bias_up = small[features_in : features_in + hidden_in]
    ln_grads = small[features_in + hidden_in :].reshape(2, width)
    return (grad_w2, grad_w1_t.T, bias_up, bias_down, ln_grads, vit_grad)


def solution(mesh):
    return jax.shard_map(
        per_device,
        mesh=mesh,
        in_specs=(
            P("ctx", "tp"),
            P("ctx", "tp"),
            P("ctx", "tp"),
            P("ctx"),
            P(None, "tp"),
            P(None, "tp"),
            P("tp"),
            P("ctx", None),
        ),
        out_specs=(
            P("ctx", "tp"),
            P("ctx", "tp"),
            P("tp"),
            P("tp"),
            P(None, "tp"),
            P(("ctx", "tp"), None),
        ),
        check_vma=False,
    )
```

```python
import functools
import math

import jax
import jax.numpy as jnp
from jax import lax
from jax.experimental import pallas as pl
from jax.experimental.pallas import tpu as pltpu
from jax.sharding import PartitionSpec as P

CHUNKS = 2
VMEM_LIMIT = 48 * 1024 * 1024


def gelu_parts(linear):
    normal_cdf = 0.5 * (1.0 + jax.scipy.special.erf(linear * 2.0 ** (-0.5)))
    density = jnp.exp(-0.5 * linear * linear) * (2.0 * math.pi) ** (-0.5)
    return (linear * normal_cdf, normal_cdf + linear * density)


def slot_numbers(owners, capacity):
    position = jnp.arange(owners.shape[0])
    earlier = (owners[None, :] == owners[:, None]) & (position[None, :] < position[:, None])
    return owners * capacity + jnp.sum(earlier.astype(jnp.int32), axis=1)


def divisor(extent, most, unit):
    return max(d for d in range(unit, most + 1, unit) if extent % d == 0)


def ring_order(count):
    depth = 4 if count % 4 == 0 else count
    width = count // depth
    walk = [(z, 0) for z in range(depth)]
    if width > 1:
        for turn, z in enumerate(reversed(range(depth))):
            ys = list(range(1, width))
            walk += [(z, y) for y in (ys if turn % 2 == 0 else ys[::-1])]
    return [z * width + y for z, y in walk]


def ring_owners(count):
    order = ring_order(count)
    table = []
    for j in range(count):
        at = order.index(j)
        steps = [0]
        for step in range(1, count // 2):
            steps += [-step, step]
        steps += [count // 2]
        table.append([order[(at + s) % count] for s in steps])
    core = (lax.axis_index("ctx") % 2).astype(jnp.int32)
    return jnp.concatenate([jnp.array(table, jnp.int32)[lax.axis_index("tp")], core[None]])


def ring_blocks(block, count):
    order = ring_order(count)
    ahead = [(order[p], order[(p + 1) % count]) for p in range(count)]
    behind = [(order[p], order[(p - 1) % count]) for p in range(count)]
    up, down = block, block
    blocks = [block]
    for _ in range(1, count // 2):
        up = lax.ppermute(up, "tp", ahead)
        down = lax.ppermute(down, "tp", behind)
        blocks += [up, down]
    half = block.shape[0] // 2
    blocks.append(lax.ppermute(up[:half], "tp", ahead))
    blocks.append(lax.ppermute(down[half:], "tp", behind))
    return blocks


def assemble(owners_ref, block_refs, held, sems):
    rows, width = block_refs[0].shape
    half = rows // 2
    last = len(block_refs) - 2
    copies = []
    for k, ref in enumerate(block_refs):
        columns = pl.ds(pl.multiple_of(owners_ref[min(k, last)] * width, width), width)
        if k < last:
            target = held.at[:, columns]
        else:
            target = held.at[pl.ds((k - last) * half, half), columns]
        copies.append(pltpu.make_async_copy(ref, target, sems.at[k]))
    return copies


def spread(ring_ref, held, full_ref, swap_ref, chunk, image_rows, sems):
    rows, part_rows = held.shape[0], image_rows // CHUNKS
    all_rows, member_width = full_ref.shape[0], swap_ref.shape[1]
    other = 1 - ring_ref[ring_ref.shape[0] - 1]
    copies = []
    for i in range(rows // part_rows):
        source = pl.ds(i * part_rows, part_rows)
        place = i * image_rows + chunk * part_rows
        copies.append((held.at[source, :], full_ref.at[pl.ds(place, part_rows), :]))
        for chip in range(swap_ref.shape[0] // all_rows):
            columns = pl.ds(
                pl.multiple_of((2 * chip + other) * member_width, member_width), member_width
            )
            target = swap_ref.at[pl.ds(chip * all_rows + place, part_rows), :]
            copies.append((held.at[source, columns], target))
    return [
        pltpu.make_async_copy(source, target, sems.at[n])
        for n, (source, target) in enumerate(copies)
    ]


def spread_shapes(rows, chunk_rows, full, ctx_count, images):
    shapes = (
        jax.ShapeDtypeStruct((rows, full), jnp.bfloat16),
        jax.ShapeDtypeStruct((rows * (ctx_count // 2), full // ctx_count), jnp.bfloat16),
    )
    scratch = [
        pltpu.VMEM((chunk_rows, full), jnp.bfloat16),
        pltpu.SemaphoreType.DMA((2 * tp_most(),)),
        pltpu.SemaphoreType.DMA((images * (1 + ctx_count // 2),)),
    ]
    return shapes, scratch


def tp_most():
    return lax.axis_size("tp")


def back_kernel(chunk, image_rows, blocks, carried, ring_ref, *refs):
    block_refs, refs = refs[:blocks], refs[blocks:]
    w_ref, slope_ref, *refs = refs
    back_ref, sum_ref, full_ref, swap_ref, held, sems, out_sems = refs[carried:]
    copies = assemble(ring_ref, block_refs, held, sems)
    for copy in copies:
        copy.start()
    for copy in copies:
        copy.wait()
    outs = spread(ring_ref, held, full_ref, swap_ref, chunk, image_rows, out_sems)
    for copy in outs:
        copy.start()
    rows, part_rows = held.shape[0], image_rows // CHUNKS
    tile = divisor(rows, 256, part_rows)
    sums = jnp.zeros(sum_ref.shape, jnp.float32)
    for start in range(0, rows, tile):
        total = jnp.dot(
            held[start : start + tile, :], w_ref[...], preferred_element_type=jnp.float32
        )
        for n in range(tile // part_rows):
            image = start // part_rows + n
            place = image * image_rows + chunk * part_rows
            part = (
                total[n * part_rows : (n + 1) * part_rows]
                * slope_ref[place : place + part_rows, :]
            ).astype(back_ref.dtype)
            back_ref[image * part_rows : (image + 1) * part_rows, :] = part
            sums += jnp.sum(part.astype(jnp.float32), axis=0, keepdims=True)
    sum_ref[...] = sums
    for copy in outs:
        copy.wait()


def back_part(ring, blocks, w_down, slope, chunk, image_rows, ctx_count, so_far):
    rows = blocks[0].shape[0]
    full, width = w_down.shape
    images = slope.shape[0] // image_rows
    shapes, scratch = spread_shapes(slope.shape[0], rows, full, ctx_count, images)
    first = 1 + len(blocks) + 2
    return pl.pallas_call(
        functools.partial(back_kernel, chunk, image_rows, len(blocks), len(so_far)),
        out_shape=(
            jax.ShapeDtypeStruct((rows, width), jnp.bfloat16),
            jax.ShapeDtypeStruct((1, width), jnp.float32),
        )
        + shapes,
        in_specs=[pl.BlockSpec(memory_space=pltpu.SMEM)]
        + [pl.BlockSpec(memory_space=pl.ANY)] * len(blocks)
        + [pl.BlockSpec(memory_space=pltpu.VMEM)] * 2
        + [pl.BlockSpec(memory_space=pltpu.HBM)] * len(so_far),
        out_specs=(pl.BlockSpec(memory_space=pltpu.VMEM),) * 2
        + (pl.BlockSpec(memory_space=pltpu.HBM),) * 2,
        scratch_shapes=scratch,
        input_output_aliases={first + n: 2 + n for n in range(len(so_far))},
        compiler_params=pltpu.CompilerParams(vmem_limit_bytes=VMEM_LIMIT),
        cost_estimate=pl.CostEstimate(
            flops=2 * rows * full * width,
            bytes_accessed=2 * (2 * rows * full + full * width),
            transcendentals=0,
        ),
    )(ring, *blocks, w_down, slope, *so_far)


def norm_kernel(chunk, image_rows, blocks, images, carried, ring_ref, *refs):
    block_refs, refs = refs[:blocks], refs[blocks:]
    w_ref, gain_ref, *refs = refs
    normed_refs, refs = refs[:images], refs[images:]
    gained_ref, sums_ref, ln_ref, full_ref, swap_ref, held, sems, out_sems = refs[carried:]
    step = pl.program_id(0)
    outs = spread(ring_ref, held, full_ref, swap_ref, chunk, image_rows, out_sems)

    @pl.when(step == 0)
    def _():
        copies = assemble(ring_ref, block_refs, held, sems)
        for copy in copies:
            copy.start()
        for copy in copies:
            copy.wait()
        for copy in outs:
            copy.start()
        sums_ref[...] = jnp.zeros_like(sums_ref)

    grad = lax.dot_general(
        w_ref[...], held[...], (((1,), (1,)), ((), ())), preferred_element_type=jnp.float32
    )
    features = jnp.concatenate([ref[...] for ref in normed_refs], axis=1).astype(jnp.float32)
    gained = gain_ref[...] * grad
    gained_ref[...] = gained
    sums_ref[0:1, :] += jnp.sum(gained, axis=0, keepdims=True)
    sums_ref[1:2, :] += jnp.sum(gained * features, axis=0, keepdims=True)
    gains = jnp.sum(grad * features, axis=1, keepdims=True)
    biases = jnp.sum(grad, axis=1, keepdims=True)
    lane = lax.broadcasted_iota(jnp.int32, ln_ref.shape, 1)
    ln_ref[...] = jnp.where(lane == 0, gains, biases)

    @pl.when(step == pl.num_programs(0) - 1)
    def _():
        for copy in outs:
            copy.wait()


def norm_part(ring, blocks, w_up_t, gain, normed_t, chunk, image_rows, ctx_count, so_far, after):
    rows = blocks[0].shape[0]
    width, full = w_up_t.shape
    part_rows = image_rows // CHUNKS
    images = rows // part_rows
    tile = divisor(width, 400, 16)
    shapes, scratch = spread_shapes(normed_t.shape[1], rows, full, ctx_count, images)
    first = 1 + len(blocks) + 2 + images
    return pl.pallas_call(
        functools.partial(
            norm_kernel, chunk, image_rows, len(blocks), images, len(so_far) + len(after)
        ),
        grid=(width // tile,),
        out_shape=(
            jax.ShapeDtypeStruct((width, rows), jnp.float32),
            jax.ShapeDtypeStruct((2, rows), jnp.float32),
            jax.ShapeDtypeStruct((width, 128), jnp.float32),
        )
        + shapes,
        in_specs=[pl.BlockSpec(memory_space=pltpu.SMEM)]
        + [pl.BlockSpec(memory_space=pl.ANY)] * len(blocks)
        + [
            pl.BlockSpec((tile, full), lambda t: (t, 0)),
            pl.BlockSpec((tile, 1), lambda t: (t, 0)),
        ]
        + [
            pl.BlockSpec((tile, part_rows), lambda t, i=i: (t, i * CHUNKS + chunk))
            for i in range(images)
        ]
        + [pl.BlockSpec(memory_space=pltpu.HBM)] * (len(so_far) + len(after)),
        out_specs=(
            pl.BlockSpec((tile, rows), lambda t: (t, 0)),
            pl.BlockSpec((2, rows), lambda t: (0, 0)),
            pl.BlockSpec((tile, 128), lambda t: (t, 0)),
        )
        + (pl.BlockSpec(memory_space=pltpu.HBM),) * 2,
        scratch_shapes=scratch,
        input_output_aliases={first + n: 3 + n for n in range(len(so_far))},
        compiler_params=pltpu.CompilerParams(vmem_limit_bytes=VMEM_LIMIT),
        cost_estimate=pl.CostEstimate(
            flops=2 * rows * full * width,
            bytes_accessed=2 * (full * width + 2 * rows * full) + 6 * rows * width,
            transcendentals=0,
        ),
    )(ring, *blocks, w_up_t, gain, *[normed_t] * images, *so_far, *after)


def pair_kernel(
    contract, scale, ranges, member_ref, a_ref, a_other_ref, b_ref, b_other_ref, *refs
):
    arrived, out_ref = refs[: len(ranges)], refs[-1]
    dims = (contract, ((), ()))
    total = lax.dot_general(a_ref[...], b_ref[...], dims, preferred_element_type=jnp.float32)
    total += lax.dot_general(
        a_other_ref[...], b_other_ref[...], dims, preferred_element_type=jnp.float32
    )
    total *= scale
    step = pl.program_id(0)
    for (first, last), ref in zip(ranges, arrived):
        part = ref[...].astype(jnp.float32)
        total += jnp.where((step >= first) & (step < last), part, 0.0)
    out_ref[...] = total.astype(out_ref.dtype)


def pair_product(
    operands, specs, contract, shape, tile, depth, member, scale, arrived, dtype, after
):
    row_spec = lambda first, last: pl.BlockSpec(
        (tile, shape[1]), lambda t, m: (jnp.clip(t - first, 0, last - first - 1), 0)
    )
    steps = shape[0] // tile
    return pl.pallas_call(
        functools.partial(pair_kernel, contract, scale, [span for span, _ in arrived]),
        grid_spec=pltpu.PrefetchScalarGridSpec(
            num_scalar_prefetch=1,
            grid=(steps,),
            in_specs=specs
            + [row_spec(*span) for span, _ in arrived]
            + [pl.BlockSpec(memory_space=pltpu.HBM)] * len(after),
            out_specs=row_spec(0, steps),
        ),
        out_shape=jax.ShapeDtypeStruct(shape, dtype),
        compiler_params=pltpu.CompilerParams(vmem_limit_bytes=VMEM_LIMIT),
        cost_estimate=pl.CostEstimate(
            flops=shape[0] * shape[1] * depth // 4,
            bytes_accessed=depth * (shape[0] + shape[1]) // 4,
            transcendentals=0,
        ),
    )(
        member.reshape(1).astype(jnp.int32),
        *operands,
        *[part for _, part in arrived],
        *after,
    )


def chip_products(product, spans, ctx_count, after):
    index = lax.axis_index("ctx")
    going, arrived = [], []
    for span in spans:
        for shift in range(1, ctx_count // 2):
            member = (index + 2 * shift) % ctx_count
            going.append(product(member, span, [], jnp.bfloat16, after))
            route = [(c, (c + 2 * shift) % ctx_count) for c in range(ctx_count)]
            arrived.append((span, lax.ppermute(going[-1], "ctx", route)))
    return going, arrived


def tie_kernel(*refs):
    del refs


def tie(values, others, place=pl.ANY):
    spaces = [place] + [pl.ANY] * (len(values) - 1) + [place] * len(others)
    return pl.pallas_call(
        tie_kernel,
        in_specs=[pl.BlockSpec(memory_space=space) for space in spaces],
        out_specs=[pl.BlockSpec(memory_space=space) for space in spaces[: len(values)]],
        out_shape=[jax.ShapeDtypeStruct(value.shape, value.dtype) for value in values],
        input_output_aliases={n: n for n in range(len(values))},
        compiler_params=pltpu.CompilerParams(vmem_limit_bytes=VMEM_LIMIT),
    )(*values, *others)


def visual_kernel(
    source_ref, present_ref, gained_ref, normed_ref, means_ref, inverse_ref, out_ref
):
    slot = pl.program_id(0)

    @pl.when(present_ref[slot] == 0)
    def _():
        out_ref[...] = jnp.zeros_like(out_ref)

    @pl.when(present_ref[slot] != 0)
    def _():
        gained = gained_ref[...]
        features = normed_ref[...].astype(jnp.float32)
        first, second = means_ref[0:1, :], means_ref[1:2, :]
        out_ref[0] = (inverse_ref[...] * (gained - first - features * second)).astype(
            out_ref.dtype
        )


def visual_slots(source, present, gained_t, normed_t, means, inverse, chunk, part_rows):
    width = gained_t.shape[0]
    slots = source.shape[0]
    picked = lambda s, source, present: (0, source[s])
    natural = lambda s, source, present: (0, source[s] * CHUNKS + chunk)
    return pl.pallas_call(
        visual_kernel,
        grid_spec=pltpu.PrefetchScalarGridSpec(
            num_scalar_prefetch=2,
            grid=(slots,),
            in_specs=[
                pl.BlockSpec((width, part_rows), picked),
                pl.BlockSpec((width, part_rows), natural),
                pl.BlockSpec((2, part_rows), picked),
                pl.BlockSpec((1, part_rows), natural),
            ],
            out_specs=pl.BlockSpec((1, width, part_rows), lambda s, source, present: (s, 0, 0)),
        ),
        out_shape=jax.ShapeDtypeStruct((slots, width, part_rows), jnp.bfloat16),
        compiler_params=pltpu.CompilerParams(vmem_limit_bytes=VMEM_LIMIT),
        cost_estimate=pl.CostEstimate(
            flops=6 * slots * width * part_rows,
            bytes_accessed=8 * slots * width * part_rows,
            transcendentals=0,
        ),
    )(source, present, gained_t, normed_t, means, inverse)


def turn_kernel(in_ref, *refs):
    refs[-1][...] = in_ref[...].T


def turn_rows(received, chunk, rows, so_far, after):
    full, part_rows = received.shape
    tile = divisor(full, 2560, 128)
    operands, aliases = [received], {}
    if so_far is not None:
        operands.append(so_far)
        aliases = {1: 0}
    operands += after
    specs = [pl.BlockSpec((tile, part_rows), lambda t: (t, 0))]
    specs += [pl.BlockSpec(memory_space=pltpu.HBM)] * (len(operands) - 1)
    return pl.pallas_call(
        turn_kernel,
        grid=(full // tile,),
        in_specs=specs,
        out_specs=pl.BlockSpec((part_rows, tile), lambda t: (chunk, t)),
        out_shape=jax.ShapeDtypeStruct((rows, full), received.dtype),
        input_output_aliases=aliases,
        compiler_params=pltpu.CompilerParams(vmem_limit_bytes=VMEM_LIMIT),
        cost_estimate=pl.CostEstimate(
            flops=0, bytes_accessed=4 * part_rows * full, transcendentals=0
        ),
    )(*operands)


def core_swap(value, ctx_count):
    return lax.ppermute(value, "ctx", [(c, c ^ 1) for c in range(ctx_count)])


def doubling_sum(value, axis, count, after=()):
    bit = 1
    while bit < count:
        if after and 2 * bit >= count:
            (value,) = tie([value], after)
        value = value + lax.ppermute(value, axis, [(t, t ^ bit) for t in range(count)])
        bit *= 2
    return value


def per_device(out_grad, pre_act, normed, inverse_std, w_up, w_down, ln_gain, owner_map):
    ctx_count = lax.axis_size("ctx")
    tp_count = lax.axis_size("tp")
    row_count = out_grad.shape[0]
    width = normed.shape[1]
    grad_scale = float(row_count * ctx_count) ** (-0.5)
    full_width = float(width * tp_count)

    owners = owner_map[0]
    image_count = owners.shape[0]
    image_rows = row_count // image_count
    part_rows = image_rows // CHUNKS
    chunk_rows = row_count // CHUNKS
    capacity = max(1, 2 * image_count // tp_count)
    slot_of = slot_numbers(owners, capacity)
    slot_ids = jnp.arange(tp_count * capacity)
    matches = slot_of[None, :] == slot_ids[:, None]
    present = jnp.any(matches, axis=1).astype(jnp.int32)
    source = jnp.sum(jnp.where(matches, jnp.arange(image_count)[None, :], 0), axis=1).astype(
        jnp.int32
    )

    def chunk_of(array, chunk):
        images = array.reshape((image_count, image_rows) + array.shape[1:])
        piece = images[:, chunk * part_rows : (chunk + 1) * part_rows]
        return piece.reshape((chunk_rows,) + array.shape[1:])

    ring = ring_owners(tp_count)
    gelu_value, slope = gelu_parts(pre_act.astype(jnp.float32))
    hidden = gelu_value.astype(jnp.bfloat16)
    hidden_other = core_swap(hidden, ctx_count)
    normed_t = normed.T
    normed_other = core_swap(normed_t, ctx_count)
    gain = ln_gain[:, None]
    w_up_t = w_up.T

    def back_of(chunk, blocks, so_far):
        return back_part(ring, blocks, w_down, slope, chunk, image_rows, ctx_count, so_far)

    first_grads, second_grads = [
        ring_blocks(chunk_of(out_grad, chunk), tp_count) for chunk in range(CHUNKS)
    ]
    first_back, first_sum, *so_far = back_of(0, first_grads, ())
    first_backs = ring_blocks(first_back, tp_count)
    second_back, second_sum, grads, grads_swap = back_of(1, second_grads, so_far)
    second_backs = ring_blocks(second_back, tp_count)
    grads_other = core_swap(grads_swap, ctx_count)
    back_sum = first_sum[0] + second_sum[0]

    def grad_w2_share(member, span, arrived, dtype, after):
        share, local = grads.shape[1] // ctx_count, hidden.shape[1]
        tile = divisor(share, 256, 128)
        steps = share // tile
        return pair_product(
            (grads, grads_other, hidden, hidden_other),
            [
                pl.BlockSpec((row_count, tile), lambda t, m: (0, m[0] * steps + t)),
                pl.BlockSpec((row_count, tile), lambda t, m: (m[0] // 2, t)),
                pl.BlockSpec((row_count, local), lambda t, m: (0, 0)),
                pl.BlockSpec((row_count, local), lambda t, m: (0, 0)),
            ],
            ((0,), (0,)), (share, local), tile, row_count, member, grad_scale, arrived, dtype,
            after,
        )

    w2_span = (0, grads.shape[1] // ctx_count // divisor(grads.shape[1] // ctx_count, 256, 128))
    going_w2, arrived_w2 = chip_products(grad_w2_share, [w2_span], ctx_count, [])
    member = lax.axis_index("ctx")

    def norm_of(chunk, blocks, so_far, after):
        return norm_part(
            ring, blocks, w_up_t, gain, normed_t, chunk, image_rows, ctx_count, so_far, after
        )

    def slots_of(chunk, gained_t, means):
        return visual_slots(
            source, present, gained_t, normed_t, means, inverse_std[None, :], chunk, part_rows
        )

    first_gained, first_rows, first_ln, *so_far = norm_of(0, first_backs, (), [])
    first_means = doubling_sum(first_rows, "tp", tp_count) / full_width
    second_gained, second_rows, second_ln, backs, backs_swap = norm_of(
        1, second_backs, so_far, [first_means]
    )
    second_means = doubling_sum(second_rows, "tp", tp_count) / full_width
    first_slots, second_means = tie(
        [slots_of(0, first_gained, first_means), second_means], [], pltpu.HBM
    )
    first_received = lax.all_to_all(first_slots, "tp", split_axis=0, concat_axis=0, tiled=True)
    backs_other = core_swap(backs_swap, ctx_count)

    w1_tile = divisor(width, 400, 16)
    w1_tiles = width // w1_tile

    def grad_w1_share(member, span, arrived, dtype, after):
        share = backs.shape[1] // ctx_count
        first, last = span
        return pair_product(
            (normed_t, normed_other, backs, backs_other),
            [
                pl.BlockSpec((w1_tile, row_count), lambda t, m: (first + t, 0)),
                pl.BlockSpec((w1_tile, row_count), lambda t, m: (first + t, 0)),
                pl.BlockSpec((row_count, share), lambda t, m: (0, m[0])),
                pl.BlockSpec((row_count, share), lambda t, m: (m[0] // 2, 0)),
            ],
            ((1,), (0,)), ((last - first) * w1_tile, share), w1_tile, row_count, member,
            grad_scale, arrived, dtype, after,
        )

    cut = w1_tiles // 2
    spans = [(0, cut), (cut, w1_tiles)] if cut else [(0, w1_tiles)]
    _, arrived_w1 = chip_products(grad_w1_share, spans, ctx_count, [second_means])

    early = [part for span, part in arrived_w1 if span == spans[0]]
    (second_slots,) = tie(
        [slots_of(1, second_gained, second_means)], early + [first_received], pltpu.HBM
    )
    received = [
        first_received,
        lax.all_to_all(second_slots, "tp", split_axis=0, concat_axis=0, tiled=True),
    ]
    ln_sum = (first_ln + second_ln)[:, :2]
    small = jnp.concatenate(
        [jnp.sum(out_grad.astype(jnp.float32), axis=0), back_sum, ln_sum.T.reshape(-1)]
    )
    (small,) = tie([small], [part for _, part in arrived_w1])
    grad_w2 = grad_w2_share(member, w2_span, arrived_w2, jnp.float32, [small])
    small = doubling_sum(small, "ctx", ctx_count) * grad_scale
    grad_w1_t = grad_w1_share(member, (0, w1_tiles), arrived_w1, jnp.float32, [])
    assert capacity == 1
    vit_grad = None
    for chunk in range(CHUNKS):
        columns = received[chunk].reshape(tp_count * width, part_rows)
        after = [grad_w1_t, grad_w2] if chunk + 1 == CHUNKS else []
        vit_grad = turn_rows(columns, chunk, image_rows, vit_grad, after)

    features_in = out_grad.shape[1]
    hidden_in = pre_act.shape[1]
    bias_down = small[:features_in]
    bias_up = small[features_in : features_in + hidden_in]
    ln_grads = small[features_in + hidden_in :].reshape(2, width)
    return (grad_w2, grad_w1_t.T, bias_up, bias_down, ln_grads, vit_grad)


def solution(mesh):
    return jax.shard_map(
        per_device,
        mesh=mesh,
        in_specs=(
            P("ctx", "tp"),
            P("ctx", "tp"),
            P("ctx", "tp"),
            P("ctx"),
            P(None, "tp"),
            P(None, "tp"),
            P("tp"),
            P("ctx", None),
        ),
        out_specs=(
            P("ctx", "tp"),
            P("ctx", "tp"),
            P("tp"),
            P("tp"),
            P(None, "tp"),
            P(("ctx", "tp"), None),
        ),
        check_vma=False,
    )
```

```python
import functools
import math

import jax
import jax.numpy as jnp
from jax import lax
from jax.experimental import pallas as pl
from jax.experimental.pallas import tpu as pltpu
from jax.sharding import PartitionSpec as P

CHUNKS = 2
VMEM_LIMIT = 48 * 1024 * 1024


def gelu_parts(linear):
    normal_cdf = 0.5 * (1.0 + jax.scipy.special.erf(linear * 2.0 ** (-0.5)))
    density = jnp.exp(-0.5 * linear * linear) * (2.0 * math.pi) ** (-0.5)
    return (linear * normal_cdf, normal_cdf + linear * density)


def slot_numbers(owners, capacity):
    position = jnp.arange(owners.shape[0])
    earlier = (owners[None, :] == owners[:, None]) & (position[None, :] < position[:, None])
    return owners * capacity + jnp.sum(earlier.astype(jnp.int32), axis=1)


def divisor(extent, most, unit):
    return max(d for d in range(unit, most + 1, unit) if extent % d == 0)


def ring_order(count):
    depth = 4 if count % 4 == 0 else count
    width = count // depth
    walk = [(z, 0) for z in range(depth)]
    if width > 1:
        for turn, z in enumerate(reversed(range(depth))):
            ys = list(range(1, width))
            walk += [(z, y) for y in (ys if turn % 2 == 0 else ys[::-1])]
    return [z * width + y for z, y in walk]


def ring_owners(count):
    order = ring_order(count)
    table = []
    for j in range(count):
        at = order.index(j)
        steps = [0]
        for step in range(1, count // 2):
            steps += [-step, step]
        steps += [count // 2]
        table.append([order[(at + s) % count] for s in steps])
    core = (lax.axis_index("ctx") % 2).astype(jnp.int32)
    return jnp.concatenate([jnp.array(table, jnp.int32)[lax.axis_index("tp")], core[None]])


def ring_blocks(block, count):
    order = ring_order(count)
    ahead = [(order[p], order[(p + 1) % count]) for p in range(count)]
    behind = [(order[p], order[(p - 1) % count]) for p in range(count)]
    up, down = block, block
    blocks = [block]
    for _ in range(1, count // 2):
        up = lax.ppermute(up, "tp", ahead)
        down = lax.ppermute(down, "tp", behind)
        blocks += [up, down]
    half = block.shape[0] // 2
    blocks.append(lax.ppermute(up[:half], "tp", ahead))
    blocks.append(lax.ppermute(down[half:], "tp", behind))
    return blocks


def assemble(owners_ref, block_refs, held, sems):
    rows, width = block_refs[0].shape
    half = rows // 2
    last = len(block_refs) - 2
    copies = []
    for k, ref in enumerate(block_refs):
        columns = pl.ds(pl.multiple_of(owners_ref[min(k, last)] * width, width), width)
        if k < last:
            target = held.at[:, columns]
        else:
            target = held.at[pl.ds((k - last) * half, half), columns]
        copies.append(pltpu.make_async_copy(ref, target, sems.at[k]))
    return copies


def spread(ring_ref, held, full_ref, swap_ref, chunk, image_rows, sems):
    rows, part_rows = held.shape[0], image_rows // CHUNKS
    all_rows, member_width = full_ref.shape[0], swap_ref.shape[1]
    other = 1 - ring_ref[ring_ref.shape[0] - 1]
    copies = []
    for i in range(rows // part_rows):
        source = pl.ds(i * part_rows, part_rows)
        place = i * image_rows + chunk * part_rows
        copies.append((held.at[source, :], full_ref.at[pl.ds(place, part_rows), :]))
        for chip in range(swap_ref.shape[0] // all_rows):
            columns = pl.ds(
                pl.multiple_of((2 * chip + other) * member_width, member_width), member_width
            )
            target = swap_ref.at[pl.ds(chip * all_rows + place, part_rows), :]
            copies.append((held.at[source, columns], target))
    return [
        pltpu.make_async_copy(source, target, sems.at[n])
        for n, (source, target) in enumerate(copies)
    ]


def spread_shapes(rows, chunk_rows, full, ctx_count, images):
    shapes = (
        jax.ShapeDtypeStruct((rows, full), jnp.bfloat16),
        jax.ShapeDtypeStruct((rows * (ctx_count // 2), full // ctx_count), jnp.bfloat16),
    )
    scratch = [
        pltpu.VMEM((chunk_rows, full), jnp.bfloat16),
        pltpu.SemaphoreType.DMA((2 * tp_most(),)),
        pltpu.SemaphoreType.DMA((images * (1 + ctx_count // 2),)),
    ]
    return shapes, scratch


def tp_most():
    return lax.axis_size("tp")


def back_kernel(chunk, image_rows, blocks, carried, ring_ref, *refs):
    block_refs, refs = refs[:blocks], refs[blocks:]
    w_ref, slope_ref, *refs = refs
    back_ref, sum_ref, full_ref, swap_ref, held, sems, out_sems = refs[carried:]
    copies = assemble(ring_ref, block_refs, held, sems)
    for copy in copies:
        copy.start()
    for copy in copies:
        copy.wait()
    outs = spread(ring_ref, held, full_ref, swap_ref, chunk, image_rows, out_sems)
    for copy in outs:
        copy.start()
    rows, part_rows = held.shape[0], image_rows // CHUNKS
    tile = divisor(rows, 256, part_rows)
    sums = jnp.zeros(sum_ref.shape, jnp.float32)
    for start in range(0, rows, tile):
        total = jnp.dot(
            held[start : start + tile, :], w_ref[...], preferred_element_type=jnp.float32
        )
        for n in range(tile // part_rows):
            image = start // part_rows + n
            place = image * image_rows + chunk * part_rows
            part = (
                total[n * part_rows : (n + 1) * part_rows]
                * slope_ref[place : place + part_rows, :]
            ).astype(back_ref.dtype)
            back_ref[image * part_rows : (image + 1) * part_rows, :] = part
            sums += jnp.sum(part.astype(jnp.float32), axis=0, keepdims=True)
    sum_ref[...] = sums
    for copy in outs:
        copy.wait()


def back_part(ring, blocks, w_down, slope, chunk, image_rows, ctx_count, so_far):
    rows = blocks[0].shape[0]
    full, width = w_down.shape
    images = slope.shape[0] // image_rows
    shapes, scratch = spread_shapes(slope.shape[0], rows, full, ctx_count, images)
    first = 1 + len(blocks) + 2
    return pl.pallas_call(
        functools.partial(back_kernel, chunk, image_rows, len(blocks), len(so_far)),
        out_shape=(
            jax.ShapeDtypeStruct((rows, width), jnp.bfloat16),
            jax.ShapeDtypeStruct((1, width), jnp.float32),
        )
        + shapes,
        in_specs=[pl.BlockSpec(memory_space=pltpu.SMEM)]
        + [pl.BlockSpec(memory_space=pl.ANY)] * len(blocks)
        + [pl.BlockSpec(memory_space=pltpu.VMEM)] * 2
        + [pl.BlockSpec(memory_space=pltpu.HBM)] * len(so_far),
        out_specs=(pl.BlockSpec(memory_space=pltpu.VMEM),) * 2
        + (pl.BlockSpec(memory_space=pltpu.HBM),) * 2,
        scratch_shapes=scratch,
        input_output_aliases={first + n: 2 + n for n in range(len(so_far))},
        compiler_params=pltpu.CompilerParams(vmem_limit_bytes=VMEM_LIMIT),
        cost_estimate=pl.CostEstimate(
            flops=2 * rows * full * width,
            bytes_accessed=2 * (2 * rows * full + full * width),
            transcendentals=0,
        ),
    )(ring, *blocks, w_down, slope, *so_far)


def norm_kernel(chunk, image_rows, blocks, images, carried, ring_ref, *refs):
    block_refs, refs = refs[:blocks], refs[blocks:]
    w_ref, gain_ref, *refs = refs
    normed_refs, refs = refs[:images], refs[images:]
    gained_ref, sums_ref, ln_ref, full_ref, swap_ref, held, sems, out_sems = refs[carried:]
    step = pl.program_id(0)
    outs = spread(ring_ref, held, full_ref, swap_ref, chunk, image_rows, out_sems)

    @pl.when(step == 0)
    def _():
        copies = assemble(ring_ref, block_refs, held, sems)
        for copy in copies:
            copy.start()
        for copy in copies:
            copy.wait()
        for copy in outs:
            copy.start()
        sums_ref[...] = jnp.zeros_like(sums_ref)

    grad = lax.dot_general(
        w_ref[...], held[...], (((1,), (1,)), ((), ())), preferred_element_type=jnp.float32
    )
    features = jnp.concatenate([ref[...] for ref in normed_refs], axis=1).astype(jnp.float32)
    gained = gain_ref[...] * grad
    gained_ref[...] = gained
    sums_ref[0:1, :] += jnp.sum(gained, axis=0, keepdims=True)
    sums_ref[1:2, :] += jnp.sum(gained * features, axis=0, keepdims=True)
    gains = jnp.sum(grad * features, axis=1, keepdims=True)
    biases = jnp.sum(grad, axis=1, keepdims=True)
    lane = lax.broadcasted_iota(jnp.int32, ln_ref.shape, 1)
    ln_ref[...] = jnp.where(lane == 0, gains, biases)

    @pl.when(step == pl.num_programs(0) - 1)
    def _():
        for copy in outs:
            copy.wait()


def norm_part(ring, blocks, w_up_t, gain, normed_t, chunk, image_rows, ctx_count, so_far, after):
    rows = blocks[0].shape[0]
    width, full = w_up_t.shape
    part_rows = image_rows // CHUNKS
    images = rows // part_rows
    tile = divisor(width, 400, 16)
    shapes, scratch = spread_shapes(normed_t.shape[1], rows, full, ctx_count, images)
    first = 1 + len(blocks) + 2 + images
    return pl.pallas_call(
        functools.partial(
            norm_kernel, chunk, image_rows, len(blocks), images, len(so_far) + len(after)
        ),
        grid=(width // tile,),
        out_shape=(
            jax.ShapeDtypeStruct((width, rows), jnp.float32),
            jax.ShapeDtypeStruct((2, rows), jnp.float32),
            jax.ShapeDtypeStruct((width, 128), jnp.float32),
        )
        + shapes,
        in_specs=[pl.BlockSpec(memory_space=pltpu.SMEM)]
        + [pl.BlockSpec(memory_space=pl.ANY)] * len(blocks)
        + [
            pl.BlockSpec((tile, full), lambda t: (t, 0)),
            pl.BlockSpec((tile, 1), lambda t: (t, 0)),
        ]
        + [
            pl.BlockSpec((tile, part_rows), lambda t, i=i: (t, i * CHUNKS + chunk))
            for i in range(images)
        ]
        + [pl.BlockSpec(memory_space=pltpu.HBM)] * (len(so_far) + len(after)),
        out_specs=(
            pl.BlockSpec((tile, rows), lambda t: (t, 0)),
            pl.BlockSpec((2, rows), lambda t: (0, 0)),
            pl.BlockSpec((tile, 128), lambda t: (t, 0)),
        )
        + (pl.BlockSpec(memory_space=pltpu.HBM),) * 2,
        scratch_shapes=scratch,
        input_output_aliases={first + n: 3 + n for n in range(len(so_far))},
        compiler_params=pltpu.CompilerParams(vmem_limit_bytes=VMEM_LIMIT),
        cost_estimate=pl.CostEstimate(
            flops=2 * rows * full * width,
            bytes_accessed=2 * (full * width + 2 * rows * full) + 6 * rows * width,
            transcendentals=0,
        ),
    )(ring, *blocks, w_up_t, gain, *[normed_t] * images, *so_far, *after)


def pair_kernel(
    contract, scale, ranges, member_ref, a_ref, a_other_ref, b_ref, b_other_ref, *refs
):
    arrived, out_ref = refs[: len(ranges)], refs[-1]
    dims = (contract, ((), ()))
    total = lax.dot_general(a_ref[...], b_ref[...], dims, preferred_element_type=jnp.float32)
    total += lax.dot_general(
        a_other_ref[...], b_other_ref[...], dims, preferred_element_type=jnp.float32
    )
    total *= scale
    step = pl.program_id(0)
    for (first, last), ref in zip(ranges, arrived):
        part = ref[...].astype(jnp.float32)
        total += jnp.where((step >= first) & (step < last), part, 0.0)
    out_ref[...] = total.astype(out_ref.dtype)


def pair_product(
    operands, specs, contract, shape, tile, depth, member, scale, arrived, dtype, after
):
    row_spec = lambda first, last: pl.BlockSpec(
        (tile, shape[1]), lambda t, m: (jnp.clip(t - first, 0, last - first - 1), 0)
    )
    steps = shape[0] // tile
    return pl.pallas_call(
        functools.partial(pair_kernel, contract, scale, [span for span, _ in arrived]),
        grid_spec=pltpu.PrefetchScalarGridSpec(
            num_scalar_prefetch=1,
            grid=(steps,),
            in_specs=specs
            + [row_spec(*span) for span, _ in arrived]
            + [pl.BlockSpec(memory_space=pltpu.HBM)] * len(after),
            out_specs=row_spec(0, steps),
        ),
        out_shape=jax.ShapeDtypeStruct(shape, dtype),
        compiler_params=pltpu.CompilerParams(vmem_limit_bytes=VMEM_LIMIT),
        cost_estimate=pl.CostEstimate(
            flops=4 * shape[0] * shape[1] * depth,
            bytes_accessed=4 * depth * (shape[0] + shape[1]) + 4 * shape[0] * shape[1],
            transcendentals=0,
        ),
    )(
        member.reshape(1).astype(jnp.int32),
        *operands,
        *[part for _, part in arrived],
        *after,
    )


def chip_products(product, spans, ctx_count, after):
    index = lax.axis_index("ctx")
    going, arrived = [], []
    for span in spans:
        for shift in range(1, ctx_count // 2):
            member = (index + 2 * shift) % ctx_count
            going.append(product(member, span, [], jnp.bfloat16, after))
            route = [(c, (c + 2 * shift) % ctx_count) for c in range(ctx_count)]
            arrived.append((span, lax.ppermute(going[-1], "ctx", route)))
    return going, arrived


def tie_kernel(*refs):
    del refs


def tie(values, others, place=pl.ANY):
    spaces = [place] + [pl.ANY] * (len(values) + len(others) - 1)
    return pl.pallas_call(
        tie_kernel,
        in_specs=[pl.BlockSpec(memory_space=space) for space in spaces],
        out_specs=[pl.BlockSpec(memory_space=space) for space in spaces[: len(values)]],
        out_shape=[jax.ShapeDtypeStruct(value.shape, value.dtype) for value in values],
        input_output_aliases={n: n for n in range(len(values))},
        compiler_params=pltpu.CompilerParams(vmem_limit_bytes=VMEM_LIMIT),
    )(*values, *others)


def visual_kernel(
    source_ref, present_ref, gained_ref, normed_ref, means_ref, inverse_ref, out_ref
):
    slot = pl.program_id(0)

    @pl.when(present_ref[slot] == 0)
    def _():
        out_ref[...] = jnp.zeros_like(out_ref)

    @pl.when(present_ref[slot] != 0)
    def _():
        gained = gained_ref[...]
        features = normed_ref[...].astype(jnp.float32)
        first, second = means_ref[0:1, :], means_ref[1:2, :]
        out_ref[0] = (inverse_ref[...] * (gained - first - features * second)).astype(
            out_ref.dtype
        )


def visual_slots(source, present, gained_t, normed_t, means, inverse, chunk, part_rows):
    width = gained_t.shape[0]
    slots = source.shape[0]
    picked = lambda s, source, present: (0, source[s])
    natural = lambda s, source, present: (0, source[s] * CHUNKS + chunk)
    return pl.pallas_call(
        visual_kernel,
        grid_spec=pltpu.PrefetchScalarGridSpec(
            num_scalar_prefetch=2,
            grid=(slots,),
            in_specs=[
                pl.BlockSpec((width, part_rows), picked),
                pl.BlockSpec((width, part_rows), natural),
                pl.BlockSpec((2, part_rows), picked),
                pl.BlockSpec((1, part_rows), natural),
            ],
            out_specs=pl.BlockSpec((1, width, part_rows), lambda s, source, present: (s, 0, 0)),
        ),
        out_shape=jax.ShapeDtypeStruct((slots, width, part_rows), jnp.bfloat16),
        compiler_params=pltpu.CompilerParams(vmem_limit_bytes=VMEM_LIMIT),
        cost_estimate=pl.CostEstimate(
            flops=6 * slots * width * part_rows,
            bytes_accessed=8 * slots * width * part_rows,
            transcendentals=0,
        ),
    )(source, present, gained_t, normed_t, means, inverse)


def turn_kernel(in_ref, *refs):
    refs[-1][...] = in_ref[...].T


def turn_rows(received, chunk, rows, so_far, after):
    full, part_rows = received.shape
    tile = divisor(full, 2560, 128)
    operands, aliases = [received], {}
    if so_far is not None:
        operands.append(so_far)
        aliases = {1: 0}
    operands += after
    specs = [pl.BlockSpec((tile, part_rows), lambda t: (t, 0))]
    specs += [pl.BlockSpec(memory_space=pltpu.HBM)] * (len(operands) - 1)
    return pl.pallas_call(
        turn_kernel,
        grid=(full // tile,),
        in_specs=specs,
        out_specs=pl.BlockSpec((part_rows, tile), lambda t: (chunk, t)),
        out_shape=jax.ShapeDtypeStruct((rows, full), received.dtype),
        input_output_aliases=aliases,
        compiler_params=pltpu.CompilerParams(vmem_limit_bytes=VMEM_LIMIT),
        cost_estimate=pl.CostEstimate(
            flops=0, bytes_accessed=4 * part_rows * full, transcendentals=0
        ),
    )(*operands)


def core_swap(value, ctx_count):
    return lax.ppermute(value, "ctx", [(c, c ^ 1) for c in range(ctx_count)])


def doubling_sum(value, axis, count, after=()):
    bit = 1
    while bit < count:
        if after and 2 * bit >= count:
            (value,) = tie([value], after)
        value = value + lax.ppermute(value, axis, [(t, t ^ bit) for t in range(count)])
        bit *= 2
    return value


def per_device(out_grad, pre_act, normed, inverse_std, w_up, w_down, ln_gain, owner_map):
    ctx_count = lax.axis_size("ctx")
    tp_count = lax.axis_size("tp")
    row_count = out_grad.shape[0]
    width = normed.shape[1]
    grad_scale = float(row_count * ctx_count) ** (-0.5)
    full_width = float(width * tp_count)

    owners = owner_map[0]
    image_count = owners.shape[0]
    image_rows = row_count // image_count
    part_rows = image_rows // CHUNKS
    chunk_rows = row_count // CHUNKS
    capacity = max(1, 2 * image_count // tp_count)
    slot_of = slot_numbers(owners, capacity)
    slot_ids = jnp.arange(tp_count * capacity)
    matches = slot_of[None, :] == slot_ids[:, None]
    present = jnp.any(matches, axis=1).astype(jnp.int32)
    source = jnp.sum(jnp.where(matches, jnp.arange(image_count)[None, :], 0), axis=1).astype(
        jnp.int32
    )

    def chunk_of(array, chunk):
        images = array.reshape((image_count, image_rows) + array.shape[1:])
        piece = images[:, chunk * part_rows : (chunk + 1) * part_rows]
        return piece.reshape((chunk_rows,) + array.shape[1:])

    ring = ring_owners(tp_count)
    gelu_value, slope = gelu_parts(pre_act.astype(jnp.float32))
    hidden = gelu_value.astype(jnp.bfloat16)
    hidden_other = core_swap(hidden, ctx_count)
    normed_t = normed.T
    normed_other = core_swap(normed_t, ctx_count)
    gain = ln_gain[:, None]
    w_up_t = w_up.T

    def back_of(chunk, blocks, so_far):
        return back_part(ring, blocks, w_down, slope, chunk, image_rows, ctx_count, so_far)

    first_grads, second_grads = [
        ring_blocks(chunk_of(out_grad, chunk), tp_count) for chunk in range(CHUNKS)
    ]
    first_back, first_sum, *so_far = back_of(0, first_grads, ())
    first_backs = ring_blocks(first_back, tp_count)
    second_back, second_sum, grads, grads_swap = back_of(1, second_grads, so_far)
    second_backs = ring_blocks(second_back, tp_count)
    grads_other = core_swap(grads_swap, ctx_count)
    back_sum = first_sum[0] + second_sum[0]

    def grad_w2_share(member, span, arrived, dtype, after):
        share, local = grads.shape[1] // ctx_count, hidden.shape[1]
        tile = divisor(share, 256, 128)
        steps = share // tile
        return pair_product(
            (grads, grads_other, hidden, hidden_other),
            [
                pl.BlockSpec((row_count, tile), lambda t, m: (0, m[0] * steps + t)),
                pl.BlockSpec((row_count, tile), lambda t, m: (m[0] // 2, t)),
                pl.BlockSpec((row_count, local), lambda t, m: (0, 0)),
                pl.BlockSpec((row_count, local), lambda t, m: (0, 0)),
            ],
            ((0,), (0,)), (share, local), tile, row_count, member, grad_scale, arrived, dtype,
            after,
        )

    w2_span = (0, grads.shape[1] // ctx_count // divisor(grads.shape[1] // ctx_count, 256, 128))
    going_w2, arrived_w2 = chip_products(grad_w2_share, [w2_span], ctx_count, [])
    member = lax.axis_index("ctx")

    def norm_of(chunk, blocks, so_far, after):
        return norm_part(
            ring, blocks, w_up_t, gain, normed_t, chunk, image_rows, ctx_count, so_far, after
        )

    def slots_of(chunk, gained_t, means):
        return visual_slots(
            source, present, gained_t, normed_t, means, inverse_std[None, :], chunk, part_rows
        )

    first_gained, first_rows, first_ln, *so_far = norm_of(0, first_backs, (), [])
    first_means = doubling_sum(first_rows, "tp", tp_count) / full_width
    first_slots, first_means = tie(
        [slots_of(0, first_gained, first_means), first_means], second_backs[-2:], pltpu.HBM
    )
    outgoing = [first_slots]
    second_gained, second_rows, second_ln, backs, backs_swap = norm_of(
        1, second_backs, so_far, [core_swap(first_means, ctx_count)]
    )
    backs_other = core_swap(backs_swap, ctx_count)

    w1_tile = divisor(width, 400, 16)
    w1_tiles = width // w1_tile

    def grad_w1_share(member, span, arrived, dtype, after):
        share = backs.shape[1] // ctx_count
        first, last = span
        return pair_product(
            (normed_t, normed_other, backs, backs_other),
            [
                pl.BlockSpec((w1_tile, row_count), lambda t, m: (first + t, 0)),
                pl.BlockSpec((w1_tile, row_count), lambda t, m: (first + t, 0)),
                pl.BlockSpec((row_count, share), lambda t, m: (0, m[0])),
                pl.BlockSpec((row_count, share), lambda t, m: (m[0] // 2, 0)),
            ],
            ((1,), (0,)), ((last - first) * w1_tile, share), w1_tile, row_count, member,
            grad_scale, arrived, dtype, after,
        )

    cut = w1_tiles // 2
    spans = [(0, cut), (cut, w1_tiles)] if cut else [(0, w1_tiles)]
    going_w1, arrived_w1 = chip_products(grad_w1_share, spans, ctx_count, [])

    second_means = doubling_sum(second_rows, "tp", tp_count, going_w1) / full_width
    early = [part for span, part in arrived_w1 if span == spans[0]]
    outgoing += tie([slots_of(1, second_gained, second_means)], early, pltpu.HBM)
    received = [
        lax.all_to_all(part, "tp", split_axis=0, concat_axis=0, tiled=True) for part in outgoing
    ]
    ln_sum = (first_ln + second_ln)[:, :2]
    small = jnp.concatenate(
        [jnp.sum(out_grad.astype(jnp.float32), axis=0), back_sum, ln_sum.T.reshape(-1)]
    )
    (small,) = tie([small], [part for _, part in arrived_w1])
    grad_w2 = grad_w2_share(member, w2_span, arrived_w2, jnp.float32, [small])
    small = doubling_sum(small, "ctx", ctx_count) * grad_scale
    grad_w1_t = grad_w1_share(member, (0, w1_tiles), arrived_w1, jnp.float32, [])
    assert capacity == 1
    vit_grad = None
    for chunk in range(CHUNKS):
        columns = received[chunk].reshape(tp_count * width, part_rows)
        after = [grad_w1_t, grad_w2] if chunk + 1 == CHUNKS else []
        vit_grad = turn_rows(columns, chunk, image_rows, vit_grad, after)

    features_in = out_grad.shape[1]
    hidden_in = pre_act.shape[1]
    bias_down = small[:features_in]
    bias_up = small[features_in : features_in + hidden_in]
    ln_grads = small[features_in + hidden_in :].reshape(2, width)
    return (grad_w2, grad_w1_t.T, bias_up, bias_down, ln_grads, vit_grad)


def solution(mesh):
    return jax.shard_map(
        per_device,
        mesh=mesh,
        in_specs=(
            P("ctx", "tp"),
            P("ctx", "tp"),
            P("ctx", "tp"),
            P("ctx"),
            P(None, "tp"),
            P(None, "tp"),
            P("tp"),
            P("ctx", None),
        ),
        out_specs=(
            P("ctx", "tp"),
            P("ctx", "tp"),
            P("tp"),
            P("tp"),
            P(None, "tp"),
            P(("ctx", "tp"), None),
        ),
        check_vma=False,
    )
```

```python
import functools
import math

import jax
import jax.numpy as jnp
from jax import lax
from jax.experimental import pallas as pl
from jax.experimental.pallas import tpu as pltpu
from jax.sharding import PartitionSpec as P

CHUNKS = 2
VMEM_LIMIT = 48 * 1024 * 1024


def gelu_parts(linear):
    normal_cdf = 0.5 * (1.0 + jax.scipy.special.erf(linear * 2.0 ** (-0.5)))
    density = jnp.exp(-0.5 * linear * linear) * (2.0 * math.pi) ** (-0.5)
    return (linear * normal_cdf, normal_cdf + linear * density)


def slot_numbers(owners, capacity):
    position = jnp.arange(owners.shape[0])
    earlier = (owners[None, :] == owners[:, None]) & (position[None, :] < position[:, None])
    return owners * capacity + jnp.sum(earlier.astype(jnp.int32), axis=1)


def divisor(extent, most, unit):
    return max(d for d in range(unit, most + 1, unit) if extent % d == 0)


def ring_order(count):
    depth = 4 if count % 4 == 0 else count
    width = count // depth
    walk = [(z, 0) for z in range(depth)]
    if width > 1:
        for turn, z in enumerate(reversed(range(depth))):
            ys = list(range(1, width))
            walk += [(z, y) for y in (ys if turn % 2 == 0 else ys[::-1])]
    return [z * width + y for z, y in walk]


def ring_owners(count):
    order = ring_order(count)
    table = []
    for j in range(count):
        at = order.index(j)
        steps = [0]
        for step in range(1, count // 2):
            steps += [-step, step]
        steps += [count // 2]
        table.append([order[(at + s) % count] for s in steps])
    core = (lax.axis_index("ctx") % 2).astype(jnp.int32)
    return jnp.concatenate([jnp.array(table, jnp.int32)[lax.axis_index("tp")], core[None]])


def ring_blocks(block, count):
    order = ring_order(count)
    ahead = [(order[p], order[(p + 1) % count]) for p in range(count)]
    behind = [(order[p], order[(p - 1) % count]) for p in range(count)]
    up, down = block, block
    blocks = [block]
    for _ in range(1, count // 2):
        up = lax.ppermute(up, "tp", ahead)
        down = lax.ppermute(down, "tp", behind)
        blocks += [up, down]
    half = block.shape[0] // 2
    blocks.append(lax.ppermute(up[:half], "tp", ahead))
    blocks.append(lax.ppermute(down[half:], "tp", behind))
    return blocks


def assemble(owners_ref, block_refs, held, sems):
    rows, width = block_refs[0].shape
    half = rows // 2
    last = len(block_refs) - 2
    copies = []
    for k, ref in enumerate(block_refs):
        columns = pl.ds(pl.multiple_of(owners_ref[min(k, last)] * width, width), width)
        if k < last:
            target = held.at[:, columns]
        else:
            target = held.at[pl.ds((k - last) * half, half), columns]
        copies.append(pltpu.make_async_copy(ref, target, sems.at[k]))
    return copies


def spread(ring_ref, held, full_ref, swap_ref, chunk, image_rows, sems):
    rows, part_rows = held.shape[0], image_rows // CHUNKS
    all_rows, member_width = full_ref.shape[0], swap_ref.shape[1]
    other = 1 - ring_ref[ring_ref.shape[0] - 1]
    copies = []
    for i in range(rows // part_rows):
        source = pl.ds(i * part_rows, part_rows)
        place = i * image_rows + chunk * part_rows
        copies.append((held.at[source, :], full_ref.at[pl.ds(place, part_rows), :]))
        for chip in range(swap_ref.shape[0] // all_rows):
            columns = pl.ds(
                pl.multiple_of((2 * chip + other) * member_width, member_width), member_width
            )
            target = swap_ref.at[pl.ds(chip * all_rows + place, part_rows), :]
            copies.append((held.at[source, columns], target))
    return [
        pltpu.make_async_copy(source, target, sems.at[n])
        for n, (source, target) in enumerate(copies)
    ]


def spread_shapes(rows, chunk_rows, full, ctx_count, images):
    shapes = (
        jax.ShapeDtypeStruct((rows, full), jnp.bfloat16),
        jax.ShapeDtypeStruct((rows * (ctx_count // 2), full // ctx_count), jnp.bfloat16),
    )
    scratch = [
        pltpu.VMEM((chunk_rows, full), jnp.bfloat16),
        pltpu.SemaphoreType.DMA((2 * tp_most(),)),
        pltpu.SemaphoreType.DMA((images * (1 + ctx_count // 2),)),
    ]
    return shapes, scratch


def tp_most():
    return lax.axis_size("tp")


def back_kernel(chunk, image_rows, blocks, carried, ring_ref, *refs):
    block_refs, refs = refs[:blocks], refs[blocks:]
    w_ref, slope_ref, *refs = refs
    back_ref, sum_ref, full_ref, swap_ref, held, sems, out_sems = refs[carried:]
    copies = assemble(ring_ref, block_refs, held, sems)
    for copy in copies:
        copy.start()
    for copy in copies:
        copy.wait()
    outs = spread(ring_ref, held, full_ref, swap_ref, chunk, image_rows, out_sems)
    for copy in outs:
        copy.start()
    rows, part_rows = held.shape[0], image_rows // CHUNKS
    tile = divisor(rows, 256, part_rows)
    sums = jnp.zeros(sum_ref.shape, jnp.float32)
    for start in range(0, rows, tile):
        total = jnp.dot(
            held[start : start + tile, :], w_ref[...], preferred_element_type=jnp.float32
        )
        for n in range(tile // part_rows):
            image = start // part_rows + n
            place = image * image_rows + chunk * part_rows
            part = (
                total[n * part_rows : (n + 1) * part_rows]
                * slope_ref[place : place + part_rows, :]
            ).astype(back_ref.dtype)
            back_ref[image * part_rows : (image + 1) * part_rows, :] = part
            sums += jnp.sum(part.astype(jnp.float32), axis=0, keepdims=True)
    sum_ref[...] = sums
    for copy in outs:
        copy.wait()


def back_part(ring, blocks, w_down, slope, chunk, image_rows, ctx_count, so_far):
    rows = blocks[0].shape[0]
    full, width = w_down.shape
    images = slope.shape[0] // image_rows
    shapes, scratch = spread_shapes(slope.shape[0], rows, full, ctx_count, images)
    first = 1 + len(blocks) + 2
    return pl.pallas_call(
        functools.partial(back_kernel, chunk, image_rows, len(blocks), len(so_far)),
        out_shape=(
            jax.ShapeDtypeStruct((rows, width), jnp.bfloat16),
            jax.ShapeDtypeStruct((1, width), jnp.float32),
        )
        + shapes,
        in_specs=[pl.BlockSpec(memory_space=pltpu.SMEM)]
        + [pl.BlockSpec(memory_space=pl.ANY)] * len(blocks)
        + [pl.BlockSpec(memory_space=pltpu.VMEM)] * 2
        + [pl.BlockSpec(memory_space=pltpu.HBM)] * len(so_far),
        out_specs=(pl.BlockSpec(memory_space=pltpu.VMEM),) * 2
        + (pl.BlockSpec(memory_space=pltpu.HBM),) * 2,
        scratch_shapes=scratch,
        input_output_aliases={first + n: 2 + n for n in range(len(so_far))},
        compiler_params=pltpu.CompilerParams(vmem_limit_bytes=VMEM_LIMIT),
        cost_estimate=pl.CostEstimate(
            flops=2 * rows * full * width,
            bytes_accessed=2 * (2 * rows * full + full * width),
            transcendentals=0,
        ),
    )(ring, *blocks, w_down, slope, *so_far)


def norm_kernel(chunk, image_rows, blocks, images, carried, ring_ref, *refs):
    block_refs, refs = refs[:blocks], refs[blocks:]
    w_ref, gain_ref, *refs = refs
    normed_refs, refs = refs[:images], refs[images:]
    grad_ref, sums_ref, ln_ref, full_ref, swap_ref, held, sems, out_sems = refs[carried:]
    step = pl.program_id(0)
    outs = spread(ring_ref, held, full_ref, swap_ref, chunk, image_rows, out_sems)

    @pl.when(step == 0)
    def _():
        copies = assemble(ring_ref, block_refs, held, sems)
        for copy in copies:
            copy.start()
        for copy in copies:
            copy.wait()
        for copy in outs:
            copy.start()
        sums_ref[...] = jnp.zeros_like(sums_ref)

    grad = lax.dot_general(
        w_ref[...], held[...], (((1,), (1,)), ((), ())), preferred_element_type=jnp.float32
    )
    grad_ref[...] = grad
    features = jnp.concatenate([ref[...] for ref in normed_refs], axis=1).astype(jnp.float32)
    gained = gain_ref[...] * grad
    sums_ref[0:1, :] += jnp.sum(gained, axis=0, keepdims=True)
    sums_ref[1:2, :] += jnp.sum(gained * features, axis=0, keepdims=True)
    gains = jnp.sum(grad * features, axis=1, keepdims=True)
    biases = jnp.sum(grad, axis=1, keepdims=True)
    lane = lax.broadcasted_iota(jnp.int32, ln_ref.shape, 1)
    ln_ref[...] = jnp.where(lane == 0, gains, biases)

    @pl.when(step == pl.num_programs(0) - 1)
    def _():
        for copy in outs:
            copy.wait()


def norm_part(ring, blocks, w_up_t, gain, normed_t, chunk, image_rows, ctx_count, so_far, after):
    rows = blocks[0].shape[0]
    width, full = w_up_t.shape
    part_rows = image_rows // CHUNKS
    images = rows // part_rows
    tile = divisor(width, 400, 16)
    shapes, scratch = spread_shapes(normed_t.shape[1], rows, full, ctx_count, images)
    first = 1 + len(blocks) + 2 + images
    return pl.pallas_call(
        functools.partial(
            norm_kernel, chunk, image_rows, len(blocks), images, len(so_far) + len(after)
        ),
        grid=(width // tile,),
        out_shape=(
            jax.ShapeDtypeStruct((width, rows), jnp.float32),
            jax.ShapeDtypeStruct((2, rows), jnp.float32),
            jax.ShapeDtypeStruct((width, 128), jnp.float32),
        )
        + shapes,
        in_specs=[pl.BlockSpec(memory_space=pltpu.SMEM)]
        + [pl.BlockSpec(memory_space=pl.ANY)] * len(blocks)
        + [
            pl.BlockSpec((tile, full), lambda t: (t, 0)),
            pl.BlockSpec((tile, 1), lambda t: (t, 0)),
        ]
        + [
            pl.BlockSpec((tile, part_rows), lambda t, i=i: (t, i * CHUNKS + chunk))
            for i in range(images)
        ]
        + [pl.BlockSpec(memory_space=pltpu.HBM)] * (len(so_far) + len(after)),
        out_specs=(
            pl.BlockSpec((tile, rows), lambda t: (t, 0)),
            pl.BlockSpec((2, rows), lambda t: (0, 0)),
            pl.BlockSpec((tile, 128), lambda t: (t, 0)),
        )
        + (pl.BlockSpec(memory_space=pltpu.HBM),) * 2,
        scratch_shapes=scratch,
        input_output_aliases={first + n: 3 + n for n in range(len(so_far))},
        compiler_params=pltpu.CompilerParams(vmem_limit_bytes=VMEM_LIMIT),
        cost_estimate=pl.CostEstimate(
            flops=2 * rows * full * width,
            bytes_accessed=2 * (full * width + 2 * rows * full) + 6 * rows * width,
            transcendentals=0,
        ),
    )(ring, *blocks, w_up_t, gain, *[normed_t] * images, *so_far, *after)


def pair_kernel(
    contract, scale, ranges, member_ref, a_ref, a_other_ref, b_ref, b_other_ref, *refs
):
    arrived, out_ref = refs[: len(ranges)], refs[-1]
    dims = (contract, ((), ()))
    total = lax.dot_general(a_ref[...], b_ref[...], dims, preferred_element_type=jnp.float32)
    total += lax.dot_general(
        a_other_ref[...], b_other_ref[...], dims, preferred_element_type=jnp.float32
    )
    total *= scale
    step = pl.program_id(0)
    for (first, last), ref in zip(ranges, arrived):
        part = ref[...].astype(jnp.float32)
        total += jnp.where((step >= first) & (step < last), part, 0.0)
    out_ref[...] = total.astype(out_ref.dtype)


def pair_product(
    operands, specs, contract, shape, tile, depth, member, scale, arrived, dtype, after
):
    row_spec = lambda first, last: pl.BlockSpec(
        (tile, shape[1]), lambda t, m: (jnp.clip(t - first, 0, last - first - 1), 0)
    )
    steps = shape[0] // tile
    return pl.pallas_call(
        functools.partial(pair_kernel, contract, scale, [span for span, _ in arrived]),
        grid_spec=pltpu.PrefetchScalarGridSpec(
            num_scalar_prefetch=1,
            grid=(steps,),
            in_specs=specs
            + [row_spec(*span) for span, _ in arrived]
            + [pl.BlockSpec(memory_space=pltpu.HBM)] * len(after),
            out_specs=row_spec(0, steps),
        ),
        out_shape=jax.ShapeDtypeStruct(shape, dtype),
        compiler_params=pltpu.CompilerParams(vmem_limit_bytes=VMEM_LIMIT),
        cost_estimate=pl.CostEstimate(
            flops=4 * shape[0] * shape[1] * depth,
            bytes_accessed=4 * depth * (shape[0] + shape[1]) + 4 * shape[0] * shape[1],
            transcendentals=0,
        ),
    )(
        member.reshape(1).astype(jnp.int32),
        *operands,
        *[part for _, part in arrived],
        *after,
    )


def chip_products(product, spans, ctx_count, after):
    index = lax.axis_index("ctx")
    going, arrived = [], []
    for span in spans:
        for shift in range(1, ctx_count // 2):
            member = (index + 2 * shift) % ctx_count
            going.append(product(member, span, [], jnp.bfloat16, after))
            route = [(c, (c + 2 * shift) % ctx_count) for c in range(ctx_count)]
            arrived.append((span, lax.ppermute(going[-1], "ctx", route)))
    return going, arrived


def tie_kernel(*refs):
    del refs


def tie(values, others):
    return pl.pallas_call(
        tie_kernel,
        in_specs=[pl.BlockSpec(memory_space=pl.ANY)] * (len(values) + len(others)),
        out_specs=[pl.BlockSpec(memory_space=pl.ANY)] * len(values),
        out_shape=[jax.ShapeDtypeStruct(value.shape, value.dtype) for value in values],
        input_output_aliases={n: n for n in range(len(values))},
        compiler_params=pltpu.CompilerParams(vmem_limit_bytes=VMEM_LIMIT),
    )(*values, *others)


def visual_kernel(
    source_ref, present_ref, grad_ref, normed_ref, gain_ref, means_ref, inverse_ref, *refs
):
    out_ref = refs[-1]
    slot = pl.program_id(0)

    @pl.when(present_ref[slot] == 0)
    def _():
        out_ref[...] = jnp.zeros_like(out_ref)

    @pl.when(present_ref[slot] != 0)
    def _():
        gained = gain_ref[...] * grad_ref[...]
        features = normed_ref[...].astype(jnp.float32)
        first, second = means_ref[0:1, :], means_ref[1:2, :]
        out_ref[0] = (inverse_ref[...] * (gained - first - features * second)).astype(
            out_ref.dtype
        )


def visual_slots(source, present, grad_t, normed_t, gain, means, inverse, chunk, part_rows, after):
    width = grad_t.shape[0]
    slots = source.shape[0]
    picked = lambda s, source, present: (0, source[s])
    natural = lambda s, source, present: (0, source[s] * CHUNKS + chunk)
    return pl.pallas_call(
        visual_kernel,
        grid_spec=pltpu.PrefetchScalarGridSpec(
            num_scalar_prefetch=2,
            grid=(slots,),
            in_specs=[
                pl.BlockSpec((width, part_rows), picked),
                pl.BlockSpec((width, part_rows), natural),
                pl.BlockSpec((width, 1), lambda s, source, present: (0, 0)),
                pl.BlockSpec((2, part_rows), picked),
                pl.BlockSpec((1, part_rows), natural),
            ]
            + [pl.BlockSpec(memory_space=pltpu.HBM)] * len(after),
            out_specs=pl.BlockSpec((1, width, part_rows), lambda s, source, present: (s, 0, 0)),
        ),
        out_shape=jax.ShapeDtypeStruct((slots, width, part_rows), jnp.bfloat16),
        compiler_params=pltpu.CompilerParams(vmem_limit_bytes=VMEM_LIMIT),
        cost_estimate=pl.CostEstimate(
            flops=6 * slots * width * part_rows,
            bytes_accessed=8 * slots * width * part_rows,
            transcendentals=0,
        ),
    )(source, present, grad_t, normed_t, gain, means, inverse, *after)


def turn_kernel(in_ref, *refs):
    refs[-1][...] = in_ref[...].T


def turn_rows(received, chunk, rows, so_far, after):
    full, part_rows = received.shape
    tile = divisor(full, 2560, 128)
    operands, aliases = [received], {}
    if so_far is not None:
        operands.append(so_far)
        aliases = {1: 0}
    operands += after
    specs = [pl.BlockSpec((tile, part_rows), lambda t: (t, 0))]
    specs += [pl.BlockSpec(memory_space=pltpu.HBM)] * (len(operands) - 1)
    return pl.pallas_call(
        turn_kernel,
        grid=(full // tile,),
        in_specs=specs,
        out_specs=pl.BlockSpec((part_rows, tile), lambda t: (chunk, t)),
        out_shape=jax.ShapeDtypeStruct((rows, full), received.dtype),
        input_output_aliases=aliases,
        compiler_params=pltpu.CompilerParams(vmem_limit_bytes=VMEM_LIMIT),
        cost_estimate=pl.CostEstimate(
            flops=0, bytes_accessed=4 * part_rows * full, transcendentals=0
        ),
    )(*operands)


def core_swap(value, ctx_count):
    return lax.ppermute(value, "ctx", [(c, c ^ 1) for c in range(ctx_count)])


def doubling_sum(value, axis, count, after=()):
    bit = 1
    while bit < count:
        if after and 2 * bit >= count:
            (value,) = tie([value], after)
        value = value + lax.ppermute(value, axis, [(t, t ^ bit) for t in range(count)])
        bit *= 2
    return value


def per_device(out_grad, pre_act, normed, inverse_std, w_up, w_down, ln_gain, owner_map):
    ctx_count = lax.axis_size("ctx")
    tp_count = lax.axis_size("tp")
    row_count = out_grad.shape[0]
    width = normed.shape[1]
    grad_scale = float(row_count * ctx_count) ** (-0.5)
    full_width = float(width * tp_count)

    owners = owner_map[0]
    image_count = owners.shape[0]
    image_rows = row_count // image_count
    part_rows = image_rows // CHUNKS
    chunk_rows = row_count // CHUNKS
    capacity = max(1, 2 * image_count // tp_count)
    slot_of = slot_numbers(owners, capacity)
    slot_ids = jnp.arange(tp_count * capacity)
    matches = slot_of[None, :] == slot_ids[:, None]
    present = jnp.any(matches, axis=1).astype(jnp.int32)
    source = jnp.sum(jnp.where(matches, jnp.arange(image_count)[None, :], 0), axis=1).astype(
        jnp.int32
    )

    def chunk_of(array, chunk):
        images = array.reshape((image_count, image_rows) + array.shape[1:])
        piece = images[:, chunk * part_rows : (chunk + 1) * part_rows]
        return piece.reshape((chunk_rows,) + array.shape[1:])

    ring = ring_owners(tp_count)
    gelu_value, slope = gelu_parts(pre_act.astype(jnp.float32))
    hidden = gelu_value.astype(jnp.bfloat16)
    hidden_other = core_swap(hidden, ctx_count)
    normed_t = normed.T
    normed_other = core_swap(normed_t, ctx_count)
    gain = ln_gain[:, None]
    w_up_t = w_up.T

    def back_of(chunk, blocks, so_far):
        return back_part(ring, blocks, w_down, slope, chunk, image_rows, ctx_count, so_far)

    first_grads, second_grads = [
        ring_blocks(chunk_of(out_grad, chunk), tp_count) for chunk in range(CHUNKS)
    ]
    first_back, first_sum, *so_far = back_of(0, first_grads, ())
    first_backs = ring_blocks(first_back, tp_count)
    second_back, second_sum, grads, grads_swap = back_of(1, second_grads, so_far)
    second_backs = ring_blocks(second_back, tp_count)
    grads_other = core_swap(grads_swap, ctx_count)
    back_sum = first_sum[0] + second_sum[0]

    def grad_w2_share(member, span, arrived, dtype, after):
        share, local = grads.shape[1] // ctx_count, hidden.shape[1]
        tile = divisor(share, 256, 128)
        steps = share // tile
        return pair_product(
            (grads, grads_other, hidden, hidden_other),
            [
                pl.BlockSpec((row_count, tile), lambda t, m: (0, m[0] * steps + t)),
                pl.BlockSpec((row_count, tile), lambda t, m: (m[0] // 2, t)),
                pl.BlockSpec((row_count, local), lambda t, m: (0, 0)),
                pl.BlockSpec((row_count, local), lambda t, m: (0, 0)),
            ],
            ((0,), (0,)), (share, local), tile, row_count, member, grad_scale, arrived, dtype,
            after,
        )

    w2_span = (0, grads.shape[1] // ctx_count // divisor(grads.shape[1] // ctx_count, 256, 128))
    going_w2, arrived_w2 = chip_products(grad_w2_share, [w2_span], ctx_count, [])
    member = lax.axis_index("ctx")

    def norm_of(chunk, blocks, so_far, after):
        return norm_part(
            ring, blocks, w_up_t, gain, normed_t, chunk, image_rows, ctx_count, so_far, after
        )

    def slots_of(chunk, grad_t, means):
        return visual_slots(
            source, present, grad_t, normed_t, gain, means, inverse_std[None, :], chunk, part_rows, []
        )

    first_grad, first_rows, first_ln, *so_far = norm_of(0, first_backs, (), [])
    first_means = doubling_sum(first_rows, "tp", tp_count) / full_width
    first_slots, first_means = tie(
        [slots_of(0, first_grad, first_means), first_means], second_backs[-2:]
    )
    outgoing = [first_slots]
    second_grad, second_rows, second_ln, backs, backs_swap = norm_of(
        1, second_backs, so_far, [first_means]
    )
    backs_other = core_swap(backs_swap, ctx_count)

    w1_tile = divisor(width, 400, 16)
    w1_tiles = width // w1_tile

    def grad_w1_share(member, span, arrived, dtype, after):
        share = backs.shape[1] // ctx_count
        first, last = span
        return pair_product(
            (normed_t, normed_other, backs, backs_other),
            [
                pl.BlockSpec((w1_tile, row_count), lambda t, m: (first + t, 0)),
                pl.BlockSpec((w1_tile, row_count), lambda t, m: (first + t, 0)),
                pl.BlockSpec((row_count, share), lambda t, m: (0, m[0])),
                pl.BlockSpec((row_count, share), lambda t, m: (m[0] // 2, 0)),
            ],
            ((1,), (0,)), ((last - first) * w1_tile, share), w1_tile, row_count, member,
            grad_scale, arrived, dtype, after,
        )

    cut = w1_tiles // 2
    spans = [(0, cut), (cut, w1_tiles)] if cut else [(0, w1_tiles)]
    going_w1, arrived_w1 = chip_products(grad_w1_share, spans, ctx_count, going_w2)

    second_means = doubling_sum(second_rows, "tp", tp_count, going_w1) / full_width
    early = [part for span, part in arrived_w1 if span == spans[0]]
    outgoing += tie([slots_of(1, second_grad, second_means)], early)
    received = [
        lax.all_to_all(part, "tp", split_axis=0, concat_axis=0, tiled=True) for part in outgoing
    ]
    ln_sum = (first_ln + second_ln)[:, :2]
    small = jnp.concatenate(
        [jnp.sum(out_grad.astype(jnp.float32), axis=0), back_sum, ln_sum.T.reshape(-1)]
    )
    (small,) = tie([small], [part for _, part in arrived_w1])
    grad_w2 = grad_w2_share(member, w2_span, arrived_w2, jnp.float32, [small])
    small = doubling_sum(small, "ctx", ctx_count) * grad_scale
    grad_w1_t = grad_w1_share(member, (0, w1_tiles), arrived_w1, jnp.float32, [])
    assert capacity == 1
    vit_grad = None
    for chunk in range(CHUNKS):
        columns = received[chunk].reshape(tp_count * width, part_rows)
        after = [grad_w1_t, grad_w2] if chunk + 1 == CHUNKS else []
        vit_grad = turn_rows(columns, chunk, image_rows, vit_grad, after)

    features_in = out_grad.shape[1]
    hidden_in = pre_act.shape[1]
    bias_down = small[:features_in]
    bias_up = small[features_in : features_in + hidden_in]
    ln_grads = small[features_in + hidden_in :].reshape(2, width)
    return (grad_w2, grad_w1_t.T, bias_up, bias_down, ln_grads, vit_grad)


def solution(mesh):
    return jax.shard_map(
        per_device,
        mesh=mesh,
        in_specs=(
            P("ctx", "tp"),
            P("ctx", "tp"),
            P("ctx", "tp"),
            P("ctx"),
            P(None, "tp"),
            P(None, "tp"),
            P("tp"),
            P("ctx", None),
        ),
        out_specs=(
            P("ctx", "tp"),
            P("ctx", "tp"),
            P("tp"),
            P("tp"),
            P(None, "tp"),
            P(("ctx", "tp"), None),
        ),
        check_vma=False,
    )
```
